256 devices in a mesh: seq: 64 (over x, z, core), vocab: 4 (over y).
Axes of the slice: x: 4, y: 4, z: 8, core: 2. Of those that a mesh axis runs over, the one named last changes fastest.
Arguments:
- hidden: bfloat16 [4096, 4096], P('seq'), may hold values from -12 to 12
- head_weight: bfloat16 [4096, 126464], P(None, ('seq', 'vocab')), may hold values from -3 to 3
- teacher: bfloat16 [512, 126464], P(None, ('seq', 'vocab')), may hold values from -320 to 320
- positions: int32 [64, 8], P('seq'), may hold values from 0 to 63, as said below
- counts: int32 [64], P('seq'), may hold values from 1 to 8, 256 in all
Outputs:
- grad_hidden: bfloat16 [512, 4096], P(('seq', 'vocab'))
- grad_head: bfloat16 [4096, 126464], P(None, ('seq', 'vocab'))
The draws below stay inside these ranges and needn't reach their ends.
Inputs may be any that keep to these rules, and one draw needn't show every extreme that they name: Each row holds 8 distinct token positions within its seq shard's block of 64 tokens; the first counts[s] of row s are its masked tokens. The counts sum to exactly 256.
All inputs are finite; a program needn't handle non-finite values. No bound on the sum of `counts` on one device may be relied on, other than what follows from the above.
Results may differ from the reference program's by a relative error of at most 0.012.
Values may be sent and summed in bfloat16 or wider, within the bound.
No kernel may reach another device: no remote copies, remote signals or barrier semaphores. Data moves between devices by JAX's collectives and lax.ppermute only.
A program may use at most 64 MiB of HBM per device.

```python
import math
import jax
import jax.numpy as jnp
import numpy as np
from jax import lax

D = 4096
VOCAB = 126464
TOK_DEV = 64
SPAN = 1
CAP = 8
TOKENS = 4096
SEQS = 64
SLOTS = 512
MASKED = 256
N_SEQ = 64


def draw_hidden(key, part):
    key = jax.random.fold_in(key, 11)
    k_body, k_scale = jax.random.split(key, 2)
    row_scale = jnp.exp(jax.random.uniform(k_scale, (TOKENS, 1), minval=math.log(0.02), maxval=math.log(0.2)))
    values = jax.random.normal(k_body, (TOKENS, D)) * row_scale
    return jnp.clip(values, -12.0, 12.0).astype(jnp.bfloat16)


def draw_head_weight(key, part):
    key = jax.random.fold_in(key, 12)
    k_body, k_scale = jax.random.split(key, 2)
    col_scale = jnp.exp(jax.random.uniform(k_scale, (1, VOCAB), minval=math.log(0.9), maxval=math.log(9.0)))
    values = jax.random.normal(k_body, (D, VOCAB)) * col_scale / math.sqrt(D)
    return jnp.clip(values, -3.0, 3.0).astype(jnp.bfloat16)


def draw_teacher(key, part):
    key = jax.random.fold_in(key, 13)
    k_body, k_row, k_col = jax.random.split(key, 3)
    row_scale = jnp.exp(jax.random.uniform(k_row, (SLOTS, 1), minval=math.log(0.02), maxval=math.log(0.2)))
    col_scale = jnp.exp(jax.random.uniform(k_col, (1, VOCAB), minval=math.log(0.9), maxval=math.log(9.0)))
    values = jax.random.normal(k_body, (SLOTS, VOCAB)) * row_scale * col_scale
    return jnp.clip(values, -320.0, 320.0).astype(jnp.bfloat16)


def draw_positions(key, part):
    key = jax.random.fold_in(key, 14)
    shard_count = TOKENS // TOK_DEV
    column = jnp.arange(TOK_DEV, dtype=jnp.int32)[None, :]
    row = jnp.arange(shard_count, dtype=jnp.int32)[:, None]
    scores = jax.random.randint(key, (shard_count, TOK_DEV), 0, 1 << 20) * TOK_DEV + column
    forced = (row == 0) & ((column == 0) | (column == TOK_DEV - 1))
    scores = jnp.where(forced, (1 << 21) * TOK_DEV + column, scores)
    unused, chosen = lax.top_k(scores, CAP)
    return chosen.astype(jnp.int32)


def length_profile(count, total, limit, lean):
    loads = [(1 << 20) // math.isqrt(standing ** lean) + 1 for standing in range(2, count + 1)]
    surplus, given = total - limit - (count - 1), [1] * (count - 1)
    while surplus > 0:
        movable = [i for i in range(count - 1) if given[i] < limit]
        mass, budget = sum([loads[i] for i in movable]), surplus
        for i in movable:
            extra = min(limit - given[i], max(1, budget * loads[i] // mass), surplus)
            given[i] = given[i] + extra
            surplus = surplus - extra
    return np.array([limit] + given)


def uneven_parts(stream_key, number_of, total, bound, slope):
    if number_of == 2:
        one = jax.random.randint(stream_key, (), max(1, total - bound), min(bound, total - 1) + 1)
        return jnp.stack([one, total - one])
    lengths = jnp.asarray(length_profile(number_of, total, bound, slope), jnp.int32)
    twos = (number_of - 1) // 2
    donor, receiver = lengths[1:1 + 2 * twos:2], lengths[2:2 + 2 * twos:2]
    margin = jnp.minimum(donor - 1, bound - receiver)
    shifted = jax.random.randint(jax.random.fold_in(stream_key, 1), (twos,), 0, 1 << 20) % (margin + 1)
    lengths = lengths.at[1:1 + 2 * twos:2].set(donor - shifted).at[2:2 + 2 * twos:2].set(receiver + shifted)
    return lengths[jax.random.permutation(jax.random.fold_in(stream_key, 2), number_of)]


def setup_inputs(seed: int = 0) -> dict:
    splits = jax.random.split(jax.random.key(seed), 6)
    hidden = draw_hidden(jax.random.fold_in(splits[5], 71), 0)
    head_weight = draw_head_weight(jax.random.fold_in(splits[5], 71), 0)
    teacher = draw_teacher(jax.random.fold_in(splits[5], 71), 0)
    positions = draw_positions(jax.random.fold_in(splits[5], 71), 0)
    counts = uneven_parts(splits[4], N_SEQ, MASKED, CAP, 2).astype(jnp.int32)
    return dict(hidden=hidden, head_weight=head_weight, teacher=teacher, positions=positions, counts=counts)


loss_scale = 1024.0


def reference(hidden, head_weight, teacher, positions, counts):
    offsets = (jnp.arange(N_SEQ, dtype=jnp.int32) * TOK_DEV)[:, None]
    rows_index = (positions + offsets).reshape(-1).astype(jnp.int32)
    picked = jnp.take(hidden, rows_index, axis=0)
    seq_count = jnp.sum(counts.reshape(SEQS, SPAN), axis=1).astype(jnp.int32)
    per_slot = jnp.repeat(seq_count, SPAN * CAP)
    slot_rank = jnp.arange(CAP, dtype=jnp.int32)[None, :]
    validity = (slot_rank < counts[:, None]).reshape(-1)
    weight = jnp.where(validity, loss_scale / per_slot.astype(jnp.float32), 0.0)
    student = jnp.dot(picked, head_weight, preferred_element_type=jnp.float32)
    prob_student = jax.nn.softmax(student, axis=-1)
    prob_teacher = jax.nn.softmax(teacher.astype(jnp.float32), axis=-1)
    grad_logits = (weight[:, None] * (prob_student - prob_teacher)).astype(jnp.bfloat16)
    grad_head = lax.dot_general(picked, grad_logits, (((0,), (0,)), ((), ())), preferred_element_type=jnp.float32).astype(jnp.bfloat16)
    grad_hidden = lax.dot_general(grad_logits, head_weight, (((1,), (1,)), ((), ())), preferred_element_type=jnp.float32).astype(jnp.bfloat16)
    return grad_hidden, grad_head
```

```python
import jax
import jax.numpy as jnp
from jax import lax
from jax.experimental import pallas as pl
from jax.experimental.pallas import tpu as pltpu
from jax.sharding import Mesh, PartitionSpec as P

LOSS_SCALE = 1024.0
MASKED = 256
MARK = 64.0
INTERPRET = False

SEQ = ("x", "z", "core")
ALL = ("x", "z", "core", "y")
CHIPS = ("x", "z", "y")
NX, NZ, NCORE, NY = 4, 8, 2, 4
BLOCKS = NCORE * NY
F32, BF16 = jnp.float32, jnp.bfloat16
NT = (((1,), (1,)), ((), ()))
TN = (((0,), (0,)), ((), ()))
VMEM = pl.BlockSpec(memory_space=pltpu.VMEM)
SMEM = pl.BlockSpec(memory_space=pltpu.SMEM)


def call(body, out, *args, specs=None, flops=0, scratch=()):
    leaves = jax.tree.leaves((args, out))
    nbytes = sum(x.size * x.dtype.itemsize for x in leaves)
    return pl.pallas_call(
        body,
        out_shape=out,
        in_specs=specs or [VMEM] * len(args),
        out_specs=jax.tree.map(lambda _: VMEM, out),
        scratch_shapes=list(scratch),
        cost_estimate=pl.CostEstimate(flops=flops, bytes_accessed=nbytes, transcendentals=0),
        compiler_params=pltpu.CompilerParams(vmem_limit_bytes=40 * 2**20),
        interpret=INTERPRET,
    )(*args)


def shape(dims, dtype):
    return jax.ShapeDtypeStruct(dims, dtype)


def block_of(y, core):
    return y * NCORE + core


def columns(block, width):
    return pl.ds(pl.multiple_of(block * width, width), width)


def pick_body(positions, counts, hidden, out):
    tokens, depth = hidden.shape
    shards, capacity, width = out.shape
    y = lax.axis_index("y")
    row = lax.broadcasted_iota(jnp.int32, (2 * capacity, tokens), 0)
    column = lax.broadcasted_iota(jnp.int32, (2 * capacity, tokens), 1)
    hot = jnp.zeros((2 * capacity, tokens), F32)
    for k in range(capacity):
        hot = jnp.where((row == k) & (column == positions[0, k]), 1.0, hot)
    mine = hidden[:, columns(y, NCORE * width)]
    rows = jnp.dot(hot.astype(BF16), mine, preferred_element_type=F32)[:capacity]
    rank = lax.broadcasted_iota(jnp.int32, rows.shape, 0)
    rows = jnp.where(rank < counts[0], rows, MARK).astype(BF16)
    for s in range(shards):
        core = s % NCORE
        out[s] = rows[:, core * width : (core + 1) * width]


def compact_body(rows, picked, chosen, count):
    slots = rows.shape[0]
    capacity = 8
    valid = (rows[:, 0:128].astype(F32)[:, 0:1] < MARK / 2).astype(F32)
    a = lax.broadcasted_iota(jnp.int32, (slots, slots), 0)
    b = lax.broadcasted_iota(jnp.int32, (slots, slots), 1)
    spread = jnp.broadcast_to(valid, (slots, slots))
    rank = jnp.sum(jnp.where(a < b, spread, 0.0), axis=0, keepdims=True)
    mine = jnp.sum(jnp.where(a == b, spread, 0.0), axis=0, keepdims=True)
    total = jnp.sum(jnp.where(a // capacity == b // capacity, spread, 0.0), axis=0, keepdims=True)
    place = jnp.where(mine > 0.5, rank, -1.0).astype(jnp.int32)
    target = lax.broadcasted_iota(jnp.int32, (MASKED, slots), 0)
    hot = (target == place).astype(F32).astype(BF16)
    chosen[...] = hot
    picked[...] = jnp.dot(hot, rows[...], preferred_element_type=F32).astype(BF16)
    totals = jnp.broadcast_to(total, (8, slots)).astype(BF16)
    count[...] = lax.dot_general(totals, hot, NT, preferred_element_type=F32)


def logsumexp(x):
    top = jnp.max(x, axis=0, keepdims=True)
    return top + jnp.log(jnp.sum(jnp.exp(x - top), axis=0, keepdims=True))


def teacher_body(teacher, chosen, out, lse):
    rows = lax.dot_general(teacher[...], chosen[...], NT, preferred_element_type=F32)
    out[...] = rows.astype(BF16)
    lse[...] = jnp.broadcast_to(logsumexp(rows), lse.shape)


def student_body(*refs):
    blocks, (weight, lse_teacher, out, stats) = refs[:BLOCKS], refs[BLOCKS:]
    width = blocks[0].shape[1]
    y, core = lax.axis_index("y"), lax.axis_index("core")
    total = jnp.zeros(out.shape, F32)
    for i, block in enumerate(blocks):
        owner = block_of(lax.rem(y - i // NCORE + NY, NY), core if i % NCORE == 0 else 1 - core)
        total += lax.dot_general(
            weight[:, columns(owner, width)], block[...], NT, preferred_element_type=F32
        )
    out[...] = total
    both = jnp.concatenate([logsumexp(total), lse_teacher[0:1, :]], axis=0)
    stats[...] = jnp.broadcast_to(both[None], stats.shape)


def combine_body(stats, out):
    x = stats[...]
    top = jnp.max(x, axis=0)
    out[...] = top + jnp.log(jnp.sum(jnp.exp(x - top[None]), axis=0))


def logits_body(student, teacher, mine, other, count, weight, grad_logits, *parts):
    width = parts[0].shape[1]
    y, core = lax.axis_index("y"), lax.axis_index("core")
    top = jnp.maximum(mine[...], other[...])
    lse = top + jnp.log(jnp.exp(mine[...] - top) + jnp.exp(other[...] - top))
    scale = LOSS_SCALE / count[0:1, :]
    prob_student = jnp.exp(student[...] - lse[0:1, :])
    prob_teacher = jnp.exp(teacher[...].astype(F32) - lse[1:2, :])
    grad = (scale * (prob_student - prob_teacher)).astype(BF16)
    grad_logits[...] = grad
    for i, part in enumerate(parts):
        owner = block_of(lax.rem(y + i // NCORE, NY), core if i % NCORE == 0 else 1 - core)
        part[...] = lax.dot_general(
            grad, weight[:, columns(owner, width)], TN, preferred_element_type=F32
        ).astype(BF16)


def head_body(*refs):
    blocks, (grad_logits, out) = refs[:BLOCKS], refs[BLOCKS:]
    width = blocks[0].shape[1]
    y, core = lax.axis_index("y"), lax.axis_index("core")
    for i, block in enumerate(blocks):
        owner = block_of(lax.rem(y - i // NCORE + NY, NY), core if i % NCORE == 0 else 1 - core)
        out[:, columns(owner, width)] = jnp.dot(
            grad_logits[...], block[...], preferred_element_type=F32
        ).astype(BF16)


def spread_body(a, b, c, d, chosen, out):
    total = a[...].astype(F32) + b[...].astype(F32) + c[...].astype(F32) + d[...].astype(F32)
    out[...] = lax.dot_general(
        chosen[...], total.astype(BF16), TN, preferred_element_type=F32
    ).astype(BF16)


def swap_core(x):
    return lax.ppermute(x, "core", [(0, 1), (1, 0)])


def shift_y(x, k):
    return lax.ppermute(x, "y", [(i, (i + k) % NY) for i in range(NY)])


def per_device(hidden, head_weight, teacher, positions, counts):
    tokens, depth = hidden.shape
    capacity = positions.shape[1]
    shards = NX * NZ * NCORE
    slots = shards * capacity
    vocab = head_weight.shape[1]
    width = depth // BLOCKS
    weight_t, teacher_t = head_weight.T, teacher.T

    send = call(
        pick_body, shape((shards, capacity, width), BF16), positions, counts, hidden,
        specs=[SMEM, SMEM, VMEM],
    )
    rows = lax.all_to_all(send, SEQ, 0, 0, tiled=True).reshape(slots, width)
    mine, chosen, count = call(
        compact_body,
        (shape((MASKED, width), BF16), shape((MASKED, slots), BF16), shape((8, MASKED), F32)),
        rows, flops=2 * MASKED * slots * width,
    )
    blocks = []
    for k in range(NY):
        block = mine if k == 0 else shift_y(mine, k)
        blocks += [block, swap_core(block)]
    teacher_rows, lse_teacher = call(
        teacher_body, (shape((vocab, MASKED), BF16), shape((8, MASKED), F32)),
        teacher_t, chosen, flops=2 * vocab * slots * MASKED,
    )
    student, stats = call(
        student_body,
        (shape((vocab, MASKED), F32), shape((NX * NZ * NY, 2, MASKED), F32)),
        *blocks, weight_t, lse_teacher, flops=2 * vocab * depth * MASKED,
    )
    stats = lax.all_to_all(stats, CHIPS, 0, 0, tiled=True)
    half = call(combine_body, shape((2, MASKED), F32), stats)
    grad_logits, *parts = call(
        logits_body,
        (shape((vocab, MASKED), BF16),) + (shape((MASKED, width), BF16),) * BLOCKS,
        student, teacher_rows, half, swap_core(half), count, weight_t,
        flops=2 * vocab * depth * MASKED,
    )
    grad_head = call(
        head_body, shape((vocab, depth), BF16), *blocks, grad_logits,
        flops=2 * vocab * depth * MASKED,
    )
    sums = []
    for k in range(NY):
        both = parts[2 * k].astype(F32) + swap_core(parts[2 * k + 1]).astype(F32)
        sums.append(both.astype(BF16) if k == 0 else shift_y(both.astype(BF16), k))
    partial = call(
        spread_body, shape((slots, width), BF16), *sums, chosen,
        flops=2 * MASKED * slots * width,
    )
    own = slots // (shards * NY)
    partial = lax.all_to_all(partial.reshape(shards * NY, own, width), ALL, 0, 0, tiled=True)
    total = partial.reshape(NX * NZ, NCORE, NY, own, width).astype(F32).sum(axis=0)
    grad_hidden = total.transpose(2, 1, 0, 3).reshape(own, depth).astype(BF16)
    return grad_hidden, grad_head.T


def solution(mesh):
    fine = Mesh(mesh.devices.reshape(NX, NZ, NCORE, NY), ALL)
    return jax.shard_map(
        per_device,
        mesh=fine,
        in_specs=(P(SEQ, None), P(None, ALL), P(None, ALL), P(SEQ, None), P(SEQ)),
        out_specs=(P(ALL, None), P(None, ALL)),
        check_vma=False,
    )
```

```python
import jax
import jax.numpy as jnp
from jax import lax
from jax.experimental import pallas as pl
from jax.experimental.pallas import tpu as pltpu
from jax.sharding import Mesh, PartitionSpec as P

LOSS_SCALE = 1024.0
MASKED = 256
MARK = 64.0

SEQ = ("x", "z", "core")
ALL = ("x", "z", "core", "y")
CHIPS = ("x", "z", "y")
PLANE = ("x", "y")
NX, NZ, NCORE, NY = 4, 8, 2, 4
BLOCKS = NX * NY
F32, BF16 = jnp.float32, jnp.bfloat16
NT = (((1,), (1,)), ((), ()))
TN = (((0,), (0,)), ((), ()))
VMEM = pl.BlockSpec(memory_space=pltpu.VMEM)
HBM = pl.BlockSpec(memory_space=pltpu.HBM)
DMA = pltpu.SemaphoreType.DMA


def call(body, out, *args, specs=None, flops=0, scratch=()):
    leaves = jax.tree.leaves((args, out))
    nbytes = sum(x.size * x.dtype.itemsize for x in leaves)
    return pl.pallas_call(
        body,
        out_shape=out,
        in_specs=specs or [VMEM] * len(args),
        out_specs=jax.tree.map(lambda _: VMEM, out),
        scratch_shapes=list(scratch),
        cost_estimate=pl.CostEstimate(flops=flops, bytes_accessed=nbytes, transcendentals=0),
        compiler_params=pltpu.CompilerParams(vmem_limit_bytes=32 * 2**20),
    )(*args)


def shape(dims, dtype):
    return jax.ShapeDtypeStruct(dims, dtype)


def columns(block, width):
    return pl.ds(pl.multiple_of(block * width, width), width)


def pick_body(positions_hbm, counts_hbm, hidden, out, positions, counts, mine, sems):
    shards, capacity, width = out.shape
    tokens = hidden.shape[0]
    pair = NCORE * width
    y = lax.axis_index("y")
    copies = [
        pltpu.make_async_copy(positions_hbm, positions, sems.at[0]),
        pltpu.make_async_copy(counts_hbm, counts, sems.at[1]),
    ]
    for x in range(NX):
        copies.append(
            pltpu.make_async_copy(
                hidden.at[:, columns(x * NY + y, pair)],
                mine.at[:, x * pair : (x + 1) * pair],
                sems.at[2 + x],
            )
        )
    for copy in copies:
        copy.start()
    for copy in copies:
        copy.wait()
    row = lax.broadcasted_iota(jnp.int32, (2 * capacity, tokens), 0)
    column = lax.broadcasted_iota(jnp.int32, (2 * capacity, tokens), 1)
    hot = jnp.zeros((2 * capacity, tokens), F32)
    for k in range(capacity):
        hot = jnp.where((row == k) & (column == positions[0, k]), 1.0, hot)
    rows = jnp.dot(hot.astype(BF16), mine[...], preferred_element_type=F32)[:capacity]
    rank = lax.broadcasted_iota(jnp.int32, rows.shape, 0)
    rows = jnp.where(rank < counts[0], rows, MARK).astype(BF16)
    for s in range(shards):
        start = s // (NZ * NCORE) * pair + s % NCORE * width
        out[s] = rows[:, start : start + width]


def compact_body(rows, picked, chosen, count):
    slots = rows.shape[0]
    capacity = 8
    valid = (rows[...].astype(F32)[:, 0:1] < MARK / 2).astype(F32)
    a = lax.broadcasted_iota(jnp.int32, (slots, slots), 0)
    b = lax.broadcasted_iota(jnp.int32, (slots, slots), 1)
    spread = jnp.broadcast_to(valid, (slots, slots))
    rank = jnp.sum(jnp.where(a < b, spread, 0.0), axis=0, keepdims=True)
    mine = jnp.sum(jnp.where(a == b, spread, 0.0), axis=0, keepdims=True)
    total = jnp.sum(jnp.where(a // capacity == b // capacity, spread, 0.0), axis=0, keepdims=True)
    place = jnp.where(mine > 0.5, rank, -1.0).astype(jnp.int32)
    target = lax.broadcasted_iota(jnp.int32, (MASKED, slots), 0)
    hot = (target == place).astype(F32).astype(BF16)
    chosen[...] = hot
    mine = jnp.dot(hot, rows[...], preferred_element_type=F32).astype(BF16)
    for i in range(picked.shape[0]):
        picked[i] = mine
    totals = jnp.broadcast_to(total, (8, slots)).astype(BF16)
    count[...] = lax.dot_general(totals, hot, NT, preferred_element_type=F32)


def logsumexp(x):
    top = jnp.max(x, axis=0, keepdims=True)
    return top + jnp.log(jnp.sum(jnp.exp(x - top), axis=0, keepdims=True))


def stage_body(teacher_hbm, weight_hbm, chosen, out, lse, ours, theirs, back, teacher, sems):
    width = ours.shape[1] // BLOCKS
    core = lax.axis_index("core")
    move_teacher = pltpu.make_async_copy(teacher_hbm, teacher, sems.at[0])
    copies = []
    for which, (target, side) in enumerate(((ours, core), (theirs, 1 - core))):
        for b in range(BLOCKS):
            copies.append(
                pltpu.make_async_copy(
                    weight_hbm.at[:, columns(b * NCORE + side, width)],
                    target.at[:, b * width : (b + 1) * width],
                    sems.at[1 + which * BLOCKS + b],
                )
            )
    move_teacher.start()
    for copy in copies:
        copy.start()
    sent, masked = back.shape
    slots = chosen.shape[1]
    row = lax.broadcasted_iota(jnp.int32, (sent, slots), 0)
    chip, q = row // 4, row % 4
    slot = chip // NY * 16 + q // 2 * 8 + chip % NY * 2 + q % 2
    column = lax.broadcasted_iota(jnp.int32, (sent, slots), 1)
    pick = (column == slot).astype(F32).astype(BF16)
    back[...] = lax.dot_general(pick, chosen[...], NT, preferred_element_type=F32).astype(BF16)
    move_teacher.wait()
    rows = lax.dot_general(teacher[...], chosen[...], NT, preferred_element_type=F32)
    out[...] = rows.astype(BF16)
    lse[...] = jnp.broadcast_to(logsumexp(rows), lse.shape)
    for copy in copies:
        copy.wait()


def lay_out(blocks, flat):
    width = blocks.shape[2]
    for b in range(blocks.shape[0]):
        flat[:, b * width : (b + 1) * width] = blocks[b]


def student_ours_body(blocks, weight, total, flat):
    lay_out(blocks, flat)
    total[...] = lax.dot_general(weight[...], flat[...], NT, preferred_element_type=F32)


def student_theirs_body(blocks, weight, first, lse_teacher, out, stats, flat):
    lay_out(blocks, flat)
    total = first[...] + lax.dot_general(weight[...], flat[...], NT, preferred_element_type=F32)
    out[...] = total
    both = jnp.concatenate([logsumexp(total), lse_teacher[0:1, :]], axis=0)
    stats[...] = jnp.broadcast_to(both[None], stats.shape)


def combine_body(stats, out):
    x = stats[...]
    top = jnp.max(x, axis=0)
    out[...] = top + jnp.log(jnp.sum(jnp.exp(x - top[None]), axis=0))


def products(grad, weight, parts):
    width = parts.shape[2]
    for b in range(0, parts.shape[0], 2):
        both = lax.dot_general(
            grad, weight[:, b * width : (b + 2) * width], TN, preferred_element_type=F32
        ).astype(parts.dtype)
        parts[b] = both[:, :width]
        parts[b + 1] = both[:, width:]


def logits_body(student, teacher, mine, other, count, weight, grad_logits, parts):
    top = jnp.maximum(mine[...], other[...])
    lse = top + jnp.log(jnp.exp(mine[...] - top) + jnp.exp(other[...] - top))
    scale = LOSS_SCALE / count[0:1, :]
    prob_student = jnp.exp(student[...] - lse[0:1, :])
    prob_teacher = jnp.exp(teacher[...].astype(F32) - lse[1:2, :])
    grad = (scale * (prob_student - prob_teacher)).astype(BF16)
    grad_logits[...] = grad
    products(grad, weight, parts)


def products_body(grad_logits, weight, parts):
    products(grad_logits[...], weight, parts)


def head_body(ours, theirs, grad_logits, out):
    core = lax.axis_index("core")
    width = ours.shape[1] // BLOCKS
    for flat, side in ((ours, core), (theirs, 1 - core)):
        for b in range(0, BLOCKS, 2):
            both = jnp.dot(
                grad_logits[...], flat[:, b * width : (b + 2) * width], preferred_element_type=F32
            ).astype(BF16)
            out[:, columns(b * NCORE + side, width)] = both[:, :width]
            out[:, columns((b + 1) * NCORE + side, width)] = both[:, width:]


def spread_body(parts, back, out):
    total = parts[0].astype(F32)
    for i in range(1, parts.shape[0]):
        total += parts[i].astype(F32)
    rows = jnp.dot(back[...], total.astype(BF16), preferred_element_type=F32)
    out[...] = rows.astype(BF16)


def collect_body(parts, mine, other):
    chips, rows, width = parts.shape
    total = jnp.sum(parts[...].astype(F32).reshape(NX, NZ, NY, rows, width), axis=1)
    total = total.reshape(NX * NY, rows, width)
    low, high = total[:, : rows // 2], total[:, rows // 2 :]
    first = lax.axis_index("core") == 0
    mine[...] = jnp.where(first, low, high)
    other[...] = jnp.where(first, high, low)


def finish_body(mine, other, out, whole):
    blocks, rows, width = mine.shape
    first = lax.axis_index("core") == 0
    by_core = (
        jnp.where(first, mine[...], other[...]), jnp.where(first, other[...], mine[...]),
    )
    for b in range(blocks):
        for core in range(NCORE):
            start = (b * NCORE + core) * width
            whole[:, start : start + width] = by_core[core][b]
    out[...] = whole[...].astype(BF16)


def swap_core(x):
    return lax.ppermute(x, "core", [(0, 1), (1, 0)])


def per_device(hidden, head_weight, teacher, positions, counts):
    tokens, depth = hidden.shape
    capacity = positions.shape[1]
    shards = NX * NZ * NCORE
    slots = shards * capacity
    vocab = head_weight.shape[1]
    width = depth // (BLOCKS * NCORE)
    share = depth // NCORE
    own = capacity // NY
    chips = NX * NZ * NY
    products_flops = vocab * depth * MASKED
    parts_shape = shape((BLOCKS, MASKED, width), BF16)

    send = call(
        pick_body, shape((shards, capacity, width), BF16), positions, counts, hidden,
        specs=[HBM] * 3,
        scratch=[
            pltpu.SMEM(positions.shape, jnp.int32), pltpu.SMEM(counts.shape, jnp.int32),
            pltpu.VMEM((tokens, NX * NCORE * width), BF16), DMA((2 + NX,)),
        ],
    )
    rows = lax.all_to_all(send, SEQ, 0, 0, tiled=True).reshape(slots, width)
    picked, chosen, count = call(
        compact_body,
        (parts_shape, shape((MASKED, slots), BF16), shape((8, MASKED), F32)),
        rows, flops=2 * MASKED * slots * width,
    )
    blocks = lax.all_to_all(picked, PLANE, 0, 0, tiled=True)
    staged = call(
        stage_body,
        (
            shape((vocab, MASKED), BF16), shape((8, MASKED), F32),
            shape((vocab, share), BF16), shape((vocab, share), BF16),
            shape((slots, MASKED), BF16),
        ),
        teacher.T, head_weight.T, chosen, specs=[HBM, HBM, VMEM],
        scratch=[pltpu.VMEM((vocab, slots), BF16), DMA((1 + 2 * BLOCKS,))],
        flops=2 * vocab * slots * MASKED + 2 * slots * slots * MASKED,
    )
    blocks, staged = lax.optimization_barrier((blocks, staged))
    teacher_rows, lse_teacher, weight_ours, weight_theirs, back = staged
    total, flat_ours = call(
        student_ours_body,
        (shape((vocab, MASKED), F32), shape((MASKED, share), BF16)),
        blocks, weight_ours, flops=products_flops,
    )
    student, stats, flat_theirs = call(
        student_theirs_body,
        (
            shape((vocab, MASKED), F32), shape((chips, 2, MASKED), F32),
            shape((MASKED, share), BF16),
        ),
        swap_core(blocks), weight_theirs, total, lse_teacher, flops=products_flops,
    )
    stats = lax.all_to_all(stats, CHIPS, 0, 0, tiled=True)
    half = call(combine_body, shape((2, MASKED), F32), stats)
    grad_logits, parts_theirs = call(
        logits_body, (shape((vocab, MASKED), BF16), parts_shape),
        student, teacher_rows, half, swap_core(half), count, weight_theirs, flops=products_flops,
    )
    parts_ours = call(
        products_body, shape(parts_shape.shape, F32), grad_logits, weight_ours,
        flops=products_flops,
    )
    parts = (parts_ours + swap_core(parts_theirs).astype(F32)).astype(BF16)
    parts = lax.all_to_all(parts, PLANE, 0, 0, tiled=True)
    grad_head = call(
        head_body, shape((vocab, depth), BF16), flat_ours, flat_theirs, grad_logits,
        flops=2 * products_flops,
    )
    parts, grad_head = lax.optimization_barrier((parts, grad_head))
    partial = call(
        spread_body, shape((slots, width), BF16), parts, back, flops=2 * MASKED * slots * width,
    )
    partial = lax.all_to_all(
        partial.reshape(chips, NCORE * own, width), CHIPS, 0, 0, tiled=True
    )
    mine, other = call(collect_body, (shape((BLOCKS, own, width), F32),) * 2, partial)
    grad_hidden = call(
        finish_body, shape((own, depth), BF16), mine, swap_core(other),
        scratch=[pltpu.VMEM((own, depth), F32)],
    )
    return grad_hidden, grad_head.T


def solution(mesh):
    fine = Mesh(mesh.devices.reshape(NX, NZ, NCORE, NY), ALL)
    return jax.shard_map(
        per_device,
        mesh=fine,
        in_specs=(P(SEQ, None), P(None, ALL), P(None, ALL), P(SEQ, None), P(SEQ)),
        out_specs=(P(ALL, None), P(None, ALL)),
        check_vma=False,
    )
```

```python
import jax
import jax.numpy as jnp
from jax import lax
from jax.experimental import pallas as pl
from jax.experimental.pallas import tpu as pltpu
from jax.sharding import Mesh, PartitionSpec as P

LOSS_SCALE = 1024.0
MASKED = 256
MARK = 64.0

SEQ = ("x", "z", "core")
ALL = ("x", "z", "core", "y")
CHIPS = ("x", "z", "y")
PLANE = ("x", "y")
NX, NZ, NCORE, NY = 4, 8, 2, 4
BLOCKS = NX * NY
F32, BF16 = jnp.float32, jnp.bfloat16
NT = (((1,), (1,)), ((), ()))
TN = (((0,), (0,)), ((), ()))
VMEM = pl.BlockSpec(memory_space=pltpu.VMEM)
HBM = pl.BlockSpec(memory_space=pltpu.HBM)
DMA = pltpu.SemaphoreType.DMA
LIMIT, WIDE_LIMIT = 32, 60


def call(body, out, *args, specs=None, outs=VMEM, flops=0, scratch=(), limit=LIMIT):
    leaves = jax.tree.leaves((args, out))
    nbytes = sum(x.size * x.dtype.itemsize for x in leaves)
    return pl.pallas_call(
        body,
        out_shape=out,
        in_specs=specs or [VMEM] * len(args),
        out_specs=jax.tree.map(lambda _: outs, out),
        scratch_shapes=list(scratch),
        cost_estimate=pl.CostEstimate(flops=flops, bytes_accessed=nbytes, transcendentals=0),
        compiler_params=pltpu.CompilerParams(vmem_limit_bytes=limit * 2**20),
    )(*args)


def shape(dims, dtype):
    return jax.ShapeDtypeStruct(dims, dtype)


def columns(block, width):
    return pl.ds(pl.multiple_of(block * width, width), width)


def pick_body(positions_hbm, counts_hbm, hidden, out, positions, counts, mine, sems):
    shards, capacity, width = out.shape
    tokens = hidden.shape[0]
    pair = NCORE * width
    y = lax.axis_index("y")
    copies = [
        pltpu.make_async_copy(positions_hbm, positions, sems.at[0]),
        pltpu.make_async_copy(counts_hbm, counts, sems.at[1]),
    ]
    for x in range(NX):
        copies.append(
            pltpu.make_async_copy(
                hidden.at[:, columns(x * NY + y, pair)],
                mine.at[:, x * pair : (x + 1) * pair],
                sems.at[2 + x],
            )
        )
    for copy in copies:
        copy.start()
    for copy in copies:
        copy.wait()
    row = lax.broadcasted_iota(jnp.int32, (2 * capacity, tokens), 0)
    column = lax.broadcasted_iota(jnp.int32, (2 * capacity, tokens), 1)
    hot = jnp.zeros((2 * capacity, tokens), F32)
    for k in range(capacity):
        hot = jnp.where((row == k) & (column == positions[0, k]), 1.0, hot)
    rows = jnp.dot(hot.astype(BF16), mine[...], preferred_element_type=F32)[:capacity]
    rank = lax.broadcasted_iota(jnp.int32, rows.shape, 0)
    rows = jnp.where(rank < counts[0], rows, MARK).astype(BF16)
    for s in range(shards):
        start = s // (NZ * NCORE) * pair + s % NCORE * width
        out[s] = rows[:, start : start + width]


def compact_body(rows, picked, chosen, count):
    slots = rows.shape[0]
    capacity = 8
    valid = (rows[...].astype(F32)[:, 0:1] < MARK / 2).astype(F32)
    a = lax.broadcasted_iota(jnp.int32, (slots, slots), 0)
    b = lax.broadcasted_iota(jnp.int32, (slots, slots), 1)
    spread = jnp.broadcast_to(valid, (slots, slots))
    rank = jnp.sum(jnp.where(a < b, spread, 0.0), axis=0, keepdims=True)
    mine = jnp.sum(jnp.where(a == b, spread, 0.0), axis=0, keepdims=True)
    total = jnp.sum(jnp.where(a // capacity == b // capacity, spread, 0.0), axis=0, keepdims=True)
    place = jnp.where(mine > 0.5, rank, -1.0).astype(jnp.int32)
    target = lax.broadcasted_iota(jnp.int32, (MASKED, slots), 0)
    hot = (target == place).astype(F32).astype(BF16)
    chosen[...] = hot
    mine = jnp.dot(hot, rows[...], preferred_element_type=F32).astype(BF16)
    for i in range(picked.shape[0]):
        picked[i] = mine
    totals = jnp.broadcast_to(total, (8, slots)).astype(BF16)
    count[...] = lax.dot_general(totals, hot, NT, preferred_element_type=F32)


def logsumexp(x):
    top = jnp.max(x, axis=0, keepdims=True)
    return top + jnp.log(jnp.sum(jnp.exp(x - top), axis=0, keepdims=True))


def teacher_body(teacher_hbm, chosen, out, lse, back, teacher, sem):
    move = pltpu.make_async_copy(teacher_hbm, teacher, sem)
    move.start()
    sent, masked = back.shape
    slots = chosen.shape[1]
    row = lax.broadcasted_iota(jnp.int32, (sent, slots), 0)
    chip, q = row // 4, row % 4
    slot = chip // NY * 16 + q // 2 * 8 + chip % NY * 2 + q % 2
    column = lax.broadcasted_iota(jnp.int32, (sent, slots), 1)
    pick = (column == slot).astype(F32).astype(BF16)
    back[...] = lax.dot_general(pick, chosen[...], NT, preferred_element_type=F32).astype(BF16)
    move.wait()
    rows = lax.dot_general(teacher[...], chosen[...], NT, preferred_element_type=F32)
    out[...] = rows.astype(BF16)
    lse[...] = jnp.broadcast_to(logsumexp(rows), lse.shape)


def load_blocks(weight_hbm, target, side, sems):
    width = target.shape[1] // BLOCKS
    copies = [
        pltpu.make_async_copy(
            weight_hbm.at[:, columns(b * NCORE + side, width)],
            target.at[:, b * width : (b + 1) * width],
            sems.at[b],
        )
        for b in range(BLOCKS)
    ]
    for copy in copies:
        copy.start()
    return copies


def lay_out(blocks, flat):
    width = blocks.shape[2]
    for b in range(blocks.shape[0]):
        flat[:, b * width : (b + 1) * width] = blocks[b]


def student_ours_body(blocks, weight_hbm, total, theirs, ours, flat, sems, their_sems):
    core = lax.axis_index("core")
    copies = load_blocks(weight_hbm, ours, core, sems)
    later = load_blocks(weight_hbm, theirs, 1 - core, their_sems)
    lay_out(blocks, flat)
    for copy in copies:
        copy.wait()
    total[...] = lax.dot_general(ours[...], flat[...], NT, preferred_element_type=F32)
    for copy in later:
        copy.wait()


def student_theirs_body(blocks, weight, first, lse_teacher, out, stats, flat):
    lay_out(blocks, flat)
    total = first[...] + lax.dot_general(weight[...], flat[...], NT, preferred_element_type=F32)
    out[...] = total
    both = jnp.concatenate([logsumexp(total), lse_teacher[0:1, :]], axis=0)
    stats[...] = jnp.broadcast_to(both[None], stats.shape)


def combine_body(stats, out):
    x = stats[...]
    top = jnp.max(x, axis=0)
    out[...] = top + jnp.log(jnp.sum(jnp.exp(x - top[None]), axis=0))


def products(grad, copies, weight, parts):
    width = parts.shape[2]
    for b in range(0, parts.shape[0], 2):
        copies[b].wait()
        copies[b + 1].wait()
        both = lax.dot_general(
            grad, weight[:, b * width : (b + 2) * width], TN, preferred_element_type=F32
        ).astype(parts.dtype)
        parts[b] = both[:, :width]
        parts[b + 1] = both[:, width:]


def logits_body(student, teacher, mine, other, count, weight_hbm, grad_logits, parts, weight, sems):
    copies = load_blocks(weight_hbm, weight, 1 - lax.axis_index("core"), sems)
    top = jnp.maximum(mine[...], other[...])
    lse = top + jnp.log(jnp.exp(mine[...] - top) + jnp.exp(other[...] - top))
    scale = LOSS_SCALE / count[0:1, :]
    prob_student = jnp.exp(student[...] - lse[0:1, :])
    prob_teacher = jnp.exp(teacher[...].astype(F32) - lse[1:2, :])
    grad = (scale * (prob_student - prob_teacher)).astype(BF16)
    grad_logits[...] = grad
    products(grad, copies, weight, parts)


def products_body(grad_logits, weight_hbm, parts, weight, sems):
    copies = load_blocks(weight_hbm, weight, lax.axis_index("core"), sems)
    products(grad_logits[...], copies, weight, parts)


def head_body(ours, theirs, grad_logits, out_hbm, flat_ours, flat_theirs, out, sems):
    core = lax.axis_index("core")
    width = ours.shape[2]
    lay_out(ours, flat_ours)
    lay_out(theirs, flat_theirs)
    copies = []
    for b in range(0, BLOCKS, 2):
        for flat, side in ((flat_ours, core), (flat_theirs, 1 - core)):
            both = jnp.dot(
                grad_logits[...], flat[:, b * width : (b + 2) * width], preferred_element_type=F32
            ).astype(BF16)
            out[:, columns(b * NCORE + side, width)] = both[:, :width]
            out[:, columns((b + 1) * NCORE + side, width)] = both[:, width:]
        span = slice(b * NCORE * width, (b + 2) * NCORE * width)
        copy = pltpu.make_async_copy(out.at[:, span], out_hbm.at[:, span], sems.at[b])
        copy.start()
        copies.append(copy)
    for copy in copies:
        copy.wait()


def spread_body(parts, back, out):
    total = parts[0].astype(F32)
    for i in range(1, parts.shape[0]):
        total += parts[i].astype(F32)
    rows = jnp.dot(back[...], total.astype(BF16), preferred_element_type=F32)
    out[...] = rows.astype(BF16)


def collect_body(parts, mine, other):
    chips, rows, width = parts.shape
    total = jnp.sum(parts[...].astype(F32).reshape(NX, NZ, NY, rows, width), axis=1)
    total = total.reshape(NX * NY, rows, width)
    low, high = total[:, : rows // 2], total[:, rows // 2 :]
    first = lax.axis_index("core") == 0
    mine[...] = jnp.where(first, low, high)
    other[...] = jnp.where(first, high, low)


def finish_body(mine, other, out, whole):
    blocks, rows, width = mine.shape
    first = lax.axis_index("core") == 0
    by_core = (
        jnp.where(first, mine[...], other[...]), jnp.where(first, other[...], mine[...]),
    )
    for b in range(blocks):
        for core in range(NCORE):
            start = (b * NCORE + core) * width
            whole[:, start : start + width] = by_core[core][b]
    out[...] = whole[...].astype(BF16)


def swap_core(x):
    return lax.ppermute(x, "core", [(0, 1), (1, 0)])


def per_device(hidden, head_weight, teacher, positions, counts):
    tokens, depth = hidden.shape
    capacity = positions.shape[1]
    shards = NX * NZ * NCORE
    slots = shards * capacity
    vocab = head_weight.shape[1]
    width = depth // (BLOCKS * NCORE)
    share = depth // NCORE
    own = capacity // NY
    chips = NX * NZ * NY
    products_flops = vocab * depth * MASKED
    parts_shape = shape((BLOCKS, MASKED, width), BF16)

    send = call(
        pick_body, shape((shards, capacity, width), BF16), positions, counts, hidden,
        specs=[HBM] * 3,
        scratch=[
            pltpu.SMEM(positions.shape, jnp.int32), pltpu.SMEM(counts.shape, jnp.int32),
            pltpu.VMEM((tokens, NX * NCORE * width), BF16), DMA((2 + NX,)),
        ],
        limit=WIDE_LIMIT,
    )
    rows = lax.all_to_all(send, SEQ, 0, 0, tiled=True).reshape(slots, width)
    picked, chosen, count = call(
        compact_body,
        (parts_shape, shape((MASKED, slots), BF16), shape((8, MASKED), F32)),
        rows, flops=2 * MASKED * slots * width,
    )
    blocks = lax.all_to_all(picked, PLANE, 0, 0, tiled=True)
    swapped = swap_core(blocks)
    blocks, chosen = lax.optimization_barrier((blocks, chosen))
    staged = call(
        teacher_body,
        (
            shape((vocab, MASKED), BF16), shape((8, MASKED), F32), shape((slots, MASKED), BF16),
        ),
        teacher.T, chosen, specs=[HBM, VMEM],
        scratch=[pltpu.VMEM((vocab, slots), BF16), DMA(())],
        flops=2 * vocab * slots * MASKED + 2 * slots * slots * MASKED,
    )
    weight = head_weight.T
    some_weight, flat = pltpu.VMEM((vocab, share), BF16), pltpu.VMEM((MASKED, share), BF16)
    total, weight_theirs = call(
        student_ours_body,
        (shape((vocab, MASKED), F32), shape((vocab, share), BF16)),
        blocks, weight, specs=[VMEM, HBM],
        scratch=[some_weight, flat, DMA((BLOCKS,)), DMA((BLOCKS,))],
        flops=products_flops,
    )
    swapped, staged, total = lax.optimization_barrier((swapped, staged, total))
    teacher_rows, lse_teacher, back = staged
    student, stats = call(
        student_theirs_body,
        (shape((vocab, MASKED), F32), shape((chips, 2, MASKED), F32)),
        swapped, weight_theirs, total, lse_teacher, scratch=[flat], flops=products_flops,
    )
    stats = lax.all_to_all(stats, CHIPS, 0, 0, tiled=True)
    half = call(combine_body, shape((2, MASKED), F32), stats)
    grad_logits, parts_theirs = call(
        logits_body, (shape((vocab, MASKED), BF16), parts_shape),
        student, teacher_rows, half, swap_core(half), count, weight, specs=[VMEM] * 5 + [HBM],
        scratch=[some_weight, DMA((BLOCKS,))], flops=products_flops,
    )
    parts_ours = call(
        products_body, shape(parts_shape.shape, F32), grad_logits, weight, specs=[VMEM, HBM],
        scratch=[some_weight, DMA((BLOCKS,))], flops=products_flops,
    )
    grad_head = call(
        head_body, shape((vocab, depth), BF16), blocks, swapped, grad_logits,
        outs=HBM, scratch=[flat, flat, pltpu.VMEM((vocab, depth), BF16), DMA((BLOCKS,))],
        flops=2 * products_flops,
    )
    parts_theirs, parts_ours, grad_head = lax.optimization_barrier(
        (swap_core(parts_theirs), parts_ours, grad_head)
    )
    parts = (parts_ours + parts_theirs.astype(F32)).astype(BF16)
    parts = lax.all_to_all(parts, PLANE, 0, 0, tiled=True)
    partial = call(
        spread_body, shape((slots, width), BF16), parts, back, flops=2 * MASKED * slots * width,
    )
    partial = lax.all_to_all(
        partial.reshape(chips, NCORE * own, width), CHIPS, 0, 0, tiled=True
    )
    mine, other = call(collect_body, (shape((BLOCKS, own, width), F32),) * 2, partial)
    grad_hidden = call(
        finish_body, shape((own, depth), BF16), mine, swap_core(other),
        scratch=[pltpu.VMEM((own, depth), F32)],
    )
    return grad_hidden, grad_head.T


def solution(mesh):
    fine = Mesh(mesh.devices.reshape(NX, NZ, NCORE, NY), ALL)
    return jax.shard_map(
        per_device,
        mesh=fine,
        in_specs=(P(SEQ, None), P(None, ALL), P(None, ALL), P(SEQ, None), P(SEQ)),
        out_specs=(P(ALL, None), P(None, ALL)),
        check_vma=False,
    )
```

```python
import jax
import jax.numpy as jnp
from jax import lax
from jax.experimental import pallas as pl
from jax.experimental.pallas import tpu as pltpu
from jax.sharding import Mesh, PartitionSpec as P

LOSS_SCALE = 1024.0
MASKED = 256
MARK = 64.0

SEQ = ("x", "z", "core")
ALL = ("x", "z", "core", "y")
CHIPS = ("x", "z", "y")
PLANE = ("x", "y")
NX, NZ, NCORE, NY = 4, 8, 2, 4
BLOCKS = NX * NY
F32, BF16 = jnp.float32, jnp.bfloat16
NT = (((1,), (1,)), ((), ()))
TN = (((0,), (0,)), ((), ()))
VMEM = pl.BlockSpec(memory_space=pltpu.VMEM)
HBM = pl.BlockSpec(memory_space=pltpu.HBM)
DMA = pltpu.SemaphoreType.DMA
LIMIT, PICK_LIMIT = 32 << 20, 62717952


def call(body, out, *args, specs=None, outs=VMEM, flops=0, scratch=(), limit=LIMIT):
    leaves = jax.tree.leaves((args, out))
    nbytes = sum(x.size * x.dtype.itemsize for x in leaves)
    return pl.pallas_call(
        body,
        out_shape=out,
        in_specs=specs or [VMEM] * len(args),
        out_specs=jax.tree.map(lambda _: outs, out),
        scratch_shapes=list(scratch),
        cost_estimate=pl.CostEstimate(flops=flops, bytes_accessed=nbytes, transcendentals=0),
        compiler_params=pltpu.CompilerParams(vmem_limit_bytes=limit),
    )(*args)


def shape(dims, dtype):
    return jax.ShapeDtypeStruct(dims, dtype)


def columns(block, width):
    return pl.ds(pl.multiple_of(block * width, width), width)


def part_of(y, core):
    return y * NCORE + core


def pick_body(positions_hbm, counts_hbm, hidden, out, positions, counts, mine, sems):
    shards, capacity, width = out.shape
    tokens = hidden.shape[0]
    y = lax.axis_index("y")
    copies = [
        pltpu.make_async_copy(positions_hbm, positions, sems.at[0]),
        pltpu.make_async_copy(counts_hbm, counts, sems.at[1]),
        pltpu.make_async_copy(hidden.at[:, columns(y, mine.shape[1])], mine, sems.at[2]),
    ]
    for copy in copies:
        copy.start()
    for copy in copies:
        copy.wait()
    row = lax.broadcasted_iota(jnp.int32, (2 * capacity, tokens), 0)
    column = lax.broadcasted_iota(jnp.int32, (2 * capacity, tokens), 1)
    hot = jnp.zeros((2 * capacity, tokens), F32)
    for k in range(capacity):
        hot = jnp.where((row == k) & (column == positions[0, k]), 1.0, hot)
    rows = jnp.dot(hot.astype(BF16), mine[...], preferred_element_type=F32)[:capacity]
    rank = lax.broadcasted_iota(jnp.int32, rows.shape, 0)
    rows = jnp.where(rank < counts[0, 0], rows, MARK).astype(BF16)
    for s in range(shards):
        start = (s % NCORE * NX + s // (NZ * NCORE)) * width
        out[s] = rows[:, start : start + width]


def compact_body(rows, picked, chosen, count):
    slots = rows.shape[0]
    capacity = 8
    valid = (rows[...].astype(F32)[:, 0:1] < MARK / 2).astype(F32)
    a = lax.broadcasted_iota(jnp.int32, (slots, slots), 0)
    b = lax.broadcasted_iota(jnp.int32, (slots, slots), 1)
    spread = jnp.broadcast_to(valid, (slots, slots))
    rank = jnp.sum(jnp.where(a < b, spread, 0.0), axis=0, keepdims=True)
    mine = jnp.sum(jnp.where(a == b, spread, 0.0), axis=0, keepdims=True)
    total = jnp.sum(jnp.where(a // capacity == b // capacity, spread, 0.0), axis=0, keepdims=True)
    place = jnp.where(mine > 0.5, rank, -1.0).astype(jnp.int32)
    target = lax.broadcasted_iota(jnp.int32, (MASKED, slots), 0)
    hot = (target == place).astype(F32).astype(BF16)
    chosen[...] = hot
    mine = jnp.dot(hot, rows[...], preferred_element_type=F32).astype(BF16)
    for i in range(picked.shape[0]):
        picked[i] = mine
    totals = jnp.broadcast_to(total, (8, slots)).astype(BF16)
    count[...] = lax.dot_general(totals, hot, NT, preferred_element_type=F32)


def logsumexp(x):
    top = jnp.max(x, axis=0, keepdims=True)
    return top + jnp.log(jnp.sum(jnp.exp(x - top), axis=0, keepdims=True))


def teacher_body(teacher_hbm, chosen, out, lse, back, teacher, sem):
    move = pltpu.make_async_copy(teacher_hbm, teacher, sem)
    move.start()
    halves, sent, masked = back.shape
    slots = chosen.shape[1]
    row = lax.broadcasted_iota(jnp.int32, (sent, slots), 0)
    chip, q = row // 8, row % 8
    slot = chip // NY * 16 + q // 4 * 8 + chip % NY * 2 + q // 2 % 2
    column = lax.broadcasted_iota(jnp.int32, (sent, slots), 1)
    pick = (column == slot).astype(F32).astype(BF16)
    placed = lax.dot_general(pick, chosen[...], NT, preferred_element_type=F32)
    odd = lax.broadcasted_iota(jnp.int32, (sent, masked), 0) % 2
    for h in range(halves):
        back[h] = jnp.where(odd == h, placed, 0.0).astype(BF16)
    move.wait()
    rows = lax.dot_general(teacher[...], chosen[...], NT, preferred_element_type=F32)
    out[...] = rows.astype(BF16)
    lse[...] = jnp.broadcast_to(logsumexp(rows), lse.shape)


def lay_out(blocks, flat):
    width = blocks.shape[2]
    for x in range(NX):
        for y in range(NY):
            start = (y * NX + x) * width
            flat[:, start : start + width] = blocks[x * NY + y]


def student_part(blocks, weight, side, flat):
    lay_out(blocks, flat)
    width = flat.shape[1] // NY
    total = jnp.zeros((weight.shape[0], MASKED), F32)
    for y in range(NY):
        total += lax.dot_general(
            weight[:, columns(part_of(y, side), width)], flat[:, y * width : (y + 1) * width],
            NT, preferred_element_type=F32,
        )
    return total


def student_ours_body(blocks, weight, total, flat):
    total[...] = student_part(blocks, weight, lax.axis_index("core"), flat)


def student_theirs_body(blocks, weight, first, lse_teacher, out, stats, flat):
    total = first[...] + student_part(blocks, weight, 1 - lax.axis_index("core"), flat)
    out[...] = total
    both = jnp.concatenate([logsumexp(total), lse_teacher[0:1, :]], axis=0)
    stats[...] = jnp.broadcast_to(both[None], stats.shape)


def combine_body(stats, out):
    x = stats[...]
    top = jnp.max(x, axis=0)
    out[...] = top + jnp.log(jnp.sum(jnp.exp(x - top[None]), axis=0))


def products(grad, weight, side, parts):
    y = lax.axis_index("y")
    for k, part in enumerate(parts):
        owner = part_of(lax.rem(y + k, NY), side)
        part[...] = lax.dot_general(
            grad, weight[:, columns(owner, part.shape[1])], TN, preferred_element_type=F32
        ).astype(part.dtype)


def logits_body(student, teacher, mine, other, count, weight, grad_logits, *parts):
    top = jnp.maximum(mine[...], other[...])
    lse = top + jnp.log(jnp.exp(mine[...] - top) + jnp.exp(other[...] - top))
    scale = LOSS_SCALE / count[0:1, :]
    prob_student = jnp.exp(student[...] - lse[0:1, :])
    prob_teacher = jnp.exp(teacher[...].astype(F32) - lse[1:2, :])
    grad = (scale * (prob_student - prob_teacher)).astype(BF16)
    grad_logits[...] = grad
    products(grad, weight, 1 - lax.axis_index("core"), parts)


def products_body(grad_logits, weight, *parts):
    products(grad_logits[...], weight, lax.axis_index("core"), parts)


def head_body(ours, theirs, grad_logits, out_hbm, flat_ours, flat_theirs, out, sems):
    core = lax.axis_index("core")
    width = flat_ours.shape[1] // NY
    lay_out(ours, flat_ours)
    lay_out(theirs, flat_theirs)
    copies = []
    for y in range(NY):
        for flat, side in ((flat_ours, core), (flat_theirs, 1 - core)):
            out[:, columns(part_of(y, side), width)] = jnp.dot(
                grad_logits[...], flat[:, y * width : (y + 1) * width], preferred_element_type=F32
            ).astype(BF16)
        span = slice(y * NCORE * width, (y + 1) * NCORE * width)
        copy = pltpu.make_async_copy(out.at[:, span], out_hbm.at[:, span], sems.at[y])
        copy.start()
        copies.append(copy)
    for copy in copies:
        copy.wait()


def spread_body(a, b, c, d, back, out):
    total = a[...].astype(F32) + b[...].astype(F32) + c[...].astype(F32) + d[...].astype(F32)
    total = total.astype(BF16)
    half = out.shape[1]
    out[...] = (
        jnp.dot(back[0], total[:, :half], preferred_element_type=F32)
        + jnp.dot(back[1], total[:, half:], preferred_element_type=F32)
    ).astype(BF16)


def collect_body(parts, mine, other):
    chips, rows, half = parts.shape
    total = jnp.sum(parts[...].astype(F32).reshape(NX * NZ, NY, rows, half), axis=0)
    low, high = total[:, : rows // 2], total[:, rows // 2 :]
    first = lax.axis_index("core") == 0
    mine[...] = jnp.where(first, low, high)
    other[...] = jnp.where(first, high, low)


def finish_body(mine, other, out, whole):
    half = mine.shape[2]
    first = lax.axis_index("core") == 0
    by_core = (
        jnp.where(first, mine[...], other[...]), jnp.where(first, other[...], mine[...]),
    )
    for i in range(out.shape[0]):
        for y in range(NY):
            for core in range(NCORE):
                for h in range(2):
                    start = (part_of(y, core) * 2 + h) * half
                    row = 2 * i + h
                    whole[i : i + 1, start : start + half] = by_core[core][y, row : row + 1]
    out[...] = whole[...].astype(BF16)


def swap_core(x):
    return lax.ppermute(x, "core", [(0, 1), (1, 0)])


def shift_y(x, k):
    return lax.ppermute(x, "y", [(i, (i + k) % NY) for i in range(NY)])


def per_device(hidden, head_weight, teacher, positions, counts):
    tokens, depth = hidden.shape
    capacity = positions.shape[1]
    shards = NX * NZ * NCORE
    slots = shards * capacity
    vocab = head_weight.shape[1]
    part = depth // (NY * NCORE)
    width = part // NX
    own = capacity // NY
    chips = NX * NZ * NY
    weight = head_weight.T
    half_flops = vocab * depth * MASKED
    logits_shape = shape((vocab, MASKED), F32)
    flat = pltpu.VMEM((MASKED, depth // NCORE), BF16)

    send = call(
        pick_body, shape((shards, capacity, width), BF16),
        positions, counts.reshape(1, 1), hidden, specs=[HBM] * 3,
        scratch=[
            pltpu.SMEM(positions.shape, jnp.int32), pltpu.SMEM((1, 1), jnp.int32),
            pltpu.VMEM((tokens, depth // NY), BF16), DMA((3,)),
        ],
        limit=PICK_LIMIT,
    )
    rows = lax.all_to_all(send, SEQ, 0, 0, tiled=True).reshape(slots, width)
    picked, chosen, count = call(
        compact_body,
        (
            shape((BLOCKS, MASKED, width), BF16), shape((MASKED, slots), BF16),
            shape((8, MASKED), F32),
        ),
        rows, flops=2 * MASKED * slots * width,
    )
    blocks = lax.all_to_all(picked, PLANE, 0, 0, tiled=True)
    swapped = swap_core(blocks)
    blocks, chosen = lax.optimization_barrier((blocks, chosen))
    staged = call(
        teacher_body,
        (
            shape((vocab, MASKED), BF16), shape((8, MASKED), F32),
            shape((2, 2 * slots, MASKED), BF16),
        ),
        teacher.T, chosen, specs=[HBM, VMEM],
        scratch=[pltpu.VMEM((vocab, slots), BF16), DMA(())],
        flops=2 * vocab * slots * MASKED + 4 * slots * slots * MASKED,
    )
    total = call(
        student_ours_body, logits_shape, blocks, weight, scratch=[flat], flops=half_flops
    )
    swapped, staged, total = lax.optimization_barrier((swapped, staged, total))
    teacher_rows, lse_teacher, back = staged
    student, stats = call(
        student_theirs_body, (logits_shape, shape((chips, 2, MASKED), F32)),
        swapped, weight, total, lse_teacher, scratch=[flat], flops=half_flops,
    )
    stats = lax.all_to_all(stats, CHIPS, 0, 0, tiled=True)
    lse = call(combine_body, shape((2, MASKED), F32), stats)
    grad_logits, *theirs = call(
        logits_body,
        (shape((vocab, MASKED), BF16),) + (shape((MASKED, part), BF16),) * NY,
        student, teacher_rows, lse, swap_core(lse), count, weight, flops=half_flops,
    )
    ours = call(
        products_body, (shape((MASKED, part), F32),) * NY, grad_logits, weight, flops=half_flops
    )
    sums = [(a + swap_core(b).astype(F32)).astype(BF16) for a, b in zip(ours, theirs)]
    sums = sums[:1] + [shift_y(sums[k], k) for k in range(1, NY)]
    grad_head = call(
        head_body, shape((vocab, depth), BF16), blocks, swapped, grad_logits, outs=HBM,
        scratch=[flat, flat, pltpu.VMEM((vocab, depth), BF16), DMA((NY,))],
        flops=2 * half_flops,
    )
    sums[1], grad_head = lax.optimization_barrier((sums[1], grad_head))
    partial = call(
        spread_body, shape((2 * slots, part // 2), BF16), *sums, back,
        flops=4 * MASKED * slots * part,
    )
    partial = lax.all_to_all(partial.reshape(chips, 8, part // 2), CHIPS, 0, 0, tiled=True)
    mine, other = call(collect_body, (shape((NY, 4, part // 2), F32),) * 2, partial)
    grad_hidden = call(
        finish_body, shape((own, depth), BF16), mine, swap_core(other),
        scratch=[pltpu.VMEM((own, depth), F32)],
    )
    return grad_hidden, grad_head.T


def solution(mesh):
    fine = Mesh(mesh.devices.reshape(NX, NZ, NCORE, NY), ALL)
    return jax.shard_map(
        per_device,
        mesh=fine,
        in_specs=(P(SEQ, None), P(None, ALL), P(None, ALL), P(SEQ, None), P(SEQ)),
        out_specs=(P(ALL, None), P(None, ALL)),
        check_vma=False,
    )
```

```python
import jax
import jax.numpy as jnp
from jax import lax
from jax.experimental import pallas as pl
from jax.experimental.pallas import tpu as pltpu
from jax.sharding import Mesh, PartitionSpec as P

LOSS_SCALE = 1024.0
MASKED = 256
MARK = 64.0

SEQ = ("x", "z", "core")
ALL = ("x", "z", "core", "y")
CHIPS = ("x", "z", "y")
NX, NZ, NCORE, NY = 4, 8, 2, 4
RING = 4
assert NX == NY == RING
F32, BF16 = jnp.float32, jnp.bfloat16
NT = (((1,), (1,)), ((), ()))
TN = (((0,), (0,)), ((), ()))
VMEM = pl.BlockSpec(memory_space=pltpu.VMEM)
HBM = pl.BlockSpec(memory_space=pltpu.HBM)
DMA = pltpu.SemaphoreType.DMA
LIMIT, PICK_LIMIT = 32 << 20, 62717952


def call(body, out, *args, specs=None, outs=VMEM, flops=0, scratch=(), limit=LIMIT):
    leaves = jax.tree.leaves((args, out))
    nbytes = sum(x.size * x.dtype.itemsize for x in leaves)
    return pl.pallas_call(
        body,
        out_shape=out,
        in_specs=specs or [VMEM] * len(args),
        out_specs=jax.tree.map(lambda _: outs, out),
        scratch_shapes=list(scratch),
        cost_estimate=pl.CostEstimate(flops=flops, bytes_accessed=nbytes, transcendentals=0),
        compiler_params=pltpu.CompilerParams(vmem_limit_bytes=limit),
    )(*args)


def shape(dims, dtype):
    return jax.ShapeDtypeStruct(dims, dtype)


def columns(block, width):
    return pl.ds(pl.multiple_of(block * width, width), width)


def place(core):
    return jnp.where(core == 0, lax.axis_index("y"), lax.axis_index("x"))


def part_at(side, steps):
    core = lax.axis_index("core")
    core = core if side == 0 else 1 - core
    return core * RING + lax.rem(place(core) + steps + RING, RING)


def pick_body(positions_hbm, counts_hbm, hidden, out, positions, counts, mine, sems):
    shards, capacity, width = out.shape
    tokens, depth = hidden.shape
    copies = [
        pltpu.make_async_copy(positions_hbm, positions, sems.at[0]),
        pltpu.make_async_copy(counts_hbm, counts, sems.at[1]),
        pltpu.make_async_copy(
            hidden.at[:, columns(lax.axis_index("y"), width)], mine.at[:, :width], sems.at[2]
        ),
        pltpu.make_async_copy(hidden.at[:, depth // 2 :], mine.at[:, width:], sems.at[3]),
    ]
    for copy in copies:
        copy.start()
    for copy in copies:
        copy.wait()
    row = lax.broadcasted_iota(jnp.int32, (2 * capacity, tokens), 0)
    column = lax.broadcasted_iota(jnp.int32, (2 * capacity, tokens), 1)
    hot = jnp.zeros((2 * capacity, tokens), F32)
    for k in range(capacity):
        hot = jnp.where((row == k) & (column == positions[0, k]), 1.0, hot)
    rows = jnp.dot(hot.astype(BF16), mine[...], preferred_element_type=F32)[:capacity]
    rank = lax.broadcasted_iota(jnp.int32, rows.shape, 0)
    rows = jnp.where(rank < counts[0, 0], rows, MARK).astype(BF16)
    for s in range(shards):
        start = s % NCORE * (1 + s // (NZ * NCORE)) * width
        out[s] = rows[:, start : start + width]


def compact_body(rows, picked, chosen, count):
    slots = rows.shape[0]
    capacity = 8
    valid = (rows[...].astype(F32)[:, 0:1] < MARK / 2).astype(F32)
    a = lax.broadcasted_iota(jnp.int32, (slots, slots), 0)
    b = lax.broadcasted_iota(jnp.int32, (slots, slots), 1)
    spread = jnp.broadcast_to(valid, (slots, slots))
    rank = jnp.sum(jnp.where(a < b, spread, 0.0), axis=0, keepdims=True)
    mine = jnp.sum(jnp.where(a == b, spread, 0.0), axis=0, keepdims=True)
    total = jnp.sum(jnp.where(a // capacity == b // capacity, spread, 0.0), axis=0, keepdims=True)
    place = jnp.where(mine > 0.5, rank, -1.0).astype(jnp.int32)
    target = lax.broadcasted_iota(jnp.int32, (MASKED, slots), 0)
    hot = (target == place).astype(F32).astype(BF16)
    chosen[...] = hot
    picked[...] = jnp.dot(hot, rows[...], preferred_element_type=F32).astype(BF16)
    totals = jnp.broadcast_to(total, (8, slots)).astype(BF16)
    count[...] = lax.dot_general(totals, hot, NT, preferred_element_type=F32)


def logsumexp(x):
    top = jnp.max(x, axis=0, keepdims=True)
    return top + jnp.log(jnp.sum(jnp.exp(x - top), axis=0, keepdims=True))


def teacher_body(teacher_hbm, chosen, out, lse, back, teacher, sem):
    move = pltpu.make_async_copy(teacher_hbm, teacher, sem)
    move.start()
    halves, sent, masked = back.shape
    slots = chosen.shape[1]
    row = lax.broadcasted_iota(jnp.int32, (sent, slots), 0)
    chip, q = row // 8, row % 8
    slot = chip // NY * 16 + q // 4 * 8 + chip % NY * 2 + q // 2 % 2
    column = lax.broadcasted_iota(jnp.int32, (sent, slots), 1)
    pick = (column == slot).astype(F32).astype(BF16)
    placed = lax.dot_general(pick, chosen[...], NT, preferred_element_type=F32)
    odd = lax.broadcasted_iota(jnp.int32, (sent, masked), 0) % 2
    for h in range(halves):
        back[h] = jnp.where(odd == h, placed, 0.0).astype(BF16)
    move.wait()
    rows = lax.dot_general(teacher[...], chosen[...], NT, preferred_element_type=F32)
    out[...] = rows.astype(BF16)
    lse[...] = jnp.broadcast_to(logsumexp(rows), lse.shape)


def student_part(blocks, weight, side):
    total = jnp.zeros((weight.shape[0], MASKED), F32)
    for k, block in enumerate(blocks):
        total += lax.dot_general(
            weight[:, columns(part_at(side, -k), block.shape[1])], block[...],
            NT, preferred_element_type=F32,
        )
    return total


def student_ours_body(a, b, c, d, weight, total):
    total[...] = student_part((a, b, c, d), weight, 0)


def student_theirs_body(a, b, c, d, weight, first, lse_teacher, out, stats):
    total = first[...] + student_part((a, b, c, d), weight, 1)
    out[...] = total
    both = jnp.concatenate([logsumexp(total), lse_teacher[0:1, :]], axis=0)
    stats[...] = jnp.broadcast_to(both[None], stats.shape)


def combine_body(stats, out):
    x = stats[...]
    top = jnp.max(x, axis=0)
    out[...] = top + jnp.log(jnp.sum(jnp.exp(x - top[None]), axis=0))


def products(grad, weight, side, parts):
    for k, part in enumerate(parts):
        part[...] = lax.dot_general(
            grad, weight[:, columns(part_at(side, k), part.shape[1])], TN,
            preferred_element_type=F32,
        ).astype(part.dtype)


def logits_body(student, teacher, mine, other, count, weight, grad_logits, *parts):
    top = jnp.maximum(mine[...], other[...])
    lse = top + jnp.log(jnp.exp(mine[...] - top) + jnp.exp(other[...] - top))
    scale = LOSS_SCALE / count[0:1, :]
    prob_student = jnp.exp(student[...] - lse[0:1, :])
    prob_teacher = jnp.exp(teacher[...].astype(F32) - lse[1:2, :])
    grad = (scale * (prob_student - prob_teacher)).astype(BF16)
    grad_logits[...] = grad
    products(grad, weight, 1, parts)


def products_body(grad_logits, weight, *parts):
    products(grad_logits[...], weight, 0, parts)


def head_body(*refs):
    blocks, (grad_logits, out_hbm, out, sems) = refs[: NCORE * RING], refs[NCORE * RING :]
    copies = []
    for i, block in enumerate(blocks):
        span = columns(part_at(i // RING, -(i % RING)), block.shape[1])
        out[i] = jnp.dot(
            grad_logits[...], block[...], preferred_element_type=F32
        ).astype(BF16)
        copy = pltpu.make_async_copy(out.at[i], out_hbm.at[:, span], sems.at[i])
        copy.start()
        copies.append(copy)
    for copy in copies:
        copy.wait()


def spread_body(a, b, c, d, back, out):
    total = a[...].astype(F32) + b[...].astype(F32) + c[...].astype(F32) + d[...].astype(F32)
    total = total.astype(BF16)
    half = out.shape[1]
    out[...] = (
        jnp.dot(back[0], total[:, :half], preferred_element_type=F32)
        + jnp.dot(back[1], total[:, half:], preferred_element_type=F32)
    ).astype(BF16)


def collect_body(parts, mine, other):
    chips, rows, half = parts.shape
    total = jnp.sum(parts[...].astype(F32).reshape(NX, NZ, NY, rows, half), axis=1)
    first = lax.axis_index("core") == 0
    total = jnp.where(first, jnp.sum(total, axis=0), jnp.sum(total, axis=1))
    low, high = total[:, : rows // 2], total[:, rows // 2 :]
    mine[...] = jnp.where(first, low, high)
    other[...] = jnp.where(first, high, low)


def finish_body(mine, other, out, whole):
    half = mine.shape[2]
    first = lax.axis_index("core") == 0
    by_core = (
        jnp.where(first, mine[...], other[...]), jnp.where(first, other[...], mine[...]),
    )
    for i in range(out.shape[0]):
        for core in range(NCORE):
            for at in range(RING):
                for h in range(2):
                    start = ((core * RING + at) * 2 + h) * half
                    row = 2 * i + h
                    whole[i : i + 1, start : start + half] = by_core[core][at, row : row + 1]
    out[...] = whole[...].astype(BF16)


def swap_core(x):
    return lax.ppermute(x, "core", [(0, 1), (1, 0)])


def shift(v, k):
    moves = []
    for x in range(NX):
        for z in range(NZ):
            for y in range(NY):
                for core, (to_x, to_y) in enumerate(((x, (y + k) % NY), ((x + k) % NX, y))):
                    moves.append(
                        (((x * NZ + z) * NCORE + core) * NY + y,
                         ((to_x * NZ + z) * NCORE + core) * NY + to_y)
                    )
    return lax.ppermute(v, ALL, moves)


def per_device(hidden, head_weight, teacher, positions, counts):
    tokens, depth = hidden.shape
    capacity = positions.shape[1]
    shards = NX * NZ * NCORE
    slots = shards * capacity
    vocab = head_weight.shape[1]
    part = depth // (RING * NCORE)
    own = capacity // NY
    chips = NX * NZ * NY
    weight = head_weight.T
    half_flops = vocab * depth * MASKED
    logits_shape = shape((vocab, MASKED), F32)

    send = call(
        pick_body, shape((shards, capacity, part), BF16),
        positions, counts.reshape(1, 1), hidden, specs=[HBM] * 3,
        scratch=[
            pltpu.SMEM(positions.shape, jnp.int32), pltpu.SMEM((1, 1), jnp.int32),
            pltpu.VMEM((tokens, part + depth // 2), BF16), DMA((4,)),
        ],
        limit=PICK_LIMIT,
    )
    rows = lax.all_to_all(send, SEQ, 0, 0, tiled=True).reshape(slots, part)
    picked, chosen, count = call(
        compact_body,
        (
            shape((MASKED, part), BF16), shape((MASKED, slots), BF16), shape((8, MASKED), F32),
        ),
        rows, flops=2 * MASKED * slots * part,
    )
    blocks = [picked] + [shift(picked, k) for k in range(1, RING)]
    staged = call(
        teacher_body,
        (
            shape((vocab, MASKED), BF16), shape((8, MASKED), F32),
            shape((2, 2 * slots, MASKED), BF16),
        ),
        teacher.T, chosen, specs=[HBM, VMEM],
        scratch=[pltpu.VMEM((vocab, slots), BF16), DMA(())],
        flops=2 * vocab * slots * MASKED + 4 * slots * slots * MASKED,
    )
    blocks[1], staged = lax.optimization_barrier((blocks[1], staged))
    teacher_rows, lse_teacher, back = staged
    others = [swap_core(block) for block in blocks]
    total = call(student_ours_body, logits_shape, *blocks, weight, flops=half_flops)
    others[-1], total = lax.optimization_barrier((others[-1], total))
    student, stats = call(
        student_theirs_body, (logits_shape, shape((chips, 2, MASKED), F32)),
        *others, weight, total, lse_teacher, flops=half_flops,
    )
    stats = lax.all_to_all(stats, CHIPS, 0, 0, tiled=True)
    lse = call(combine_body, shape((2, MASKED), F32), stats)
    grad_logits, *theirs = call(
        logits_body,
        (shape((vocab, MASKED), BF16),) + (shape((MASKED, part), BF16),) * RING,
        student, teacher_rows, lse, swap_core(lse), count, weight, flops=half_flops,
    )
    ours = call(
        products_body, (shape((MASKED, part), F32),) * RING, grad_logits, weight,
        flops=half_flops,
    )
    sums = [(a + swap_core(b).astype(F32)).astype(BF16) for a, b in zip(ours, theirs)]
    sums = sums[:1] + [shift(sums[k], k) for k in range(1, RING)]
    grad_head = call(
        head_body, shape((vocab, depth), BF16), *blocks, *others, grad_logits, outs=HBM,
        scratch=[pltpu.VMEM((NCORE * RING, vocab, part), BF16), DMA((NCORE * RING,))],
        flops=2 * half_flops,
    )
    sums[1], grad_head = lax.optimization_barrier((sums[1], grad_head))
    partial = call(
        spread_body, shape((2 * slots, part // 2), BF16), *sums, back,
        flops=4 * MASKED * slots * part,
    )
    partial = lax.all_to_all(partial.reshape(chips, 8, part // 2), CHIPS, 0, 0, tiled=True)
    mine, other = call(collect_body, (shape((RING, 4, part // 2), F32),) * 2, partial)
    grad_hidden = call(
        finish_body, shape((own, depth), BF16), mine, swap_core(other),
        scratch=[pltpu.VMEM((own, depth), F32)],
    )
    return grad_hidden, grad_head.T


def solution(mesh):
    fine = Mesh(mesh.devices.reshape(NX, NZ, NCORE, NY), ALL)
    return jax.shard_map(
        per_device,
        mesh=fine,
        in_specs=(P(SEQ, None), P(None, ALL), P(None, ALL), P(SEQ, None), P(SEQ)),
        out_specs=(P(ALL, None), P(None, ALL)),
        check_vma=False,
    )
```

```python
import functools

import jax
import jax.numpy as jnp
from jax import lax
from jax.experimental import pallas as pl
from jax.experimental.pallas import tpu as pltpu
from jax.sharding import Mesh, PartitionSpec as P

LOSS_SCALE = 1024.0
MASKED = 256
MARK = 64.0

SEQ = ("x", "z", "core")
ALL = ("x", "z", "core", "y")
CHIPS = ("x", "z", "y")
NX, NZ, NCORE, NY = 4, 8, 2, 4
RING = 4
FIRST = ((0, 0), (0, 1), (0, 2), (0, 3), (1, 0), (1, 2))
LAST = ((1, 3), (1, 1))
assert NX == NY == RING
F32, BF16 = jnp.float32, jnp.bfloat16
NT = (((1,), (1,)), ((), ()))
TN = (((0,), (0,)), ((), ()))
VMEM = pl.BlockSpec(memory_space=pltpu.VMEM)
HBM = pl.BlockSpec(memory_space=pltpu.HBM)
DMA = pltpu.SemaphoreType.DMA
LIMIT, PICK_LIMIT = 32 << 20, 62717952


def call(body, out, *args, specs=None, outs=VMEM, flops=0, scratch=(), limit=LIMIT):
    leaves = jax.tree.leaves((args, out))
    nbytes = sum(x.size * x.dtype.itemsize for x in leaves)
    return pl.pallas_call(
        body,
        out_shape=out,
        in_specs=specs or [VMEM] * len(args),
        out_specs=jax.tree.map(lambda _: outs, out),
        scratch_shapes=list(scratch),
        cost_estimate=pl.CostEstimate(flops=flops, bytes_accessed=nbytes, transcendentals=0),
        compiler_params=pltpu.CompilerParams(vmem_limit_bytes=limit),
    )(*args)


def shape(dims, dtype):
    return jax.ShapeDtypeStruct(dims, dtype)


def columns(block, width):
    return pl.ds(pl.multiple_of(block * width, width), width)


def place(core):
    return jnp.where(core == 0, lax.axis_index("y"), lax.axis_index("x"))


def part_at(side, steps):
    core = lax.axis_index("core")
    core = core if side == 0 else 1 - core
    return core * RING + lax.rem(place(core) + steps + RING, RING)


def pick_body(positions_hbm, counts_hbm, hidden, out, positions, counts, mine, sems):
    shards, capacity, width = out.shape
    tokens, depth = hidden.shape
    copies = [
        pltpu.make_async_copy(positions_hbm, positions, sems.at[0]),
        pltpu.make_async_copy(counts_hbm, counts, sems.at[1]),
        pltpu.make_async_copy(
            hidden.at[:, columns(lax.axis_index("y"), width)], mine.at[:, :width], sems.at[2]
        ),
        pltpu.make_async_copy(hidden.at[:, depth // 2 :], mine.at[:, width:], sems.at[3]),
    ]
    for copy in copies:
        copy.start()
    for copy in copies:
        copy.wait()
    row = lax.broadcasted_iota(jnp.int32, (2 * capacity, tokens), 0)
    column = lax.broadcasted_iota(jnp.int32, (2 * capacity, tokens), 1)
    hot = jnp.zeros((2 * capacity, tokens), F32)
    for k in range(capacity):
        hot = jnp.where((row == k) & (column == positions[0, k]), 1.0, hot)
    rows = jnp.dot(hot.astype(BF16), mine[...], preferred_element_type=F32)[:capacity]
    rank = lax.broadcasted_iota(jnp.int32, rows.shape, 0)
    rows = jnp.where(rank < counts[0, 0], rows, MARK).astype(BF16)
    for s in range(shards):
        start = s % NCORE * (1 + s // (NZ * NCORE)) * width
        out[s] = rows[:, start : start + width]


def compact_body(rows, picked, chosen, count):
    slots = rows.shape[0]
    capacity = 8
    valid = (rows[...].astype(F32)[:, 0:1] < MARK / 2).astype(F32)
    a = lax.broadcasted_iota(jnp.int32, (slots, slots), 0)
    b = lax.broadcasted_iota(jnp.int32, (slots, slots), 1)
    spread = jnp.broadcast_to(valid, (slots, slots))
    rank = jnp.sum(jnp.where(a < b, spread, 0.0), axis=0, keepdims=True)
    mine = jnp.sum(jnp.where(a == b, spread, 0.0), axis=0, keepdims=True)
    total = jnp.sum(jnp.where(a // capacity == b // capacity, spread, 0.0), axis=0, keepdims=True)
    place = jnp.where(mine > 0.5, rank, -1.0).astype(jnp.int32)
    target = lax.broadcasted_iota(jnp.int32, (MASKED, slots), 0)
    hot = (target == place).astype(F32).astype(BF16)
    chosen[...] = hot
    picked[...] = jnp.dot(hot, rows[...], preferred_element_type=F32).astype(BF16)
    totals = jnp.broadcast_to(total, (8, slots)).astype(BF16)
    count[...] = lax.dot_general(totals, hot, NT, preferred_element_type=F32)


def logsumexp(x):
    top = jnp.max(x, axis=0, keepdims=True)
    return top + jnp.log(jnp.sum(jnp.exp(x - top), axis=0, keepdims=True))


def teacher_body(teacher_hbm, chosen, out, lse, back, teacher, sem):
    move = pltpu.make_async_copy(teacher_hbm, teacher, sem)
    move.start()
    halves, sent, masked = back.shape
    slots = chosen.shape[1]
    row = lax.broadcasted_iota(jnp.int32, (sent, slots), 0)
    chip, q = row // 8, row % 8
    slot = chip // NY * 16 + q // 4 * 8 + chip % NY * 2 + q // 2 % 2
    column = lax.broadcasted_iota(jnp.int32, (sent, slots), 1)
    pick = (column == slot).astype(F32).astype(BF16)
    placed = lax.dot_general(pick, chosen[...], NT, preferred_element_type=F32)
    odd = lax.broadcasted_iota(jnp.int32, (sent, masked), 0) % 2
    for h in range(halves):
        back[h] = jnp.where(odd == h, placed, 0.0).astype(BF16)
    move.wait()
    rows = lax.dot_general(teacher[...], chosen[...], NT, preferred_element_type=F32)
    out[...] = rows.astype(BF16)
    lse[...] = jnp.broadcast_to(logsumexp(rows), lse.shape)


def student_part(blocks, which, weight, total):
    for block, (side, k) in zip(blocks, which):
        total += lax.dot_general(
            weight[:, columns(part_at(side, -k), block.shape[1])], block[...],
            NT, preferred_element_type=F32,
        )
    return total


def student_first_body(*refs):
    blocks, (weight, total) = refs[: len(FIRST)], refs[len(FIRST) :]
    total[...] = student_part(blocks, FIRST, weight, jnp.zeros(total.shape, F32))


def student_last_body(*refs):
    blocks, (weight, first, lse_teacher, out, stats) = refs[: len(LAST)], refs[len(LAST) :]
    total = student_part(blocks, LAST, weight, first[...])
    out[...] = total
    both = jnp.concatenate([logsumexp(total), lse_teacher[0:1, :]], axis=0)
    stats[...] = jnp.broadcast_to(both[None], stats.shape)


def combine_body(stats, out):
    x = stats[...]
    top = jnp.max(x, axis=0)
    out[...] = top + jnp.log(jnp.sum(jnp.exp(x - top[None]), axis=0))


def products(grad, weight, which, parts):
    for part, (side, k) in zip(parts, which):
        part[...] = lax.dot_general(
            grad, weight[:, columns(part_at(side, k), part.shape[1])], TN,
            preferred_element_type=F32,
        ).astype(part.dtype)


def logits_body(student, teacher, mine, other, count, weight, grad_logits, *parts, which):
    top = jnp.maximum(mine[...], other[...])
    lse = top + jnp.log(jnp.exp(mine[...] - top) + jnp.exp(other[...] - top))
    scale = LOSS_SCALE / count[0:1, :]
    prob_student = jnp.exp(student[...] - lse[0:1, :])
    prob_teacher = jnp.exp(teacher[...].astype(F32) - lse[1:2, :])
    grad = (scale * (prob_student - prob_teacher)).astype(BF16)
    grad_logits[...] = grad
    products(grad, weight, which, parts)


def products_body(grad_logits, weight, *parts, which):
    products(grad_logits[...], weight, which, parts)


def head_body(*refs):
    blocks, (grad_logits, out_hbm, out, sems) = refs[: NCORE * RING], refs[NCORE * RING :]
    copies = []
    for i, block in enumerate(blocks):
        span = columns(part_at(i // RING, -(i % RING)), block.shape[1])
        out[i] = jnp.dot(
            grad_logits[...], block[...], preferred_element_type=F32
        ).astype(BF16)
        copy = pltpu.make_async_copy(out.at[i], out_hbm.at[:, span], sems.at[i])
        copy.start()
        copies.append(copy)
    for copy in copies:
        copy.wait()


def spread_body(a, b, c, d, back, out):
    total = a[...].astype(F32) + b[...].astype(F32) + c[...].astype(F32) + d[...].astype(F32)
    total = total.astype(BF16)
    half = out.shape[1]
    out[...] = (
        jnp.dot(back[0], total[:, :half], preferred_element_type=F32)
        + jnp.dot(back[1], total[:, half:], preferred_element_type=F32)
    ).astype(BF16)


def collect_body(parts, mine, other):
    chips, rows, half = parts.shape
    total = jnp.sum(parts[...].astype(F32).reshape(NX, NZ, NY, rows, half), axis=1)
    first = lax.axis_index("core") == 0
    total = jnp.where(first, jnp.sum(total, axis=0), jnp.sum(total, axis=1))
    low, high = total[:, : rows // 2], total[:, rows // 2 :]
    mine[...] = jnp.where(first, low, high)
    other[...] = jnp.where(first, high, low)


def finish_body(mine, other, out, whole):
    half = mine.shape[2]
    first = lax.axis_index("core") == 0
    by_core = (
        jnp.where(first, mine[...], other[...]), jnp.where(first, other[...], mine[...]),
    )
    for i in range(out.shape[0]):
        for core in range(NCORE):
            for at in range(RING):
                for h in range(2):
                    start = ((core * RING + at) * 2 + h) * half
                    row = 2 * i + h
                    whole[i : i + 1, start : start + half] = by_core[core][at, row : row + 1]
    out[...] = whole[...].astype(BF16)


def swap_core(x):
    return lax.ppermute(x, "core", [(0, 1), (1, 0)])


def shift(v, k):
    moves = []
    for x in range(NX):
        for z in range(NZ):
            for y in range(NY):
                for core, (to_x, to_y) in enumerate(((x, (y + k) % NY), ((x + k) % NX, y))):
                    moves.append(
                        (((x * NZ + z) * NCORE + core) * NY + y,
                         ((to_x * NZ + z) * NCORE + core) * NY + to_y)
                    )
    return lax.ppermute(v, ALL, moves)


def per_device(hidden, head_weight, teacher, positions, counts):
    tokens, depth = hidden.shape
    capacity = positions.shape[1]
    shards = NX * NZ * NCORE
    slots = shards * capacity
    vocab = head_weight.shape[1]
    part = depth // (RING * NCORE)
    own = capacity // NY
    chips = NX * NZ * NY
    weight = head_weight.T
    half_flops = vocab * depth * MASKED
    logits_shape = shape((vocab, MASKED), F32)

    send = call(
        pick_body, shape((shards, capacity, part), BF16),
        positions, counts.reshape(1, 1), hidden, specs=[HBM] * 3,
        scratch=[
            pltpu.SMEM(positions.shape, jnp.int32), pltpu.SMEM((1, 1), jnp.int32),
            pltpu.VMEM((tokens, part + depth // 2), BF16), DMA((4,)),
        ],
        limit=PICK_LIMIT,
    )
    rows = lax.all_to_all(send, SEQ, 0, 0, tiled=True).reshape(slots, part)
    picked, chosen, count = call(
        compact_body,
        (
            shape((MASKED, part), BF16), shape((MASKED, slots), BF16), shape((8, MASKED), F32),
        ),
        rows, flops=2 * MASKED * slots * part,
    )
    blocks = {(0, 0): picked} | {(0, k): shift(picked, k) for k in range(1, RING)}
    staged = call(
        teacher_body,
        (
            shape((vocab, MASKED), BF16), shape((8, MASKED), F32),
            shape((2, 2 * slots, MASKED), BF16),
        ),
        teacher.T, chosen, specs=[HBM, VMEM],
        scratch=[pltpu.VMEM((vocab, slots), BF16), DMA(())],
        flops=2 * vocab * slots * MASKED + 4 * slots * slots * MASKED,
    )
    blocks[0, 2], staged = lax.optimization_barrier((blocks[0, 2], staged))
    teacher_rows, lse_teacher, back = staged
    blocks |= {(1, k): swap_core(blocks[0, k]) for k in range(RING)}
    total = call(
        student_first_body, logits_shape, *[blocks[at] for at in FIRST], weight, flops=half_flops
    )
    blocks[1, 1], total = lax.optimization_barrier((blocks[1, 1], total))
    student, stats = call(
        student_last_body, (logits_shape, shape((chips, 2, MASKED), F32)),
        *[blocks[at] for at in LAST], weight, total, lse_teacher, flops=half_flops,
    )
    stats = lax.all_to_all(stats, CHIPS, 0, 0, tiled=True)
    lse = call(combine_body, shape((2, MASKED), F32), stats)
    parts = {}
    which = ((1, 2),)
    grad_logits, parts[1, 2] = call(
        functools.partial(logits_body, which=which),
        (shape((vocab, MASKED), BF16), shape((MASKED, part), BF16)),
        student, teacher_rows, lse, swap_core(lse), count, weight, flops=half_flops // 4,
    )
    for which in (((0, 2), (1, 1), (1, 3)), ((0, 1), (0, 3)), ((1, 0), (0, 0))):
        out = tuple(shape((MASKED, part), BF16 if side else F32) for side, k in which)
        made = call(
            functools.partial(products_body, which=which), out, grad_logits, weight,
            flops=half_flops * len(which) // 4,
        )
        parts |= dict(zip(which, made))
    both = {
        k: (parts[0, k] + swap_core(parts[1, k]).astype(F32)).astype(BF16) for k in range(RING)
    }
    sums = [both[0]] + [shift(both[k], k) for k in range(1, RING)]
    grad_head = call(
        head_body, shape((vocab, depth), BF16),
        *[blocks[side, k] for side in range(NCORE) for k in range(RING)], grad_logits, outs=HBM,
        scratch=[pltpu.VMEM((NCORE * RING, vocab, part), BF16), DMA((NCORE * RING,))],
        flops=2 * half_flops,
    )
    sums[1], grad_head = lax.optimization_barrier((sums[1], grad_head))
    partial = call(
        spread_body, shape((2 * slots, part // 2), BF16), *sums, back,
        flops=4 * MASKED * slots * part,
    )
    partial = lax.all_to_all(partial.reshape(chips, 8, part // 2), CHIPS, 0, 0, tiled=True)
    mine, other = call(collect_body, (shape((RING, 4, part // 2), F32),) * 2, partial)
    grad_hidden = call(
        finish_body, shape((own, depth), BF16), mine, swap_core(other),
        scratch=[pltpu.VMEM((own, depth), F32)],
    )
    return grad_hidden, grad_head.T


def solution(mesh):
    fine = Mesh(mesh.devices.reshape(NX, NZ, NCORE, NY), ALL)
    return jax.shard_map(
        per_device,
        mesh=fine,
        in_specs=(P(SEQ, None), P(None, ALL), P(None, ALL), P(SEQ, None), P(SEQ)),
        out_specs=(P(ALL, None), P(None, ALL)),
        check_vma=False,
    )
```

```python
import functools

import jax
import jax.numpy as jnp
from jax import lax
from jax.experimental import pallas as pl
from jax.experimental.pallas import tpu as pltpu
from jax.sharding import Mesh, PartitionSpec as P

LOSS_SCALE = 1024.0
MASKED = 256
MARK = 64.0

SEQ = ("x", "z", "core")
ALL = ("x", "z", "core", "y")
CHIPS = ("x", "z", "y")
NX, NZ, NCORE, NY = 4, 8, 2, 4
RING = 4
FIRST = ((0, 0), (0, 1), (0, 2), (0, 3), (1, 0), (1, 2))
LAST = ((1, 3), (1, 1))
assert NX == NY == RING
F32, BF16 = jnp.float32, jnp.bfloat16
NT = (((1,), (1,)), ((), ()))
TN = (((0,), (0,)), ((), ()))
VMEM = pl.BlockSpec(memory_space=pltpu.VMEM)
HBM = pl.BlockSpec(memory_space=pltpu.HBM)
DMA = pltpu.SemaphoreType.DMA
LIMIT, PICK_LIMIT = 32 << 20, 55996416


def call(body, out, *args, specs=None, outs=VMEM, flops=0, scratch=(), limit=LIMIT):
    leaves = jax.tree.leaves((args, out))
    nbytes = sum(x.size * x.dtype.itemsize for x in leaves)
    return pl.pallas_call(
        body,
        out_shape=out,
        in_specs=specs or [VMEM] * len(args),
        out_specs=jax.tree.map(lambda _: outs, out),
        scratch_shapes=list(scratch),
        cost_estimate=pl.CostEstimate(flops=flops, bytes_accessed=nbytes, transcendentals=0),
        compiler_params=pltpu.CompilerParams(vmem_limit_bytes=limit),
    )(*args)


def shape(dims, dtype):
    return jax.ShapeDtypeStruct(dims, dtype)


def columns(block, width):
    return pl.ds(pl.multiple_of(block * width, width), width)


def place(core):
    return jnp.where(core == 0, lax.axis_index("y"), lax.axis_index("x"))


def part_at(side, steps):
    core = lax.axis_index("core")
    core = core if side == 0 else 1 - core
    return core * RING + lax.rem(place(core) + steps + RING, RING)


def pick_body(numbers, hidden, out, mine, sems):
    shards, capacity, width = out.shape
    tokens, depth = hidden.shape
    copies = [
        pltpu.make_async_copy(
            hidden.at[:, columns(lax.axis_index("y"), width)],
            mine.at[:tokens, :width], sems.at[0],
        ),
        pltpu.make_async_copy(
            hidden.at[:, depth // 2 :], mine.at[:tokens, width:], sems.at[1]
        ),
    ]
    for copy in copies:
        copy.start()
    more = (mine.shape[0] - tokens, mine.shape[1])
    mine[tokens:, :] = (lax.broadcasted_iota(jnp.int32, more, 0) == 0).astype(F32).astype(BF16)
    position, count = numbers[...] % tokens, numbers[...] // tokens
    masked = lax.broadcasted_iota(jnp.int32, numbers.shape, 1) < count
    row = lax.broadcasted_iota(jnp.int32, (mine.shape[0], capacity), 0)
    source = jnp.where(masked, position, tokens)
    hot = jnp.where(row == source, jnp.where(masked, 1.0, MARK), 0.0).astype(BF16)
    for copy in copies:
        copy.wait()
    rows = lax.dot_general(hot, mine[...], TN, preferred_element_type=F32)
    rows = rows.astype(BF16)
    for s in range(shards):
        start = s % NCORE * (1 + s // (NZ * NCORE)) * width
        out[s] = rows[:, start : start + width]


def compact_body(rows, picked, chosen, count):
    slots = rows.shape[0]
    capacity = 8
    valid = (rows[...].astype(F32)[:, 0:1] < MARK / 2).astype(F32)
    a = lax.broadcasted_iota(jnp.int32, (slots, slots), 0)
    b = lax.broadcasted_iota(jnp.int32, (slots, slots), 1)
    spread = jnp.broadcast_to(valid, (slots, slots))
    rank = jnp.sum(jnp.where(a < b, spread, 0.0), axis=0, keepdims=True)
    mine = jnp.sum(jnp.where(a == b, spread, 0.0), axis=0, keepdims=True)
    total = jnp.sum(jnp.where(a // capacity == b // capacity, spread, 0.0), axis=0, keepdims=True)
    place = jnp.where(mine > 0.5, rank, -1.0).astype(jnp.int32)
    target = lax.broadcasted_iota(jnp.int32, (MASKED, slots), 0)
    hot = (target == place).astype(F32).astype(BF16)
    chosen[...] = hot
    picked[...] = jnp.dot(hot, rows[...], preferred_element_type=F32).astype(BF16)
    totals = jnp.broadcast_to(total, (8, slots)).astype(BF16)
    count[...] = lax.dot_general(totals, hot, NT, preferred_element_type=F32)


def logsumexp(x):
    top = jnp.max(x, axis=0, keepdims=True)
    return top + jnp.log(jnp.sum(jnp.exp(x - top), axis=0, keepdims=True))


def teacher_body(teacher_hbm, chosen, out, lse, back, teacher, sem):
    move = pltpu.make_async_copy(teacher_hbm, teacher, sem)
    move.start()
    halves, sent, masked = back.shape
    slots = chosen.shape[1]
    row = lax.broadcasted_iota(jnp.int32, (sent, slots), 0)
    chip, q = row // 8, row % 8
    slot = chip // NY * 16 + q // 4 * 8 + chip % NY * 2 + q // 2 % 2
    column = lax.broadcasted_iota(jnp.int32, (sent, slots), 1)
    pick = (column == slot).astype(F32).astype(BF16)
    placed = lax.dot_general(pick, chosen[...], NT, preferred_element_type=F32)
    odd = lax.broadcasted_iota(jnp.int32, (sent, masked), 0) % 2
    for h in range(halves):
        back[h] = jnp.where(odd == h, placed, 0.0).astype(BF16)
    move.wait()
    rows = lax.dot_general(teacher[...], chosen[...], NT, preferred_element_type=F32)
    out[...] = rows.astype(BF16)
    lse[...] = jnp.broadcast_to(logsumexp(rows), lse.shape)


def student_part(blocks, which, weight, total):
    for block, (side, k) in zip(blocks, which):
        total += lax.dot_general(
            weight[:, columns(part_at(side, -k), block.shape[1])], block[...],
            NT, preferred_element_type=F32,
        )
    return total


def student_first_body(*refs):
    blocks, (weight, total) = refs[: len(FIRST)], refs[len(FIRST) :]
    total[...] = student_part(blocks, FIRST, weight, jnp.zeros(total.shape, F32))


def student_last_body(*refs):
    blocks, (weight, first, lse_teacher, out, stats) = refs[: len(LAST)], refs[len(LAST) :]
    total = student_part(blocks, LAST, weight, first[...])
    out[...] = total
    both = jnp.concatenate([logsumexp(total), lse_teacher[0:1, :]], axis=0)
    stats[...] = jnp.broadcast_to(both[None], stats.shape)


def combine_body(stats, out):
    x = stats[...]
    top = jnp.max(x, axis=0)
    out[...] = top + jnp.log(jnp.sum(jnp.exp(x - top[None]), axis=0))


def products(grad, weight, which, parts):
    for part, (side, k) in zip(parts, which):
        part[...] = lax.dot_general(
            grad, weight[:, columns(part_at(side, k), part.shape[1])], TN,
            preferred_element_type=F32,
        ).astype(part.dtype)


def logits_body(student, teacher, mine, other, count, weight, grad_logits, *parts, which):
    top = jnp.maximum(mine[...], other[...])
    lse = top + jnp.log(jnp.exp(mine[...] - top) + jnp.exp(other[...] - top))
    scale = LOSS_SCALE / count[0:1, :]
    prob_student = jnp.exp(student[...] - lse[0:1, :])
    prob_teacher = jnp.exp(teacher[...].astype(F32) - lse[1:2, :])
    grad = (scale * (prob_student - prob_teacher)).astype(BF16)
    grad_logits[...] = grad
    products(grad, weight, which, parts)


def products_body(grad_logits, weight, *parts, which):
    products(grad_logits[...], weight, which, parts)


def head_body(*refs):
    blocks, (grad_logits, out_hbm, out, sems) = refs[: NCORE * RING], refs[NCORE * RING :]
    copies = []
    for i, block in enumerate(blocks):
        span = columns(part_at(i // RING, -(i % RING)), block.shape[1])
        out[i] = jnp.dot(
            grad_logits[...], block[...], preferred_element_type=F32
        ).astype(BF16)
        copy = pltpu.make_async_copy(out.at[i], out_hbm.at[:, span], sems.at[i])
        copy.start()
        copies.append(copy)
    for copy in copies:
        copy.wait()


def spread_body(a, b, c, d, back, out):
    total = a[...].astype(F32) + b[...].astype(F32) + c[...].astype(F32) + d[...].astype(F32)
    total = total.astype(BF16)
    half = out.shape[1]
    out[...] = (
        jnp.dot(back[0], total[:, :half], preferred_element_type=F32)
        + jnp.dot(back[1], total[:, half:], preferred_element_type=F32)
    ).astype(BF16)


def collect_body(parts, mine, other):
    chips, rows, half = parts.shape
    total = jnp.sum(parts[...].astype(F32).reshape(NX, NZ, NY, rows, half), axis=1)
    first = lax.axis_index("core") == 0
    total = jnp.where(first, jnp.sum(total, axis=0), jnp.sum(total, axis=1))
    low, high = total[:, : rows // 2], total[:, rows // 2 :]
    mine[...] = jnp.where(first, low, high)
    other[...] = jnp.where(first, high, low)


def finish_body(mine, other, out, whole):
    half = mine.shape[2]
    first = lax.axis_index("core") == 0
    by_core = (
        jnp.where(first, mine[...], other[...]), jnp.where(first, other[...], mine[...]),
    )
    for i in range(out.shape[0]):
        for core in range(NCORE):
            for at in range(RING):
                for h in range(2):
                    start = ((core * RING + at) * 2 + h) * half
                    row = 2 * i + h
                    whole[i : i + 1, start : start + half] = by_core[core][at, row : row + 1]
    out[...] = whole[...].astype(BF16)


def swap_core(x):
    return lax.ppermute(x, "core", [(0, 1), (1, 0)])


def shift(v, k):
    moves = []
    for x in range(NX):
        for z in range(NZ):
            for y in range(NY):
                for core, (to_x, to_y) in enumerate(((x, (y + k) % NY), ((x + k) % NX, y))):
                    moves.append(
                        (((x * NZ + z) * NCORE + core) * NY + y,
                         ((to_x * NZ + z) * NCORE + core) * NY + to_y)
                    )
    return lax.ppermute(v, ALL, moves)


def per_device(hidden, head_weight, teacher, positions, counts):
    tokens, depth = hidden.shape
    capacity = positions.shape[1]
    shards = NX * NZ * NCORE
    slots = shards * capacity
    vocab = head_weight.shape[1]
    part = depth // (RING * NCORE)
    own = capacity // NY
    chips = NX * NZ * NY
    weight = head_weight.T
    half_flops = vocab * depth * MASKED
    logits_shape = shape((vocab, MASKED), F32)

    numbers = positions + tokens * counts
    send = call(
        pick_body, shape((shards, capacity, part), BF16), numbers, hidden, specs=[VMEM, HBM],
        scratch=[pltpu.VMEM((tokens + 16, part + depth // 2), BF16), DMA((2,))],
        limit=PICK_LIMIT,
    )
    rows = lax.all_to_all(send, SEQ, 0, 0, tiled=True).reshape(slots, part)
    picked, chosen, count = call(
        compact_body,
        (
            shape((MASKED, part), BF16), shape((MASKED, slots), BF16), shape((8, MASKED), F32),
        ),
        rows, flops=2 * MASKED * slots * part,
    )
    blocks = {(0, 0): picked} | {(0, k): shift(picked, k) for k in range(1, RING)}
    staged = call(
        teacher_body,
        (
            shape((vocab, MASKED), BF16), shape((8, MASKED), F32),
            shape((2, 2 * slots, MASKED), BF16),
        ),
        teacher.T, chosen, specs=[HBM, VMEM],
        scratch=[pltpu.VMEM((vocab, slots), BF16), DMA(())],
        flops=2 * vocab * slots * MASKED + 4 * slots * slots * MASKED,
    )
    blocks[0, 2], staged = lax.optimization_barrier((blocks[0, 2], staged))
    teacher_rows, lse_teacher, back = staged
    blocks |= {(1, k): swap_core(blocks[0, k]) for k in range(RING)}
    total = call(
        student_first_body, logits_shape, *[blocks[at] for at in FIRST], weight, flops=half_flops
    )
    blocks[1, 1], total = lax.optimization_barrier((blocks[1, 1], total))
    student, stats = call(
        student_last_body, (logits_shape, shape((chips, 2, MASKED), F32)),
        *[blocks[at] for at in LAST], weight, total, lse_teacher, flops=half_flops,
    )
    stats = lax.all_to_all(stats, CHIPS, 0, 0, tiled=True)
    lse = call(combine_body, shape((2, MASKED), F32), stats)
    parts = {}
    which = ((1, 2),)
    grad_logits, parts[1, 2] = call(
        functools.partial(logits_body, which=which),
        (shape((vocab, MASKED), BF16), shape((MASKED, part), BF16)),
        student, teacher_rows, lse, swap_core(lse), count, weight, flops=half_flops // 4,
    )
    sums = {}

    def make(which, tie):
        grad, tie = lax.optimization_barrier((grad_logits, tie))
        out = tuple(shape((MASKED, part), BF16 if side else F32) for side, k in which)
        made = call(
            functools.partial(products_body, which=which), out, grad, weight,
            flops=half_flops * len(which) // 4,
        )
        parts.update(zip(which, made))
        return tie

    def add(k):
        return (parts[0, k] + swap_core(parts[1, k]).astype(F32)).astype(BF16)

    make(((0, 2), (1, 1)), lse)
    make(((1, 3), (0, 1), (0, 3)), lse)
    both = {k: add(k) for k in (2, 1, 3)}
    both[1] = make(((1, 0), (0, 0)), both[1])
    sums = [add(0)] + [shift(both[k], k) for k in range(1, RING)]
    grad_head = call(
        head_body, shape((vocab, depth), BF16),
        *[blocks[side, k] for side in range(NCORE) for k in range(RING)], grad_logits, outs=HBM,
        scratch=[pltpu.VMEM((NCORE * RING, vocab, part), BF16), DMA((NCORE * RING,))],
        flops=2 * half_flops,
    )
    sums[1], grad_head = lax.optimization_barrier((sums[1], grad_head))
    partial = call(
        spread_body, shape((2 * slots, part // 2), BF16), *sums, back,
        flops=4 * MASKED * slots * part,
    )
    partial = lax.all_to_all(partial.reshape(chips, 8, part // 2), CHIPS, 0, 0, tiled=True)
    mine, other = call(collect_body, (shape((RING, 4, part // 2), F32),) * 2, partial)
    grad_hidden = call(
        finish_body, shape((own, depth), BF16), mine, swap_core(other),
        scratch=[pltpu.VMEM((own, depth), F32)],
    )
    return grad_hidden, grad_head.T


def solution(mesh):
    fine = Mesh(mesh.devices.reshape(NX, NZ, NCORE, NY), ALL)
    return jax.shard_map(
        per_device,
        mesh=fine,
        in_specs=(P(SEQ, None), P(None, ALL), P(None, ALL), P(SEQ, None), P(SEQ)),
        out_specs=(P(ALL, None), P(None, ALL)),
        check_vma=False,
    )
```

```python
import functools

import jax
import jax.numpy as jnp
from jax import lax
from jax.experimental import pallas as pl
from jax.experimental.pallas import tpu as pltpu
from jax.sharding import Mesh, PartitionSpec as P

LOSS_SCALE = 1024.0
MASKED = 256
MARK = 64.0

SEQ = ("x", "z", "core")
ALL = ("x", "z", "core", "y")
CHIPS = ("x", "z", "y")
NX, NZ, NCORE, NY = 4, 8, 2, 4
RING = 4
FIRST = ((0, 0), (0, 1), (0, 2), (0, 3), (1, 0), (1, 2))
LAST = ((1, 3), (1, 1))
assert NX == NY == RING
F32, BF16 = jnp.float32, jnp.bfloat16
NT = (((1,), (1,)), ((), ()))
TN = (((0,), (0,)), ((), ()))
VMEM = pl.BlockSpec(memory_space=pltpu.VMEM)
HBM = pl.BlockSpec(memory_space=pltpu.HBM)
DMA = pltpu.SemaphoreType.DMA
LIMIT, PICK_LIMIT = 32 << 20, 55996416


def call(body, out, *args, specs=None, outs=VMEM, flops=0, scratch=(), limit=LIMIT):
    leaves = jax.tree.leaves((args, out))
    nbytes = sum(x.size * x.dtype.itemsize for x in leaves)
    return pl.pallas_call(
        body,
        out_shape=out,
        in_specs=specs or [VMEM] * len(args),
        out_specs=jax.tree.map(lambda _: outs, out),
        scratch_shapes=list(scratch),
        cost_estimate=pl.CostEstimate(flops=flops, bytes_accessed=nbytes, transcendentals=0),
        compiler_params=pltpu.CompilerParams(vmem_limit_bytes=limit),
    )(*args)


def shape(dims, dtype):
    return jax.ShapeDtypeStruct(dims, dtype)


def columns(block, width):
    return pl.ds(pl.multiple_of(block * width, width), width)


def place(core):
    return jnp.where(core == 0, lax.axis_index("y"), lax.axis_index("x"))


def second_place(core):
    return jnp.where(core == 0, lax.axis_index("x"), lax.axis_index("y"))


def part_at(side, steps):
    core = lax.axis_index("core")
    core = core if side == 0 else 1 - core
    return core * RING + lax.rem(place(core) + steps + RING, RING)


def pick_body(numbers, hidden, out, mine, sems):
    shards, capacity, width = out.shape
    tokens, depth = hidden.shape
    copies = [
        pltpu.make_async_copy(
            hidden.at[:, columns(lax.axis_index("y"), width)],
            mine.at[:tokens, :width], sems.at[0],
        ),
        pltpu.make_async_copy(
            hidden.at[:, depth // 2 :], mine.at[:tokens, width:], sems.at[1]
        ),
    ]
    for copy in copies:
        copy.start()
    more = (mine.shape[0] - tokens, mine.shape[1])
    mine[tokens:, :] = (lax.broadcasted_iota(jnp.int32, more, 0) == 0).astype(F32).astype(BF16)
    position, count = numbers[...] % tokens, numbers[...] // tokens
    masked = lax.broadcasted_iota(jnp.int32, numbers.shape, 1) < count
    row = lax.broadcasted_iota(jnp.int32, (mine.shape[0], capacity), 0)
    source = jnp.where(masked, position, tokens)
    hot = jnp.where(row == source, jnp.where(masked, 1.0, MARK), 0.0).astype(BF16)
    for copy in copies:
        copy.wait()
    rows = lax.dot_general(hot, mine[...], TN, preferred_element_type=F32)
    rows = rows.astype(BF16)
    for s in range(shards):
        start = s % NCORE * (1 + s // (NZ * NCORE)) * width
        out[s] = rows[:, start : start + width]


def compact_body(rows, picked, chosen, count):
    slots = rows.shape[0]
    capacity = 8
    valid = (rows[...].astype(F32)[:, 0:1] < MARK / 2).astype(F32)
    a = lax.broadcasted_iota(jnp.int32, (slots, slots), 0)
    b = lax.broadcasted_iota(jnp.int32, (slots, slots), 1)
    spread = jnp.broadcast_to(valid, (slots, slots))
    rank = jnp.sum(jnp.where(a < b, spread, 0.0), axis=0, keepdims=True)
    mine = jnp.sum(jnp.where(a == b, spread, 0.0), axis=0, keepdims=True)
    total = jnp.sum(jnp.where(a // capacity == b // capacity, spread, 0.0), axis=0, keepdims=True)
    place = jnp.where(mine > 0.5, rank, -1.0).astype(jnp.int32)
    target = lax.broadcasted_iota(jnp.int32, (MASKED, slots), 0)
    hot = (target == place).astype(F32).astype(BF16)
    chosen[...] = hot
    picked[...] = jnp.dot(hot, rows[...], preferred_element_type=F32).astype(BF16)
    totals = jnp.broadcast_to(total, (8, slots)).astype(BF16)
    count[...] = lax.dot_general(totals, hot, NT, preferred_element_type=F32)


def logsumexp(x):
    top = jnp.max(x, axis=0, keepdims=True)
    return top + jnp.log(jnp.sum(jnp.exp(x - top), axis=0, keepdims=True))


def teacher_body(teacher_hbm, chosen, out, lse, back, teacher, sem):
    move = pltpu.make_async_copy(teacher_hbm, teacher, sem)
    move.start()
    halves, sent, masked = back.shape
    slots = chosen.shape[1]
    row = lax.broadcasted_iota(jnp.int32, (sent, slots), 0)
    second, z, first, q = row // 256, row // 32 % NZ, row // 8 % RING, row % 8
    straight = lax.axis_index("core") == 0
    x, y = jnp.where(straight, second, first), jnp.where(straight, first, second)
    slot = (x * NZ + z) * 16 + q // 4 * 8 + y * 2 + q // 2 % 2
    column = lax.broadcasted_iota(jnp.int32, (sent, slots), 1)
    pick = (column == slot).astype(F32).astype(BF16)
    placed = lax.dot_general(pick, chosen[...], NT, preferred_element_type=F32)
    odd = lax.broadcasted_iota(jnp.int32, (sent, masked), 0) % 2
    for h in range(halves):
        back[h] = jnp.where(odd == h, placed, 0.0).astype(BF16)
    move.wait()
    rows = lax.dot_general(teacher[...], chosen[...], NT, preferred_element_type=F32)
    out[...] = rows.astype(BF16)
    lse[...] = jnp.broadcast_to(logsumexp(rows), lse.shape)


def student_part(blocks, which, weight, total):
    for block, (side, k) in zip(blocks, which):
        total += lax.dot_general(
            weight[:, columns(part_at(side, -k), block.shape[1])], block[...],
            NT, preferred_element_type=F32,
        )
    return total


def student_first_body(*refs):
    blocks, (weight, total) = refs[: len(FIRST)], refs[len(FIRST) :]
    total[...] = student_part(blocks, FIRST, weight, jnp.zeros(total.shape, F32))


def student_last_body(*refs):
    blocks, (weight, first, lse_teacher, out, stats) = refs[: len(LAST)], refs[len(LAST) :]
    total = student_part(blocks, LAST, weight, first[...])
    out[...] = total
    both = jnp.concatenate([logsumexp(total), lse_teacher[0:1, :]], axis=0)
    stats[...] = jnp.broadcast_to(both[None], stats.shape)


def combine_body(stats, out):
    x = stats[...]
    top = jnp.max(x, axis=0)
    out[...] = top + jnp.log(jnp.sum(jnp.exp(x - top[None]), axis=0))


def products(grad, weight, which, parts):
    for part, (side, k) in zip(parts, which):
        part[...] = lax.dot_general(
            grad, weight[:, columns(part_at(side, k), part.shape[1])], TN,
            preferred_element_type=F32,
        ).astype(part.dtype)


def logits_body(student, teacher, mine, other, count, weight, grad_logits, *parts, which):
    top = jnp.maximum(mine[...], other[...])
    lse = top + jnp.log(jnp.exp(mine[...] - top) + jnp.exp(other[...] - top))
    scale = LOSS_SCALE / count[0:1, :]
    prob_student = jnp.exp(student[...] - lse[0:1, :])
    prob_teacher = jnp.exp(teacher[...].astype(F32) - lse[1:2, :])
    grad = (scale * (prob_student - prob_teacher)).astype(BF16)
    grad_logits[...] = grad
    products(grad, weight, which, parts)


def products_body(grad_logits, weight, *parts, which):
    products(grad_logits[...], weight, which, parts)


def head_body(*refs):
    blocks, (grad_logits, out_hbm, out, sems) = refs[: NCORE * RING], refs[NCORE * RING :]
    copies = []
    for i, block in enumerate(blocks):
        span = columns(part_at(i // RING, -(i % RING)), block.shape[1])
        out[i] = jnp.dot(
            grad_logits[...], block[...], preferred_element_type=F32
        ).astype(BF16)
        copy = pltpu.make_async_copy(out.at[i], out_hbm.at[:, span], sems.at[i])
        copy.start()
        copies.append(copy)
    for copy in copies:
        copy.wait()


def spread_body(a, b, c, d, back, *outs):
    total = a[...].astype(F32) + b[...].astype(F32) + c[...].astype(F32) + d[...].astype(F32)
    total = total.astype(BF16)
    rows, half = outs[0].shape
    here = second_place(lax.axis_index("core"))
    for k, out in enumerate(outs):
        span = columns(lax.rem(here + k, RING), rows)
        out[...] = (
            jnp.dot(back[0, span, :], total[:, :half], preferred_element_type=F32)
            + jnp.dot(back[1, span, :], total[:, half:], preferred_element_type=F32)
        ).astype(BF16)


def collect_body(parts, mine, other):
    peers, rows, half = parts.shape
    total = jnp.sum(parts[...].astype(F32).reshape(NZ, RING, rows, half), axis=0)
    low, high = total[:, : rows // 2], total[:, rows // 2 :]
    first = lax.axis_index("core") == 0
    mine[...] = jnp.where(first, low, high)
    other[...] = jnp.where(first, high, low)


def finish_body(mine, other, out, whole):
    half = mine.shape[2]
    first = lax.axis_index("core") == 0
    by_core = (
        jnp.where(first, mine[...], other[...]), jnp.where(first, other[...], mine[...]),
    )
    for i in range(out.shape[0]):
        for core in range(NCORE):
            for at in range(RING):
                for h in range(2):
                    start = ((core * RING + at) * 2 + h) * half
                    row = 2 * i + h
                    whole[i : i + 1, start : start + half] = by_core[core][at, row : row + 1]
    out[...] = whole[...].astype(BF16)


def swap_core(x):
    return lax.ppermute(x, "core", [(0, 1), (1, 0)])


def index(x, z, core, y):
    return ((x * NZ + z) * NCORE + core) * NY + y


def shift(v, k, ring=1):
    moves = []
    for x in range(NX):
        for z in range(NZ):
            for y in range(NY):
                for core in range(NCORE):
                    if (core == 0) == (ring == 1):
                        to = index(x, z, core, (y + k) % NY)
                    else:
                        to = index((x + k) % NX, z, core, y)
                    moves.append((index(x, z, core, y), to))
    return lax.ppermute(v, ALL, moves)


def peers():
    groups = []
    for second in range(RING):
        groups.append([index(second, z, 0, y) for z in range(NZ) for y in range(NY)])
        groups.append([index(x, z, 1, second) for z in range(NZ) for x in range(NX)])
    return groups


def per_device(hidden, head_weight, teacher, positions, counts):
    tokens, depth = hidden.shape
    capacity = positions.shape[1]
    shards = NX * NZ * NCORE
    slots = shards * capacity
    vocab = head_weight.shape[1]
    part = depth // (RING * NCORE)
    own = capacity // NY
    chips = NX * NZ * NY
    weight = head_weight.T
    half_flops = vocab * depth * MASKED
    logits_shape = shape((vocab, MASKED), F32)

    numbers = positions + tokens * counts
    send = call(
        pick_body, shape((shards, capacity, part), BF16), numbers, hidden, specs=[VMEM, HBM],
        scratch=[pltpu.VMEM((tokens + 16, part + depth // 2), BF16), DMA((2,))],
        limit=PICK_LIMIT,
    )
    rows = lax.all_to_all(send, SEQ, 0, 0, tiled=True).reshape(slots, part)
    picked, chosen, count = call(
        compact_body,
        (
            shape((MASKED, part), BF16), shape((MASKED, slots), BF16), shape((8, MASKED), F32),
        ),
        rows, flops=2 * MASKED * slots * part,
    )
    blocks = {(0, 0): picked} | {(0, k): shift(picked, k) for k in range(1, RING)}
    staged = call(
        teacher_body,
        (
            shape((vocab, MASKED), BF16), shape((8, MASKED), F32),
            shape((2, 2 * slots, MASKED), BF16),
        ),
        teacher.T, chosen, specs=[HBM, VMEM],
        scratch=[pltpu.VMEM((vocab, slots), BF16), DMA(())],
        flops=2 * vocab * slots * MASKED + 4 * slots * slots * MASKED,
    )
    blocks[0, 2], staged = lax.optimization_barrier((blocks[0, 2], staged))
    teacher_rows, lse_teacher, back = staged
    blocks |= {(1, k): swap_core(blocks[0, k]) for k in range(RING)}
    total = call(
        student_first_body, logits_shape, *[blocks[at] for at in FIRST], weight, flops=half_flops
    )
    blocks[1, 1], total = lax.optimization_barrier((blocks[1, 1], total))
    student, stats = call(
        student_last_body, (logits_shape, shape((chips, 2, MASKED), F32)),
        *[blocks[at] for at in LAST], weight, total, lse_teacher, flops=half_flops,
    )
    stats = lax.all_to_all(stats, CHIPS, 0, 0, tiled=True)
    lse = call(combine_body, shape((2, MASKED), F32), stats)
    parts = {}
    which = ((1, 2),)
    grad_logits, parts[1, 2] = call(
        functools.partial(logits_body, which=which),
        (shape((vocab, MASKED), BF16), shape((MASKED, part), BF16)),
        student, teacher_rows, lse, swap_core(lse), count, weight, flops=half_flops // 4,
    )
    sums = {}

    def make(which, tie):
        grad, tie = lax.optimization_barrier((grad_logits, tie))
        out = tuple(shape((MASKED, part), BF16 if side else F32) for side, k in which)
        made = call(
            functools.partial(products_body, which=which), out, grad, weight,
            flops=half_flops * len(which) // 4,
        )
        parts.update(zip(which, made))
        return tie

    def add(k):
        return (parts[0, k] + swap_core(parts[1, k]).astype(F32)).astype(BF16)

    make(((0, 2), (1, 1)), lse)
    make(((1, 3), (0, 1), (0, 3)), lse)
    both = {k: add(k) for k in (2, 1, 3)}
    both[1] = make(((1, 0), (0, 0)), both[1])
    sums = [add(0)] + [shift(both[k], k) for k in range(1, RING)]
    grad_head = call(
        head_body, shape((vocab, depth), BF16),
        *[blocks[side, k] for side in range(NCORE) for k in range(RING)], grad_logits, outs=HBM,
        scratch=[pltpu.VMEM((NCORE * RING, vocab, part), BF16), DMA((NCORE * RING,))],
        flops=2 * half_flops,
    )
    sums[1], grad_head = lax.optimization_barrier((sums[1], grad_head))
    steps = call(
        spread_body, (shape((2 * slots // RING, part // 2), BF16),) * RING, *sums, back,
        flops=4 * MASKED * slots * part,
    )
    steps = [steps[0]] + [shift(steps[k], k, ring=2) for k in (2, 1, 3)]
    partial = sum(step.astype(F32) for step in steps).astype(BF16)
    partial = lax.all_to_all(
        partial.reshape(NZ * RING, 8, part // 2), ALL, 0, 0, tiled=True,
        axis_index_groups=peers(),
    )
    mine, other = call(collect_body, (shape((RING, 4, part // 2), F32),) * 2, partial)
    grad_hidden = call(
        finish_body, shape((own, depth), BF16), mine, swap_core(other),
        scratch=[pltpu.VMEM((own, depth), F32)],
    )
    return grad_hidden, grad_head.T


def solution(mesh):
    fine = Mesh(mesh.devices.reshape(NX, NZ, NCORE, NY), ALL)
    return jax.shard_map(
        per_device,
        mesh=fine,
        in_specs=(P(SEQ, None), P(None, ALL), P(None, ALL), P(SEQ, None), P(SEQ)),
        out_specs=(P(ALL, None), P(None, ALL)),
        check_vma=False,
    )
```

```python
import functools

import jax
import jax.numpy as jnp
from jax import lax
from jax.experimental import pallas as pl
from jax.experimental.pallas import tpu as pltpu
from jax.sharding import Mesh, PartitionSpec as P

LOSS_SCALE = 1024.0
MASKED = 256
MARK = 64.0

SEQ = ("x", "z", "core")
ALL = ("x", "z", "core", "y")
NX, NZ, NCORE, NY = 4, 8, 2, 4
RING = 4
FIRST = ((0, 0), (0, 1), (0, 2), (0, 3), (1, 0), (1, 2))
LAST = ((1, 3), (1, 1))
assert NX == NY == RING
F32, BF16 = jnp.float32, jnp.bfloat16
NT = (((1,), (1,)), ((), ()))
TN = (((0,), (0,)), ((), ()))
VMEM = pl.BlockSpec(memory_space=pltpu.VMEM)
HBM = pl.BlockSpec(memory_space=pltpu.HBM)
DMA = pltpu.SemaphoreType.DMA
LIMIT, PICK_LIMIT = 32 << 20, 55996416


def call(body, out, *args, specs=None, outs=VMEM, flops=0, scratch=(), limit=LIMIT):
    leaves = jax.tree.leaves((args, out))
    nbytes = sum(x.size * x.dtype.itemsize for x in leaves)
    return pl.pallas_call(
        body,
        out_shape=out,
        in_specs=specs or [VMEM] * len(args),
        out_specs=jax.tree.map(lambda _: outs, out),
        scratch_shapes=list(scratch),
        cost_estimate=pl.CostEstimate(flops=flops, bytes_accessed=nbytes, transcendentals=0),
        compiler_params=pltpu.CompilerParams(vmem_limit_bytes=limit),
    )(*args)


def shape(dims, dtype):
    return jax.ShapeDtypeStruct(dims, dtype)


def columns(block, width):
    return pl.ds(pl.multiple_of(block * width, width), width)


def place(core):
    return jnp.where(core == 0, lax.axis_index("y"), lax.axis_index("x"))


def second_place(core):
    return jnp.where(core == 0, lax.axis_index("x"), lax.axis_index("y"))


def part_at(side, steps):
    core = lax.axis_index("core")
    core = core if side == 0 else 1 - core
    return core * RING + lax.rem(place(core) + steps + RING, RING)


def pick_body(numbers, hidden, out, mine, sems):
    shards, capacity, width = out.shape
    tokens, depth = hidden.shape
    copies = [
        pltpu.make_async_copy(
            hidden.at[:, columns(lax.axis_index("y"), width)],
            mine.at[:tokens, :width], sems.at[0],
        ),
        pltpu.make_async_copy(
            hidden.at[:, depth // 2 :], mine.at[:tokens, width:], sems.at[1]
        ),
    ]
    for copy in copies:
        copy.start()
    more = (mine.shape[0] - tokens, mine.shape[1])
    mine[tokens:, :] = (lax.broadcasted_iota(jnp.int32, more, 0) == 0).astype(F32).astype(BF16)
    position, count = numbers[...] % tokens, numbers[...] // tokens
    masked = lax.broadcasted_iota(jnp.int32, numbers.shape, 1) < count
    row = lax.broadcasted_iota(jnp.int32, (mine.shape[0], capacity), 0)
    source = jnp.where(masked, position, tokens)
    hot = jnp.where(row == source, jnp.where(masked, 1.0, MARK), 0.0).astype(BF16)
    for copy in copies:
        copy.wait()
    rows = lax.dot_general(hot, mine[...], TN, preferred_element_type=F32)
    rows = rows.astype(BF16)
    for s in range(shards):
        start = s % NCORE * (1 + s // (NZ * NCORE)) * width
        out[s] = rows[:, start : start + width]


def compact_body(rows, picked, chosen, count):
    slots = rows.shape[0]
    capacity = 8
    valid = (rows[...].astype(F32)[:, 0:1] < MARK / 2).astype(F32)
    a = lax.broadcasted_iota(jnp.int32, (slots, slots), 0)
    b = lax.broadcasted_iota(jnp.int32, (slots, slots), 1)
    spread = jnp.broadcast_to(valid, (slots, slots))
    rank = jnp.sum(jnp.where(a < b, spread, 0.0), axis=0, keepdims=True)
    mine = jnp.sum(jnp.where(a == b, spread, 0.0), axis=0, keepdims=True)
    total = jnp.sum(jnp.where(a // capacity == b // capacity, spread, 0.0), axis=0, keepdims=True)
    place = jnp.where(mine > 0.5, rank, -1.0).astype(jnp.int32)
    target = lax.broadcasted_iota(jnp.int32, (MASKED, slots), 0)
    hot = (target == place).astype(F32).astype(BF16)
    chosen[...] = hot
    picked[...] = jnp.dot(hot, rows[...], preferred_element_type=F32).astype(BF16)
    totals = jnp.broadcast_to(total, (8, slots)).astype(BF16)
    count[...] = lax.dot_general(totals, hot, NT, preferred_element_type=F32)


def logsumexp(x):
    top = jnp.max(x, axis=0, keepdims=True)
    return top + jnp.log(jnp.sum(jnp.exp(x - top), axis=0, keepdims=True))


def teacher_body(teacher_hbm, chosen, out, lse, back, teacher, sem):
    move = pltpu.make_async_copy(teacher_hbm, teacher, sem)
    move.start()
    halves, sent, masked = back.shape
    slots = chosen.shape[1]
    row = lax.broadcasted_iota(jnp.int32, (sent, slots), 0)
    second, z, first, q = row // 256, row // 32 % NZ, row // 8 % RING, row % 8
    straight = lax.axis_index("core") == 0
    x, y = jnp.where(straight, second, first), jnp.where(straight, first, second)
    slot = (x * NZ + z) * 16 + q // 4 * 8 + y * 2 + q // 2 % 2
    column = lax.broadcasted_iota(jnp.int32, (sent, slots), 1)
    pick = (column == slot).astype(F32).astype(BF16)
    placed = lax.dot_general(pick, chosen[...], NT, preferred_element_type=F32)
    odd = lax.broadcasted_iota(jnp.int32, (sent, masked), 0) % 2
    for h in range(halves):
        back[h] = jnp.where(odd == h, placed, 0.0).astype(BF16)
    move.wait()
    rows = lax.dot_general(teacher[...], chosen[...], NT, preferred_element_type=F32)
    out[...] = rows.astype(BF16)
    lse[...] = jnp.broadcast_to(logsumexp(rows), lse.shape)


def student_part(blocks, which, weight, total):
    for block, (side, k) in zip(blocks, which):
        total += lax.dot_general(
            weight[:, columns(part_at(side, -k), block.shape[1])], block[...],
            NT, preferred_element_type=F32,
        )
    return total


def student_first_body(*refs):
    blocks, (weight, total) = refs[: len(FIRST)], refs[len(FIRST) :]
    total[...] = student_part(blocks, FIRST, weight, jnp.zeros(total.shape, F32))


def student_last_body(*refs):
    blocks, (weight, first, lse_teacher, out, stats) = refs[: len(LAST)], refs[len(LAST) :]
    total = student_part(blocks, LAST, weight, first[...])
    out[...] = total
    both = jnp.concatenate([logsumexp(total), lse_teacher[0:1, :]], axis=0)
    stats[...] = jnp.broadcast_to(both[None], stats.shape)


def combine_body(stats, out):
    x = stats[...]
    top = jnp.max(x, axis=0)
    out[...] = top + jnp.log(jnp.sum(jnp.exp(x - top[None]), axis=0))


def join_body(a, b, c, d, out):
    top = jnp.maximum(jnp.maximum(a[...], b[...]), jnp.maximum(c[...], d[...]))
    out[...] = top + jnp.log(sum(jnp.exp(x[...] - top) for x in (a, b, c, d)))


def products(grad, weight, which, parts):
    for part, (side, k) in zip(parts, which):
        part[...] = lax.dot_general(
            grad, weight[:, columns(part_at(side, k), part.shape[1])], TN,
            preferred_element_type=F32,
        ).astype(part.dtype)


def logits_body(student, teacher, mine, other, count, weight, grad_logits, *parts, which):
    top = jnp.maximum(mine[...], other[...])
    lse = top + jnp.log(jnp.exp(mine[...] - top) + jnp.exp(other[...] - top))
    scale = LOSS_SCALE / count[0:1, :]
    prob_student = jnp.exp(student[...] - lse[0:1, :])
    prob_teacher = jnp.exp(teacher[...].astype(F32) - lse[1:2, :])
    grad = (scale * (prob_student - prob_teacher)).astype(BF16)
    grad_logits[...] = grad
    products(grad, weight, which, parts)


def products_body(grad_logits, weight, *parts, which):
    products(grad_logits[...], weight, which, parts)


def head_body(*refs):
    blocks, (grad_logits, out_hbm, out, sems) = refs[: NCORE * RING], refs[NCORE * RING :]
    copies = []
    for i, block in enumerate(blocks):
        span = columns(part_at(i // RING, -(i % RING)), block.shape[1])
        out[i] = jnp.dot(
            grad_logits[...], block[...], preferred_element_type=F32
        ).astype(BF16)
        copy = pltpu.make_async_copy(out.at[i], out_hbm.at[:, span], sems.at[i])
        copy.start()
        copies.append(copy)
    for copy in copies:
        copy.wait()


def spread_body(a, b, c, d, back, *outs):
    total = a[...].astype(F32) + b[...].astype(F32) + c[...].astype(F32) + d[...].astype(F32)
    total = total.astype(BF16)
    rows, half = outs[0].shape
    here = second_place(lax.axis_index("core"))
    for k, out in enumerate(outs):
        span = columns(lax.rem(here + k, RING), rows)
        out[...] = (
            jnp.dot(back[0, span, :], total[:, :half], preferred_element_type=F32)
            + jnp.dot(back[1, span, :], total[:, half:], preferred_element_type=F32)
        ).astype(BF16)


def collect_body(parts, mine, other):
    peers, rows, half = parts.shape
    total = jnp.sum(parts[...].astype(F32).reshape(NZ, RING, rows, half), axis=0)
    low, high = total[:, : rows // 2], total[:, rows // 2 :]
    first = lax.axis_index("core") == 0
    mine[...] = jnp.where(first, low, high)
    other[...] = jnp.where(first, high, low)


def finish_body(mine, other, out, whole):
    half = mine.shape[2]
    first = lax.axis_index("core") == 0
    by_core = (
        jnp.where(first, mine[...], other[...]), jnp.where(first, other[...], mine[...]),
    )
    for i in range(out.shape[0]):
        for core in range(NCORE):
            for at in range(RING):
                for h in range(2):
                    start = ((core * RING + at) * 2 + h) * half
                    row = 2 * i + h
                    whole[i : i + 1, start : start + half] = by_core[core][at, row : row + 1]
    out[...] = whole[...].astype(BF16)


def swap_core(x):
    return lax.ppermute(x, "core", [(0, 1), (1, 0)])


def index(x, z, core, y):
    return ((x * NZ + z) * NCORE + core) * NY + y


def shift(v, k, ring=1):
    moves = []
    for x in range(NX):
        for z in range(NZ):
            for y in range(NY):
                for core in range(NCORE):
                    if (core == 0) == (ring == 1):
                        to = index(x, z, core, (y + k) % NY)
                    else:
                        to = index((x + k) % NX, z, core, y)
                    moves.append((index(x, z, core, y), to))
    return lax.ppermute(v, ALL, moves)


def peers():
    groups = []
    for second in range(RING):
        groups.append([index(second, z, 0, y) for z in range(NZ) for y in range(NY)])
        groups.append([index(x, z, 1, second) for z in range(NZ) for x in range(NX)])
    return groups


def per_device(hidden, head_weight, teacher, positions, counts):
    tokens, depth = hidden.shape
    capacity = positions.shape[1]
    shards = NX * NZ * NCORE
    slots = shards * capacity
    vocab = head_weight.shape[1]
    part = depth // (RING * NCORE)
    own = capacity // NY
    weight = head_weight.T
    half_flops = vocab * depth * MASKED
    logits_shape = shape((vocab, MASKED), F32)

    numbers = positions + tokens * counts
    send = call(
        pick_body, shape((shards, capacity, part), BF16), numbers, hidden, specs=[VMEM, HBM],
        scratch=[pltpu.VMEM((tokens + 16, part + depth // 2), BF16), DMA((2,))],
        limit=PICK_LIMIT,
    )
    rows = lax.all_to_all(send, SEQ, 0, 0, tiled=True).reshape(slots, part)
    picked, chosen, count = call(
        compact_body,
        (
            shape((MASKED, part), BF16), shape((MASKED, slots), BF16), shape((8, MASKED), F32),
        ),
        rows, flops=2 * MASKED * slots * part,
    )
    blocks = {(0, 0): picked} | {(0, k): shift(picked, k) for k in range(1, RING)}
    staged = call(
        teacher_body,
        (
            shape((vocab, MASKED), BF16), shape((8, MASKED), F32),
            shape((2, 2 * slots, MASKED), BF16),
        ),
        teacher.T, chosen, specs=[HBM, VMEM],
        scratch=[pltpu.VMEM((vocab, slots), BF16), DMA(())],
        flops=2 * vocab * slots * MASKED + 4 * slots * slots * MASKED,
    )
    blocks[0, 2], staged = lax.optimization_barrier((blocks[0, 2], staged))
    teacher_rows, lse_teacher, back = staged
    blocks |= {(1, k): swap_core(blocks[0, k]) for k in range(RING)}
    total = call(
        student_first_body, logits_shape, *[blocks[at] for at in FIRST], weight, flops=half_flops
    )
    blocks[1, 1], total = lax.optimization_barrier((blocks[1, 1], total))
    student, stats = call(
        student_last_body, (logits_shape, shape((NZ * RING, 2, MASKED), F32)),
        *[blocks[at] for at in LAST], weight, total, lse_teacher, flops=half_flops,
    )
    stats = lax.all_to_all(stats, ALL, 0, 0, tiled=True, axis_index_groups=peers())
    lse = call(combine_body, shape((2, MASKED), F32), stats)
    lse = call(join_body, shape((2, MASKED), F32), lse, *[shift(lse, k, ring=2) for k in (2, 1, 3)])
    parts = {}
    which = ((1, 2),)
    grad_logits, parts[1, 2] = call(
        functools.partial(logits_body, which=which),
        (shape((vocab, MASKED), BF16), shape((MASKED, part), BF16)),
        student, teacher_rows, lse, swap_core(lse), count, weight, flops=half_flops // 4,
    )
    sums = {}

    def make(which, tie):
        grad, tie = lax.optimization_barrier((grad_logits, tie))
        out = tuple(shape((MASKED, part), BF16 if side else F32) for side, k in which)
        made = call(
            functools.partial(products_body, which=which), out, grad, weight,
            flops=half_flops * len(which) // 4,
        )
        parts.update(zip(which, made))
        return tie

    def add(k):
        return (parts[0, k] + swap_core(parts[1, k]).astype(F32)).astype(BF16)

    make(((0, 2), (1, 1)), lse)
    make(((1, 3), (0, 1), (0, 3)), lse)
    both = {k: add(k) for k in (2, 1, 3)}
    both[1] = make(((1, 0), (0, 0)), both[1])
    sums = [add(0)] + [shift(both[k], k) for k in range(1, RING)]
    grad_head = call(
        head_body, shape((vocab, depth), BF16),
        *[blocks[side, k] for side in range(NCORE) for k in range(RING)], grad_logits, outs=HBM,
        scratch=[pltpu.VMEM((NCORE * RING, vocab, part), BF16), DMA((NCORE * RING,))],
        flops=2 * half_flops,
    )
    sums[1], grad_head = lax.optimization_barrier((sums[1], grad_head))
    steps = call(
        spread_body, (shape((2 * slots // RING, part // 2), BF16),) * RING, *sums, back,
        flops=4 * MASKED * slots * part,
    )
    steps = [steps[0]] + [shift(steps[k], k, ring=2) for k in (2, 1, 3)]
    partial = sum(step.astype(F32) for step in steps).astype(BF16)
    partial = lax.all_to_all(
        partial.reshape(NZ * RING, 8, part // 2), ALL, 0, 0, tiled=True,
        axis_index_groups=peers(),
    )
    mine, other = call(collect_body, (shape((RING, 4, part // 2), F32),) * 2, partial)
    grad_hidden = call(
        finish_body, shape((own, depth), BF16), mine, swap_core(other),
        scratch=[pltpu.VMEM((own, depth), F32)],
    )
    return grad_hidden, grad_head.T


def solution(mesh):
    fine = Mesh(mesh.devices.reshape(NX, NZ, NCORE, NY), ALL)
    return jax.shard_map(
        per_device,
        mesh=fine,
        in_specs=(P(SEQ, None), P(None, ALL), P(None, ALL), P(SEQ, None), P(SEQ)),
        out_specs=(P(ALL, None), P(None, ALL)),
        check_vma=False,
    )
```

```python
import functools

import jax
import jax.numpy as jnp
from jax import lax
from jax.experimental import pallas as pl
from jax.experimental.pallas import tpu as pltpu
from jax.sharding import Mesh, PartitionSpec as P

LOSS_SCALE = 1024.0
MASKED = 256
MARK = 64.0

SEQ = ("x", "z", "core")
ALL = ("x", "z", "core", "y")
NX, NZ, NCORE, NY = 4, 8, 2, 4
RING = 4
FIRST = ((0, 0), (0, 1), (0, 2), (0, 3), (1, 0), (1, 2))
LAST = ((1, 3), (1, 1))
Y_CORE = 1
assert NX == NY == RING
F32, BF16 = jnp.float32, jnp.bfloat16
NT = (((1,), (1,)), ((), ()))
TN = (((0,), (0,)), ((), ()))
VMEM = pl.BlockSpec(memory_space=pltpu.VMEM)
HBM = pl.BlockSpec(memory_space=pltpu.HBM)
DMA = pltpu.SemaphoreType.DMA
LIMIT, PICK_LIMIT = 32 << 20, 55996416


def call(body, out, *args, specs=None, outs=VMEM, flops=0, scratch=(), limit=LIMIT):
    leaves = jax.tree.leaves((args, out))
    nbytes = sum(x.size * x.dtype.itemsize for x in leaves)
    return pl.pallas_call(
        body,
        out_shape=out,
        in_specs=specs or [VMEM] * len(args),
        out_specs=jax.tree.map(lambda _: outs, out),
        scratch_shapes=list(scratch),
        cost_estimate=pl.CostEstimate(flops=flops, bytes_accessed=nbytes, transcendentals=0),
        compiler_params=pltpu.CompilerParams(vmem_limit_bytes=limit),
    )(*args)


def shape(dims, dtype):
    return jax.ShapeDtypeStruct(dims, dtype)


def columns(block, width):
    return pl.ds(pl.multiple_of(block * width, width), width)


def place(core):
    return jnp.where(core == Y_CORE, lax.axis_index("y"), lax.axis_index("x"))


def second_place(core):
    return jnp.where(core == Y_CORE, lax.axis_index("x"), lax.axis_index("y"))


def part_at(side, steps):
    core = lax.axis_index("core")
    core = core if side == 0 else 1 - core
    return core * RING + lax.rem(place(core) + steps + RING, RING)


def pick_body(numbers, hidden, out, mine, sems):
    shards, capacity, width = out.shape
    tokens, depth = hidden.shape
    mine_y, x_half = Y_CORE * RING + lax.axis_index("y"), (1 - Y_CORE) * (depth // 2)
    copies = [
        pltpu.make_async_copy(
            hidden.at[:, columns(mine_y, width)], mine.at[:tokens, :width], sems.at[0]
        ),
        pltpu.make_async_copy(
            hidden.at[:, x_half : x_half + depth // 2], mine.at[:tokens, width:], sems.at[1]
        ),
    ]
    for copy in copies:
        copy.start()
    more = (mine.shape[0] - tokens, mine.shape[1])
    mine[tokens:, :] = (lax.broadcasted_iota(jnp.int32, more, 0) == 0).astype(F32).astype(BF16)
    position, count = numbers[...] % tokens, numbers[...] // tokens
    masked = lax.broadcasted_iota(jnp.int32, numbers.shape, 1) < count
    row = lax.broadcasted_iota(jnp.int32, (mine.shape[0], capacity), 0)
    source = jnp.where(masked, position, tokens)
    hot = jnp.where(row == source, jnp.where(masked, 1.0, MARK), 0.0).astype(BF16)
    for copy in copies:
        copy.wait()
    rows = lax.dot_general(hot, mine[...], TN, preferred_element_type=F32)
    rows = rows.astype(BF16)
    for s in range(shards):
        start = 0 if s % NCORE == Y_CORE else (1 + s // (NZ * NCORE)) * width
        out[s] = rows[:, start : start + width]


def compact_body(rows, picked, chosen, count):
    slots = rows.shape[0]
    capacity = 8
    valid = (rows[...].astype(F32)[:, 0:1] < MARK / 2).astype(F32)
    a = lax.broadcasted_iota(jnp.int32, (slots, slots), 0)
    b = lax.broadcasted_iota(jnp.int32, (slots, slots), 1)
    spread = jnp.broadcast_to(valid, (slots, slots))
    rank = jnp.sum(jnp.where(a < b, spread, 0.0), axis=0, keepdims=True)
    mine = jnp.sum(jnp.where(a == b, spread, 0.0), axis=0, keepdims=True)
    total = jnp.sum(jnp.where(a // capacity == b // capacity, spread, 0.0), axis=0, keepdims=True)
    place = jnp.where(mine > 0.5, rank, -1.0).astype(jnp.int32)
    target = lax.broadcasted_iota(jnp.int32, (MASKED, slots), 0)
    hot = (target == place).astype(F32).astype(BF16)
    chosen[...] = hot
    picked[...] = jnp.dot(hot, rows[...], preferred_element_type=F32).astype(BF16)
    totals = jnp.broadcast_to(total, (8, slots)).astype(BF16)
    count[...] = lax.dot_general(totals, hot, NT, preferred_element_type=F32)


def logsumexp(x):
    top = jnp.max(x, axis=0, keepdims=True)
    return top + jnp.log(jnp.sum(jnp.exp(x - top), axis=0, keepdims=True))


def teacher_body(teacher_hbm, chosen, out, lse, back, teacher, sem):
    move = pltpu.make_async_copy(teacher_hbm, teacher, sem)
    move.start()
    halves, sent, masked = back.shape
    slots = chosen.shape[1]
    row = lax.broadcasted_iota(jnp.int32, (sent, slots), 0)
    second, z, first, q = row // 256, row // 32 % NZ, row // 8 % RING, row % 8
    straight = lax.axis_index("core") == Y_CORE
    x, y = jnp.where(straight, second, first), jnp.where(straight, first, second)
    slot = (x * NZ + z) * 16 + q // 4 * 8 + y * 2 + q // 2 % 2
    column = lax.broadcasted_iota(jnp.int32, (sent, slots), 1)
    pick = (column == slot).astype(F32).astype(BF16)
    placed = lax.dot_general(pick, chosen[...], NT, preferred_element_type=F32)
    odd = lax.broadcasted_iota(jnp.int32, (sent, masked), 0) % 2
    for h in range(halves):
        back[h] = jnp.where(odd == h, placed, 0.0).astype(BF16)
    move.wait()
    rows = lax.dot_general(teacher[...], chosen[...], NT, preferred_element_type=F32)
    out[...] = rows.astype(BF16)
    lse[...] = jnp.broadcast_to(logsumexp(rows), lse.shape)


def student_part(blocks, which, weight, total):
    for block, (side, k) in zip(blocks, which):
        total += lax.dot_general(
            weight[:, columns(part_at(side, -k), block.shape[1])], block[...],
            NT, preferred_element_type=F32,
        )
    return total


def student_first_body(*refs):
    blocks, (weight, total) = refs[: len(FIRST)], refs[len(FIRST) :]
    total[...] = student_part(blocks, FIRST, weight, jnp.zeros(total.shape, F32))


def student_last_body(*refs):
    blocks, (weight, first, lse_teacher, out, stats) = refs[: len(LAST)], refs[len(LAST) :]
    total = student_part(blocks, LAST, weight, first[...])
    out[...] = total
    both = jnp.concatenate([logsumexp(total), lse_teacher[0:1, :]], axis=0)
    stats[...] = jnp.broadcast_to(both[None], stats.shape)


def combine_body(stats, out):
    x = stats[...]
    top = jnp.max(x, axis=0)
    out[...] = top + jnp.log(jnp.sum(jnp.exp(x - top[None]), axis=0))


def join_body(a, b, c, d, out):
    top = jnp.maximum(jnp.maximum(a[...], b[...]), jnp.maximum(c[...], d[...]))
    out[...] = top + jnp.log(sum(jnp.exp(x[...] - top) for x in (a, b, c, d)))


def products(grad, weight, which, parts):
    for part, (side, k) in zip(parts, which):
        part[...] = lax.dot_general(
            grad, weight[:, columns(part_at(side, k), part.shape[1])], TN,
            preferred_element_type=F32,
        ).astype(part.dtype)


def logits_body(student, teacher, mine, other, count, weight, grad_logits, *parts, which):
    top = jnp.maximum(mine[...], other[...])
    lse = top + jnp.log(jnp.exp(mine[...] - top) + jnp.exp(other[...] - top))
    scale = LOSS_SCALE / count[0:1, :]
    prob_student = jnp.exp(student[...] - lse[0:1, :])
    prob_teacher = jnp.exp(teacher[...].astype(F32) - lse[1:2, :])
    grad = (scale * (prob_student - prob_teacher)).astype(BF16)
    grad_logits[...] = grad
    products(grad, weight, which, parts)


def products_body(grad_logits, weight, *parts, which):
    products(grad_logits[...], weight, which, parts)


def head_body(*refs):
    blocks, (grad_logits, out_hbm, out, sems) = refs[: NCORE * RING], refs[NCORE * RING :]
    copies = []
    for i, block in enumerate(blocks):
        span = columns(part_at(i // RING, -(i % RING)), block.shape[1])
        out[i] = jnp.dot(
            grad_logits[...], block[...], preferred_element_type=F32
        ).astype(BF16)
        copy = pltpu.make_async_copy(out.at[i], out_hbm.at[:, span], sems.at[i])
        copy.start()
        copies.append(copy)
    for copy in copies:
        copy.wait()


def spread_body(a, b, c, d, back, *outs):
    total = a[...].astype(F32) + b[...].astype(F32) + c[...].astype(F32) + d[...].astype(F32)
    total = total.astype(BF16)
    rows, half = outs[0].shape
    here = second_place(lax.axis_index("core"))
    for k, out in enumerate(outs):
        span = columns(lax.rem(here + k, RING), rows)
        out[...] = (
            jnp.dot(back[0, span, :], total[:, :half], preferred_element_type=F32)
            + jnp.dot(back[1, span, :], total[:, half:], preferred_element_type=F32)
        ).astype(BF16)


def collect_body(parts, mine, other):
    peers, rows, half = parts.shape
    total = jnp.sum(parts[...].astype(F32).reshape(NZ, RING, rows, half), axis=0)
    low, high = total[:, : rows // 2], total[:, rows // 2 :]
    first = lax.axis_index("core") == 0
    mine[...] = jnp.where(first, low, high)
    other[...] = jnp.where(first, high, low)


def finish_body(mine, other, out, whole):
    half = mine.shape[2]
    first = lax.axis_index("core") == 0
    by_core = (
        jnp.where(first, mine[...], other[...]), jnp.where(first, other[...], mine[...]),
    )
    for i in range(out.shape[0]):
        for core in range(NCORE):
            for at in range(RING):
                for h in range(2):
                    start = ((core * RING + at) * 2 + h) * half
                    row = 2 * i + h
                    whole[i : i + 1, start : start + half] = by_core[core][at, row : row + 1]
    out[...] = whole[...].astype(BF16)


def swap_core(x):
    return lax.ppermute(x, "core", [(0, 1), (1, 0)])


def index(x, z, core, y):
    return ((x * NZ + z) * NCORE + core) * NY + y


def shift(v, k, ring=1):
    moves = []
    for x in range(NX):
        for z in range(NZ):
            for y in range(NY):
                for core in range(NCORE):
                    if (core == Y_CORE) == (ring == 1):
                        to = index(x, z, core, (y + k) % NY)
                    else:
                        to = index((x + k) % NX, z, core, y)
                    moves.append((index(x, z, core, y), to))
    return lax.ppermute(v, ALL, moves)


def peers():
    groups = []
    for second in range(RING):
        groups.append([index(second, z, Y_CORE, y) for z in range(NZ) for y in range(NY)])
        groups.append([index(x, z, 1 - Y_CORE, second) for z in range(NZ) for x in range(NX)])
    return groups


def per_device(hidden, head_weight, teacher, positions, counts):
    tokens, depth = hidden.shape
    capacity = positions.shape[1]
    shards = NX * NZ * NCORE
    slots = shards * capacity
    vocab = head_weight.shape[1]
    part = depth // (RING * NCORE)
    own = capacity // NY
    weight = head_weight.T
    half_flops = vocab * depth * MASKED
    logits_shape = shape((vocab, MASKED), F32)

    numbers = positions + tokens * counts
    send = call(
        pick_body, shape((shards, capacity, part), BF16), numbers, hidden, specs=[VMEM, HBM],
        scratch=[pltpu.VMEM((tokens + 16, part + depth // 2), BF16), DMA((2,))],
        limit=PICK_LIMIT,
    )
    rows = lax.all_to_all(send, SEQ, 0, 0, tiled=True).reshape(slots, part)
    picked, chosen, count = call(
        compact_body,
        (
            shape((MASKED, part), BF16), shape((MASKED, slots), BF16), shape((8, MASKED), F32),
        ),
        rows, flops=2 * MASKED * slots * part,
    )
    blocks = {(0, 0): picked} | {(0, k): shift(picked, k) for k in range(1, RING)}
    staged = call(
        teacher_body,
        (
            shape((vocab, MASKED), BF16), shape((8, MASKED), F32),
            shape((2, 2 * slots, MASKED), BF16),
        ),
        teacher.T, chosen, specs=[HBM, VMEM],
        scratch=[pltpu.VMEM((vocab, slots), BF16), DMA(())],
        flops=2 * vocab * slots * MASKED + 4 * slots * slots * MASKED,
    )
    blocks[0, 2], staged = lax.optimization_barrier((blocks[0, 2], staged))
    teacher_rows, lse_teacher, back = staged
    blocks |= {(1, k): swap_core(blocks[0, k]) for k in range(RING)}
    total = call(
        student_first_body, logits_shape, *[blocks[at] for at in FIRST], weight, flops=half_flops
    )
    blocks[1, 1], total = lax.optimization_barrier((blocks[1, 1], total))
    student, stats = call(
        student_last_body, (logits_shape, shape((NZ * RING, 2, MASKED), F32)),
        *[blocks[at] for at in LAST], weight, total, lse_teacher, flops=half_flops,
    )
    stats = lax.all_to_all(stats, ALL, 0, 0, tiled=True, axis_index_groups=peers())
    lse = call(combine_body, shape((2, MASKED), F32), stats)
    lse = call(join_body, shape((2, MASKED), F32), lse, *[shift(lse, k, ring=2) for k in (3, 1, 2)])
    parts = {}
    which = ((1, 2),)
    grad_logits, parts[1, 2] = call(
        functools.partial(logits_body, which=which),
        (shape((vocab, MASKED), BF16), shape((MASKED, part), BF16)),
        student, teacher_rows, lse, swap_core(lse), count, weight, flops=half_flops // 4,
    )
    sums = {}

    def make(which, tie):
        grad, tie = lax.optimization_barrier((grad_logits, tie))
        out = tuple(shape((MASKED, part), BF16 if side else F32) for side, k in which)
        made = call(
            functools.partial(products_body, which=which), out, grad, weight,
            flops=half_flops * len(which) // 4,
        )
        parts.update(zip(which, made))
        return tie

    def add(k):
        return (parts[0, k] + swap_core(parts[1, k]).astype(F32)).astype(BF16)

    make(((0, 2), (1, 1)), lse)
    make(((1, 3), (0, 1), (0, 3)), lse)
    both = {k: add(k) for k in (2, 1, 3)}
    both[1] = make(((1, 0), (0, 0)), both[1])
    sums = [add(0)] + [shift(both[k], k) for k in range(1, RING)]
    grad_head = call(
        head_body, shape((vocab, depth), BF16),
        *[blocks[side, k] for side in range(NCORE) for k in range(RING)], grad_logits, outs=HBM,
        scratch=[pltpu.VMEM((NCORE * RING, vocab, part), BF16), DMA((NCORE * RING,))],
        flops=2 * half_flops,
    )
    sums[1], grad_head = lax.optimization_barrier((sums[1], grad_head))
    steps = call(
        spread_body, (shape((2 * slots // RING, part // 2), BF16),) * RING, *sums, back,
        flops=4 * MASKED * slots * part,
    )
    steps = [steps[0]] + [shift(steps[k], k, ring=2) for k in (2, 1, 3)]
    partial = sum(step.astype(F32) for step in steps).astype(BF16)
    partial = lax.all_to_all(
        partial.reshape(NZ * RING, 8, part // 2), ALL, 0, 0, tiled=True,
        axis_index_groups=peers(),
    )
    mine, other = call(collect_body, (shape((RING, 4, part // 2), F32),) * 2, partial)
    grad_hidden = call(
        finish_body, shape((own, depth), BF16), mine, swap_core(other),
        scratch=[pltpu.VMEM((own, depth), F32)],
    )
    return grad_hidden, grad_head.T


def solution(mesh):
    fine = Mesh(mesh.devices.reshape(NX, NZ, NCORE, NY), ALL)
    return jax.shard_map(
        per_device,
        mesh=fine,
        in_specs=(P(SEQ, None), P(None, ALL), P(None, ALL), P(SEQ, None), P(SEQ)),
        out_specs=(P(ALL, None), P(None, ALL)),
        check_vma=False,
    )
```

```python
import functools

import jax
import jax.numpy as jnp
from jax import lax
from jax.experimental import pallas as pl
from jax.experimental.pallas import tpu as pltpu
from jax.sharding import Mesh, PartitionSpec as P

LOSS_SCALE = 1024.0
MASKED = 256
MARK = 64.0

SEQ = ("x", "z", "core")
ALL = ("x", "z", "core", "y")
NX, NZ, NCORE, NY = 4, 8, 2, 4
RING = 4
ZS = tuple(reversed(range(NZ)))
FIRST = ((0, 0), (0, 1), (0, 2), (0, 3), (1, 0), (1, 2))
LAST = ((1, 3), (1, 1))
Y_CORE = 1
assert NX == NY == RING
F32, BF16 = jnp.float32, jnp.bfloat16
NT = (((1,), (1,)), ((), ()))
TN = (((0,), (0,)), ((), ()))
VMEM = pl.BlockSpec(memory_space=pltpu.VMEM)
HBM = pl.BlockSpec(memory_space=pltpu.HBM)
DMA = pltpu.SemaphoreType.DMA
LIMIT, PICK_LIMIT = 32 << 20, 55996416


def call(body, out, *args, specs=None, outs=VMEM, flops=0, scratch=(), limit=LIMIT):
    leaves = jax.tree.leaves((args, out))
    nbytes = sum(x.size * x.dtype.itemsize for x in leaves)
    return pl.pallas_call(
        body,
        out_shape=out,
        in_specs=specs or [VMEM] * len(args),
        out_specs=jax.tree.map(lambda _: outs, out),
        scratch_shapes=list(scratch),
        cost_estimate=pl.CostEstimate(flops=flops, bytes_accessed=nbytes, transcendentals=0),
        compiler_params=pltpu.CompilerParams(vmem_limit_bytes=limit),
    )(*args)


def shape(dims, dtype):
    return jax.ShapeDtypeStruct(dims, dtype)


def columns(block, width):
    return pl.ds(pl.multiple_of(block * width, width), width)


def place(core):
    return jnp.where(core == Y_CORE, lax.axis_index("y"), lax.axis_index("x"))


def second_place(core):
    return jnp.where(core == Y_CORE, lax.axis_index("x"), lax.axis_index("y"))


def part_at(side, steps):
    core = lax.axis_index("core")
    core = core if side == 0 else 1 - core
    return core * RING + lax.rem(place(core) + steps + RING, RING)


def pick_body(numbers, hidden, out, mine, sems):
    shards, capacity, width = out.shape
    tokens, depth = hidden.shape
    mine_y, x_half = Y_CORE * RING + lax.axis_index("y"), (1 - Y_CORE) * (depth // 2)
    copies = [
        pltpu.make_async_copy(
            hidden.at[:, columns(mine_y, width)], mine.at[:tokens, :width], sems.at[0]
        ),
        pltpu.make_async_copy(
            hidden.at[:, x_half : x_half + depth // 2], mine.at[:tokens, width:], sems.at[1]
        ),
    ]
    for copy in copies:
        copy.start()
    more = (mine.shape[0] - tokens, mine.shape[1])
    mine[tokens:, :] = (lax.broadcasted_iota(jnp.int32, more, 0) == 0).astype(F32).astype(BF16)
    position, count = numbers[...] % tokens, numbers[...] // tokens
    masked = lax.broadcasted_iota(jnp.int32, numbers.shape, 1) < count
    row = lax.broadcasted_iota(jnp.int32, (mine.shape[0], capacity), 0)
    source = jnp.where(masked, position, tokens)
    hot = jnp.where(row == source, jnp.where(masked, 1.0, MARK), 0.0).astype(BF16)
    for copy in copies:
        copy.wait()
    rows = lax.dot_general(hot, mine[...], TN, preferred_element_type=F32)
    rows = rows.astype(BF16)
    for s in range(shards):
        start = 0 if s % NCORE == Y_CORE else (1 + s // (NZ * NCORE)) * width
        out[s] = rows[:, start : start + width]


def compact_body(rows, picked, chosen, count):
    slots = rows.shape[0]
    capacity = 8
    valid = (rows[...].astype(F32)[:, 0:1] < MARK / 2).astype(F32)
    a = lax.broadcasted_iota(jnp.int32, (slots, slots), 0)
    b = lax.broadcasted_iota(jnp.int32, (slots, slots), 1)
    spread = jnp.broadcast_to(valid, (slots, slots))
    rank = jnp.sum(jnp.where(a < b, spread, 0.0), axis=0, keepdims=True)
    mine = jnp.sum(jnp.where(a == b, spread, 0.0), axis=0, keepdims=True)
    total = jnp.sum(jnp.where(a // capacity == b // capacity, spread, 0.0), axis=0, keepdims=True)
    place = jnp.where(mine > 0.5, rank, -1.0).astype(jnp.int32)
    target = lax.broadcasted_iota(jnp.int32, (MASKED, slots), 0)
    hot = (target == place).astype(F32).astype(BF16)
    chosen[...] = hot
    picked[...] = jnp.dot(hot, rows[...], preferred_element_type=F32).astype(BF16)
    totals = jnp.broadcast_to(total, (8, slots)).astype(BF16)
    count[...] = lax.dot_general(totals, hot, NT, preferred_element_type=F32)


def logsumexp(x):
    top = jnp.max(x, axis=0, keepdims=True)
    return top + jnp.log(jnp.sum(jnp.exp(x - top), axis=0, keepdims=True))


def teacher_body(teacher_hbm, chosen, out, lse, back, teacher, sem):
    move = pltpu.make_async_copy(teacher_hbm, teacher, sem)
    move.start()
    halves, sent, masked = back.shape
    slots = chosen.shape[1]
    row = lax.broadcasted_iota(jnp.int32, (sent, slots), 0)
    second, z, first, q = row // 256, NZ - 1 - row // 32 % NZ, row // 8 % RING, row % 8
    straight = lax.axis_index("core") == Y_CORE
    x, y = jnp.where(straight, second, first), jnp.where(straight, first, second)
    slot = (x * NZ + z) * 16 + q // 4 * 8 + y * 2 + q // 2 % 2
    column = lax.broadcasted_iota(jnp.int32, (sent, slots), 1)
    pick = (column == slot).astype(F32).astype(BF16)
    placed = lax.dot_general(pick, chosen[...], NT, preferred_element_type=F32)
    odd = lax.broadcasted_iota(jnp.int32, (sent, masked), 0) % 2
    for h in range(halves):
        back[h] = jnp.where(odd == h, placed, 0.0).astype(BF16)
    move.wait()
    rows = lax.dot_general(teacher[...], chosen[...], NT, preferred_element_type=F32)
    out[...] = rows.astype(BF16)
    lse[...] = jnp.broadcast_to(logsumexp(rows), lse.shape)


def student_part(blocks, which, weight, total):
    for block, (side, k) in zip(blocks, which):
        total += lax.dot_general(
            weight[:, columns(part_at(side, -k), block.shape[1])], block[...],
            NT, preferred_element_type=F32,
        )
    return total


def student_first_body(*refs):
    blocks, (weight, total) = refs[: len(FIRST)], refs[len(FIRST) :]
    total[...] = student_part(blocks, FIRST, weight, jnp.zeros(total.shape, F32))


def student_last_body(*refs):
    blocks, (weight, first, lse_teacher, out, stats) = refs[: len(LAST)], refs[len(LAST) :]
    total = student_part(blocks, LAST, weight, first[...])
    out[...] = total
    both = jnp.concatenate([logsumexp(total), lse_teacher[0:1, :]], axis=0)
    stats[...] = jnp.broadcast_to(both[None], stats.shape)


def combine_body(stats, out):
    x = stats[...]
    top = jnp.max(x, axis=0)
    out[...] = top + jnp.log(jnp.sum(jnp.exp(x - top[None]), axis=0))


def join_body(a, b, c, d, out):
    top = jnp.maximum(jnp.maximum(a[...], b[...]), jnp.maximum(c[...], d[...]))
    out[...] = top + jnp.log(sum(jnp.exp(x[...] - top) for x in (a, b, c, d)))


def products(grad, weight, which, parts):
    for part, (side, k) in zip(parts, which):
        part[...] = lax.dot_general(
            grad, weight[:, columns(part_at(side, k), part.shape[1])], TN,
            preferred_element_type=F32,
        ).astype(part.dtype)


def logits_body(student, teacher, mine, other, count, weight, grad_logits, *parts, which):
    top = jnp.maximum(mine[...], other[...])
    lse = top + jnp.log(jnp.exp(mine[...] - top) + jnp.exp(other[...] - top))
    scale = LOSS_SCALE / count[0:1, :]
    prob_student = jnp.exp(student[...] - lse[0:1, :])
    prob_teacher = jnp.exp(teacher[...].astype(F32) - lse[1:2, :])
    grad = (scale * (prob_student - prob_teacher)).astype(BF16)
    grad_logits[...] = grad
    products(grad, weight, which, parts)


def products_body(grad_logits, weight, *parts, which):
    products(grad_logits[...], weight, which, parts)


def head_body(*refs):
    blocks, (grad_logits, out_hbm, out, sems) = refs[: NCORE * RING], refs[NCORE * RING :]
    copies = []
    for i, block in enumerate(blocks):
        span = columns(part_at(i // RING, -(i % RING)), block.shape[1])
        out[i] = jnp.dot(
            grad_logits[...], block[...], preferred_element_type=F32
        ).astype(BF16)
        copy = pltpu.make_async_copy(out.at[i], out_hbm.at[:, span], sems.at[i])
        copy.start()
        copies.append(copy)
    for copy in copies:
        copy.wait()


def spread_body(a, b, c, d, back, *outs):
    total = a[...].astype(F32) + b[...].astype(F32) + c[...].astype(F32) + d[...].astype(F32)
    total = total.astype(BF16)
    rows, half = outs[0].shape
    here = second_place(lax.axis_index("core"))
    for k, out in enumerate(outs):
        span = columns(lax.rem(here + k, RING), rows)
        out[...] = (
            jnp.dot(back[0, span, :], total[:, :half], preferred_element_type=F32)
            + jnp.dot(back[1, span, :], total[:, half:], preferred_element_type=F32)
        ).astype(BF16)


def collect_body(parts, mine, other):
    peers, rows, half = parts.shape
    total = jnp.sum(parts[...].astype(F32).reshape(NZ, RING, rows, half), axis=0)
    low, high = total[:, : rows // 2], total[:, rows // 2 :]
    first = lax.axis_index("core") == 0
    mine[...] = jnp.where(first, low, high)
    other[...] = jnp.where(first, high, low)


def finish_body(mine, other, out, whole):
    half = mine.shape[2]
    first = lax.axis_index("core") == 0
    by_core = (
        jnp.where(first, mine[...], other[...]), jnp.where(first, other[...], mine[...]),
    )
    for i in range(out.shape[0]):
        for core in range(NCORE):
            for at in range(RING):
                for h in range(2):
                    start = ((core * RING + at) * 2 + h) * half
                    row = 2 * i + h
                    whole[i : i + 1, start : start + half] = by_core[core][at, row : row + 1]
    out[...] = whole[...].astype(BF16)


def swap_core(x):
    return lax.ppermute(x, "core", [(0, 1), (1, 0)])


def index(x, z, core, y):
    return ((x * NZ + z) * NCORE + core) * NY + y


def shift(v, k, ring=1):
    moves = []
    for x in range(NX):
        for z in range(NZ):
            for y in range(NY):
                for core in range(NCORE):
                    if (core == Y_CORE) == (ring == 1):
                        to = index(x, z, core, (y + k) % NY)
                    else:
                        to = index((x + k) % NX, z, core, y)
                    moves.append((index(x, z, core, y), to))
    return lax.ppermute(v, ALL, moves)


def peers():
    groups = []
    for second in range(RING):
        groups.append([index(second, z, Y_CORE, y) for z in ZS for y in range(NY)])
        groups.append([index(x, z, 1 - Y_CORE, second) for z in ZS for x in range(NX)])
    return groups


def per_device(hidden, head_weight, teacher, positions, counts):
    tokens, depth = hidden.shape
    capacity = positions.shape[1]
    shards = NX * NZ * NCORE
    slots = shards * capacity
    vocab = head_weight.shape[1]
    part = depth // (RING * NCORE)
    own = capacity // NY
    weight = head_weight.T
    half_flops = vocab * depth * MASKED
    logits_shape = shape((vocab, MASKED), F32)

    numbers = positions + tokens * counts
    send = call(
        pick_body, shape((shards, capacity, part), BF16), numbers, hidden, specs=[VMEM, HBM],
        scratch=[pltpu.VMEM((tokens + 16, part + depth // 2), BF16), DMA((2,))],
        limit=PICK_LIMIT,
    )
    rows = lax.all_to_all(send, SEQ, 0, 0, tiled=True).reshape(slots, part)
    picked, chosen, count = call(
        compact_body,
        (
            shape((MASKED, part), BF16), shape((MASKED, slots), BF16), shape((8, MASKED), F32),
        ),
        rows, flops=2 * MASKED * slots * part,
    )
    blocks = {(0, 0): picked} | {(0, k): shift(picked, k) for k in range(1, RING)}
    staged = call(
        teacher_body,
        (
            shape((vocab, MASKED), BF16), shape((8, MASKED), F32),
            shape((2, 2 * slots, MASKED), BF16),
        ),
        teacher.T, chosen, specs=[HBM, VMEM],
        scratch=[pltpu.VMEM((vocab, slots), BF16), DMA(())],
        flops=2 * vocab * slots * MASKED + 4 * slots * slots * MASKED,
    )
    blocks[0, 2], staged = lax.optimization_barrier((blocks[0, 2], staged))
    teacher_rows, lse_teacher, back = staged
    blocks |= {(1, k): swap_core(blocks[0, k]) for k in range(RING)}
    total = call(
        student_first_body, logits_shape, *[blocks[at] for at in FIRST], weight, flops=half_flops
    )
    blocks[1, 1], total = lax.optimization_barrier((blocks[1, 1], total))
    student, stats = call(
        student_last_body, (logits_shape, shape((NZ * RING, 2, MASKED), F32)),
        *[blocks[at] for at in LAST], weight, total, lse_teacher, flops=half_flops,
    )
    stats = lax.all_to_all(stats, ALL, 0, 0, tiled=True, axis_index_groups=peers())
    lse = call(combine_body, shape((2, MASKED), F32), stats)
    lse = call(join_body, shape((2, MASKED), F32), lse, *[shift(lse, k, ring=2) for k in (3, 1, 2)])
    parts = {}
    which = ((1, 2),)
    grad_logits, parts[1, 2] = call(
        functools.partial(logits_body, which=which),
        (shape((vocab, MASKED), BF16), shape((MASKED, part), BF16)),
        student, teacher_rows, lse, swap_core(lse), count, weight, flops=half_flops // 4,
    )
    sums = {}

    def make(which, tie):
        grad, tie = lax.optimization_barrier((grad_logits, tie))
        out = tuple(shape((MASKED, part), BF16 if side else F32) for side, k in which)
        made = call(
            functools.partial(products_body, which=which), out, grad, weight,
            flops=half_flops * len(which) // 4,
        )
        parts.update(zip(which, made))
        return tie

    def add(k):
        return (parts[0, k] + swap_core(parts[1, k]).astype(F32)).astype(BF16)

    make(((0, 2), (1, 1)), lse)
    make(((1, 3), (0, 1), (0, 3)), lse)
    both = {k: add(k) for k in (2, 1, 3)}
    both[1] = make(((1, 0), (0, 0)), both[1])
    sums = [add(0)] + [shift(both[k], k) for k in range(1, RING)]
    grad_head = call(
        head_body, shape((vocab, depth), BF16),
        *[blocks[side, k] for side in range(NCORE) for k in range(RING)], grad_logits, outs=HBM,
        scratch=[pltpu.VMEM((NCORE * RING, vocab, part), BF16), DMA((NCORE * RING,))],
        flops=2 * half_flops,
    )
    sums[1], grad_head = lax.optimization_barrier((sums[1], grad_head))
    steps = call(
        spread_body, (shape((2 * slots // RING, part // 2), BF16),) * RING, *sums, back,
        flops=4 * MASKED * slots * part,
    )
    steps = [steps[0]] + [shift(steps[k], k, ring=2) for k in (2, 1, 3)]
    partial = sum(step.astype(F32) for step in steps).astype(BF16)
    partial = lax.all_to_all(
        partial.reshape(NZ * RING, 8, part // 2), ALL, 0, 0, tiled=True,
        axis_index_groups=peers(),
    )
    mine, other = call(collect_body, (shape((RING, 4, part // 2), F32),) * 2, partial)
    grad_hidden = call(
        finish_body, shape((own, depth), BF16), mine, swap_core(other),
        scratch=[pltpu.VMEM((own, depth), F32)],
    )
    return grad_hidden, grad_head.T


def solution(mesh):
    fine = Mesh(mesh.devices.reshape(NX, NZ, NCORE, NY), ALL)
    return jax.shard_map(
        per_device,
        mesh=fine,
        in_specs=(P(SEQ, None), P(None, ALL), P(None, ALL), P(SEQ, None), P(SEQ)),
        out_specs=(P(ALL, None), P(None, ALL)),
        check_vma=False,
    )
```

```python
import functools

import jax
import jax.numpy as jnp
from jax import lax
from jax.experimental import pallas as pl
from jax.experimental.pallas import tpu as pltpu
from jax.sharding import Mesh, PartitionSpec as P

LOSS_SCALE = 1024.0
MASKED = 256
MARK = 64.0

SEQ = ("x", "z", "core")
ALL = ("x", "z", "core", "y")
NX, NZ, NCORE, NY = 4, 8, 2, 4
RING = 4
ZS = tuple((z + NZ // 2) % NZ for z in range(NZ))
FIRST = ((0, 0), (0, 1), (0, 2), (0, 3), (1, 0), (1, 2))
LAST = ((1, 3), (1, 1))
Y_CORE = 1
assert NX == NY == RING
F32, BF16 = jnp.float32, jnp.bfloat16
NT = (((1,), (1,)), ((), ()))
TN = (((0,), (0,)), ((), ()))
VMEM = pl.BlockSpec(memory_space=pltpu.VMEM)
HBM = pl.BlockSpec(memory_space=pltpu.HBM)
DMA = pltpu.SemaphoreType.DMA
LIMIT, PICK_LIMIT = 32 << 20, 55996416


def call(body, out, *args, specs=None, outs=VMEM, flops=0, scratch=(), limit=LIMIT):
    leaves = jax.tree.leaves((args, out))
    nbytes = sum(x.size * x.dtype.itemsize for x in leaves)
    return pl.pallas_call(
        body,
        out_shape=out,
        in_specs=specs or [VMEM] * len(args),
        out_specs=jax.tree.map(lambda _: outs, out),
        scratch_shapes=list(scratch),
        cost_estimate=pl.CostEstimate(flops=flops, bytes_accessed=nbytes, transcendentals=0),
        compiler_params=pltpu.CompilerParams(vmem_limit_bytes=limit),
    )(*args)


def shape(dims, dtype):
    return jax.ShapeDtypeStruct(dims, dtype)


def columns(block, width):
    return pl.ds(pl.multiple_of(block * width, width), width)


def place(core):
    return jnp.where(core == Y_CORE, lax.axis_index("y"), lax.axis_index("x"))


def second_place(core):
    return jnp.where(core == Y_CORE, lax.axis_index("x"), lax.axis_index("y"))


def part_at(side, steps):
    core = lax.axis_index("core")
    core = core if side == 0 else 1 - core
    return core * RING + lax.rem(place(core) + steps + RING, RING)


def pick_body(numbers, hidden, out, mine, sems):
    shards, capacity, width = out.shape
    tokens, depth = hidden.shape
    mine_y, x_half = Y_CORE * RING + lax.axis_index("y"), (1 - Y_CORE) * (depth // 2)
    copies = [
        pltpu.make_async_copy(
            hidden.at[:, columns(mine_y, width)], mine.at[:tokens, :width], sems.at[0]
        ),
        pltpu.make_async_copy(
            hidden.at[:, x_half : x_half + depth // 2], mine.at[:tokens, width:], sems.at[1]
        ),
    ]
    for copy in copies:
        copy.start()
    more = (mine.shape[0] - tokens, mine.shape[1])
    mine[tokens:, :] = (lax.broadcasted_iota(jnp.int32, more, 0) == 0).astype(F32).astype(BF16)
    position, count = numbers[...] % tokens, numbers[...] // tokens
    masked = lax.broadcasted_iota(jnp.int32, numbers.shape, 1) < count
    row = lax.broadcasted_iota(jnp.int32, (mine.shape[0], capacity), 0)
    source = jnp.where(masked, position, tokens)
    hot = jnp.where(row == source, jnp.where(masked, 1.0, MARK), 0.0).astype(BF16)
    for copy in copies:
        copy.wait()
    rows = lax.dot_general(hot, mine[...], TN, preferred_element_type=F32)
    rows = rows.astype(BF16)
    for s in range(shards):
        start = 0 if s % NCORE == Y_CORE else (1 + s // (NZ * NCORE)) * width
        out[s] = rows[:, start : start + width]


def compact_body(rows, picked, chosen, count):
    slots = rows.shape[0]
    capacity = 8
    valid = (rows[...].astype(F32)[:, 0:1] < MARK / 2).astype(F32)
    a = lax.broadcasted_iota(jnp.int32, (slots, slots), 0)
    b = lax.broadcasted_iota(jnp.int32, (slots, slots), 1)
    spread = jnp.broadcast_to(valid, (slots, slots))
    rank = jnp.sum(jnp.where(a < b, spread, 0.0), axis=0, keepdims=True)
    mine = jnp.sum(jnp.where(a == b, spread, 0.0), axis=0, keepdims=True)
    total = jnp.sum(jnp.where(a // capacity == b // capacity, spread, 0.0), axis=0, keepdims=True)
    place = jnp.where(mine > 0.5, rank, -1.0).astype(jnp.int32)
    target = lax.broadcasted_iota(jnp.int32, (MASKED, slots), 0)
    hot = (target == place).astype(F32).astype(BF16)
    chosen[...] = hot
    picked[...] = jnp.dot(hot, rows[...], preferred_element_type=F32).astype(BF16)
    totals = jnp.broadcast_to(total, (8, slots)).astype(BF16)
    count[...] = lax.dot_general(totals, hot, NT, preferred_element_type=F32)


def logsumexp(x):
    top = jnp.max(x, axis=0, keepdims=True)
    return top + jnp.log(jnp.sum(jnp.exp(x - top), axis=0, keepdims=True))


def teacher_body(teacher_hbm, chosen, out, lse, back, teacher, sem):
    move = pltpu.make_async_copy(teacher_hbm, teacher, sem)
    move.start()
    halves, sent, masked = back.shape
    slots = chosen.shape[1]
    row = lax.broadcasted_iota(jnp.int32, (sent, slots), 0)
    second, z, first, q = row // 256, (row // 32 + NZ // 2) % NZ, row // 8 % RING, row % 8
    straight = lax.axis_index("core") == Y_CORE
    x, y = jnp.where(straight, second, first), jnp.where(straight, first, second)
    slot = (x * NZ + z) * 16 + q // 4 * 8 + y * 2 + q // 2 % 2
    column = lax.broadcasted_iota(jnp.int32, (sent, slots), 1)
    pick = (column == slot).astype(F32).astype(BF16)
    placed = lax.dot_general(pick, chosen[...], NT, preferred_element_type=F32)
    odd = lax.broadcasted_iota(jnp.int32, (sent, masked), 0) % 2
    for h in range(halves):
        back[h] = jnp.where(odd == h, placed, 0.0).astype(BF16)
    move.wait()
    rows = lax.dot_general(teacher[...], chosen[...], NT, preferred_element_type=F32)
    out[...] = rows.astype(BF16)
    lse[...] = jnp.broadcast_to(logsumexp(rows), lse.shape)


def student_part(blocks, which, weight, total):
    for block, (side, k) in zip(blocks, which):
        total += lax.dot_general(
            weight[:, columns(part_at(side, -k), block.shape[1])], block[...],
            NT, preferred_element_type=F32,
        )
    return total


def student_first_body(*refs):
    blocks, (weight, total) = refs[: len(FIRST)], refs[len(FIRST) :]
    total[...] = student_part(blocks, FIRST, weight, jnp.zeros(total.shape, F32))


def student_last_body(*refs):
    blocks, (weight, first, lse_teacher, out, stats) = refs[: len(LAST)], refs[len(LAST) :]
    total = student_part(blocks, LAST, weight, first[...])
    out[...] = total
    both = jnp.concatenate([logsumexp(total), lse_teacher[0:1, :]], axis=0)
    stats[...] = jnp.broadcast_to(both[None], stats.shape)


def combine_body(stats, out):
    x = stats[...]
    top = jnp.max(x, axis=0)
    out[...] = top + jnp.log(jnp.sum(jnp.exp(x - top[None]), axis=0))


def join_body(a, b, c, d, out):
    top = jnp.maximum(jnp.maximum(a[...], b[...]), jnp.maximum(c[...], d[...]))
    out[...] = top + jnp.log(sum(jnp.exp(x[...] - top) for x in (a, b, c, d)))


def products(grad, weight, which, parts):
    for part, (side, k) in zip(parts, which):
        part[...] = lax.dot_general(
            grad, weight[:, columns(part_at(side, k), part.shape[1])], TN,
            preferred_element_type=F32,
        ).astype(part.dtype)


def logits_body(student, teacher, mine, other, count, weight, grad_logits, *parts, which):
    top = jnp.maximum(mine[...], other[...])
    lse = top + jnp.log(jnp.exp(mine[...] - top) + jnp.exp(other[...] - top))
    scale = LOSS_SCALE / count[0:1, :]
    prob_student = jnp.exp(student[...] - lse[0:1, :])
    prob_teacher = jnp.exp(teacher[...].astype(F32) - lse[1:2, :])
    grad = (scale * (prob_student - prob_teacher)).astype(BF16)
    grad_logits[...] = grad
    products(grad, weight, which, parts)


def products_body(grad_logits, weight, *parts, which):
    products(grad_logits[...], weight, which, parts)


def head_body(*refs):
    blocks, (grad_logits, out_hbm, out, sems) = refs[: NCORE * RING], refs[NCORE * RING :]
    copies = []
    for i, block in enumerate(blocks):
        span = columns(part_at(i // RING, -(i % RING)), block.shape[1])
        out[i] = jnp.dot(
            grad_logits[...], block[...], preferred_element_type=F32
        ).astype(BF16)
        copy = pltpu.make_async_copy(out.at[i], out_hbm.at[:, span], sems.at[i])
        copy.start()
        copies.append(copy)
    for copy in copies:
        copy.wait()


def spread_body(a, b, c, d, back, *outs):
    total = a[...].astype(F32) + b[...].astype(F32) + c[...].astype(F32) + d[...].astype(F32)
    total = total.astype(BF16)
    rows, half = outs[0].shape
    here = second_place(lax.axis_index("core"))
    for k, out in enumerate(outs):
        span = columns(lax.rem(here + k, RING), rows)
        out[...] = (
            jnp.dot(back[0, span, :], total[:, :half], preferred_element_type=F32)
            + jnp.dot(back[1, span, :], total[:, half:], preferred_element_type=F32)
        ).astype(BF16)


def collect_body(parts, mine, other):
    peers, rows, half = parts.shape
    total = jnp.sum(parts[...].astype(F32).reshape(NZ, RING, rows, half), axis=0)
    low, high = total[:, : rows // 2], total[:, rows // 2 :]
    first = lax.axis_index("core") == 0
    mine[...] = jnp.where(first, low, high)
    other[...] = jnp.where(first, high, low)


def finish_body(mine, other, out, whole):
    half = mine.shape[2]
    first = lax.axis_index("core") == 0
    by_core = (
        jnp.where(first, mine[...], other[...]), jnp.where(first, other[...], mine[...]),
    )
    for i in range(out.shape[0]):
        for core in range(NCORE):
            for at in range(RING):
                for h in range(2):
                    start = ((core * RING + at) * 2 + h) * half
                    row = 2 * i + h
                    whole[i : i + 1, start : start + half] = by_core[core][at, row : row + 1]
    out[...] = whole[...].astype(BF16)


def swap_core(x):
    return lax.ppermute(x, "core", [(0, 1), (1, 0)])


def index(x, z, core, y):
    return ((x * NZ + z) * NCORE + core) * NY + y


def shift(v, k, ring=1):
    moves = []
    for x in range(NX):
        for z in range(NZ):
            for y in range(NY):
                for core in range(NCORE):
                    if (core == Y_CORE) == (ring == 1):
                        to = index(x, z, core, (y + k) % NY)
                    else:
                        to = index((x + k) % NX, z, core, y)
                    moves.append((index(x, z, core, y), to))
    return lax.ppermute(v, ALL, moves)


def peers():
    groups = []
    for second in range(RING):
        groups.append([index(second, z, Y_CORE, y) for z in ZS for y in range(NY)])
        groups.append([index(x, z, 1 - Y_CORE, second) for z in ZS for x in range(NX)])
    return groups


def per_device(hidden, head_weight, teacher, positions, counts):
    tokens, depth = hidden.shape
    capacity = positions.shape[1]
    shards = NX * NZ * NCORE
    slots = shards * capacity
    vocab = head_weight.shape[1]
    part = depth // (RING * NCORE)
    own = capacity // NY
    weight = head_weight.T
    half_flops = vocab * depth * MASKED
    logits_shape = shape((vocab, MASKED), F32)

    numbers = positions + tokens * counts
    send = call(
        pick_body, shape((shards, capacity, part), BF16), numbers, hidden, specs=[VMEM, HBM],
        scratch=[pltpu.VMEM((tokens + 16, part + depth // 2), BF16), DMA((2,))],
        limit=PICK_LIMIT,
    )
    rows = lax.all_to_all(send, SEQ, 0, 0, tiled=True).reshape(slots, part)
    picked, chosen, count = call(
        compact_body,
        (
            shape((MASKED, part), BF16), shape((MASKED, slots), BF16), shape((8, MASKED), F32),
        ),
        rows, flops=2 * MASKED * slots * part,
    )
    blocks = {(0, 0): picked} | {(0, k): shift(picked, k) for k in range(1, RING)}
    staged = call(
        teacher_body,
        (
            shape((vocab, MASKED), BF16), shape((8, MASKED), F32),
            shape((2, 2 * slots, MASKED), BF16),
        ),
        teacher.T, chosen, specs=[HBM, VMEM],
        scratch=[pltpu.VMEM((vocab, slots), BF16), DMA(())],
        flops=2 * vocab * slots * MASKED + 4 * slots * slots * MASKED,
    )
    blocks[0, 2], staged = lax.optimization_barrier((blocks[0, 2], staged))
    teacher_rows, lse_teacher, back = staged
    blocks |= {(1, k): swap_core(blocks[0, k]) for k in range(RING)}
    total = call(
        student_first_body, logits_shape, *[blocks[at] for at in FIRST], weight, flops=half_flops
    )
    blocks[1, 1], total = lax.optimization_barrier((blocks[1, 1], total))
    student, stats = call(
        student_last_body, (logits_shape, shape((NZ * RING, 2, MASKED), F32)),
        *[blocks[at] for at in LAST], weight, total, lse_teacher, flops=half_flops,
    )
    stats = lax.all_to_all(stats, ALL, 0, 0, tiled=True, axis_index_groups=peers())
    lse = call(combine_body, shape((2, MASKED), F32), stats)
    lse = call(join_body, shape((2, MASKED), F32), lse, *[shift(lse, k, ring=2) for k in (3, 1, 2)])
    parts = {}
    which = ((1, 2),)
    grad_logits, parts[1, 2] = call(
        functools.partial(logits_body, which=which),
        (shape((vocab, MASKED), BF16), shape((MASKED, part), BF16)),
        student, teacher_rows, lse, swap_core(lse), count, weight, flops=half_flops // 4,
    )
    sums = {}

    def make(which, tie):
        grad, tie = lax.optimization_barrier((grad_logits, tie))
        out = tuple(shape((MASKED, part), BF16 if side else F32) for side, k in which)
        made = call(
            functools.partial(products_body, which=which), out, grad, weight,
            flops=half_flops * len(which) // 4,
        )
        parts.update(zip(which, made))
        return tie

    def add(k):
        return (parts[0, k] + swap_core(parts[1, k]).astype(F32)).astype(BF16)

    make(((0, 2), (1, 1)), lse)
    make(((1, 3), (0, 1), (0, 3)), lse)
    both = {k: add(k) for k in (2, 1, 3)}
    both[1] = make(((1, 0), (0, 0)), both[1])
    sums = [add(0)] + [shift(both[k], k) for k in range(1, RING)]
    grad_head = call(
        head_body, shape((vocab, depth), BF16),
        *[blocks[side, k] for side in range(NCORE) for k in range(RING)], grad_logits, outs=HBM,
        scratch=[pltpu.VMEM((NCORE * RING, vocab, part), BF16), DMA((NCORE * RING,))],
        flops=2 * half_flops,
    )
    sums[1], grad_head = lax.optimization_barrier((sums[1], grad_head))
    steps = call(
        spread_body, (shape((2 * slots // RING, part // 2), BF16),) * RING, *sums, back,
        flops=4 * MASKED * slots * part,
    )
    steps = [steps[0]] + [shift(steps[k], k, ring=2) for k in (2, 1, 3)]
    partial = sum(step.astype(F32) for step in steps).astype(BF16)
    partial = lax.all_to_all(
        partial.reshape(NZ * RING, 8, part // 2), ALL, 0, 0, tiled=True,
        axis_index_groups=peers(),
    )
    mine, other = call(collect_body, (shape((RING, 4, part // 2), F32),) * 2, partial)
    grad_hidden = call(
        finish_body, shape((own, depth), BF16), mine, swap_core(other),
        scratch=[pltpu.VMEM((own, depth), F32)],
    )
    return grad_hidden, grad_head.T


def solution(mesh):
    fine = Mesh(mesh.devices.reshape(NX, NZ, NCORE, NY), ALL)
    return jax.shard_map(
        per_device,
        mesh=fine,
        in_specs=(P(SEQ, None), P(None, ALL), P(None, ALL), P(SEQ, None), P(SEQ)),
        out_specs=(P(ALL, None), P(None, ALL)),
        check_vma=False,
    )
```

```python
import functools

import jax
import jax.numpy as jnp
from jax import lax
from jax.experimental import pallas as pl
from jax.experimental.pallas import tpu as pltpu
from jax.sharding import Mesh, PartitionSpec as P

LOSS_SCALE = 1024.0
MASKED = 256
MARK = 64.0

SEQ = ("x", "z", "core")
ALL = ("x", "z", "core", "y")
NX, NZ, NCORE, NY = 4, 8, 2, 4
RING = 4
ZS = tuple((z + NZ // 2) % NZ for z in range(NZ))
PLACES = tuple((place + 1) % RING for place in range(RING))
FIRST = ((0, 0), (0, 1), (0, 2), (0, 3), (1, 0), (1, 2))
LAST = ((1, 3), (1, 1))
Y_CORE = 1
assert NX == NY == RING
F32, BF16 = jnp.float32, jnp.bfloat16
NT = (((1,), (1,)), ((), ()))
TN = (((0,), (0,)), ((), ()))
VMEM = pl.BlockSpec(memory_space=pltpu.VMEM)
HBM = pl.BlockSpec(memory_space=pltpu.HBM)
DMA = pltpu.SemaphoreType.DMA
LIMIT, PICK_LIMIT = 32 << 20, 55996416


def call(body, out, *args, specs=None, outs=VMEM, flops=0, scratch=(), limit=LIMIT):
    leaves = jax.tree.leaves((args, out))
    nbytes = sum(x.size * x.dtype.itemsize for x in leaves)
    return pl.pallas_call(
        body,
        out_shape=out,
        in_specs=specs or [VMEM] * len(args),
        out_specs=jax.tree.map(lambda _: outs, out),
        scratch_shapes=list(scratch),
        cost_estimate=pl.CostEstimate(flops=flops, bytes_accessed=nbytes, transcendentals=0),
        compiler_params=pltpu.CompilerParams(vmem_limit_bytes=limit),
    )(*args)


def shape(dims, dtype):
    return jax.ShapeDtypeStruct(dims, dtype)


def columns(block, width):
    return pl.ds(pl.multiple_of(block * width, width), width)


def place(core):
    return jnp.where(core == Y_CORE, lax.axis_index("y"), lax.axis_index("x"))


def second_place(core):
    return jnp.where(core == Y_CORE, lax.axis_index("x"), lax.axis_index("y"))


def part_at(side, steps):
    core = lax.axis_index("core")
    core = core if side == 0 else 1 - core
    return core * RING + lax.rem(place(core) + steps + RING, RING)


def pick_body(numbers, hidden, out, mine, sems):
    shards, capacity, width = out.shape
    tokens, depth = hidden.shape
    mine_y, x_half = Y_CORE * RING + lax.axis_index("y"), (1 - Y_CORE) * (depth // 2)
    copies = [
        pltpu.make_async_copy(
            hidden.at[:, columns(mine_y, width)], mine.at[:tokens, :width], sems.at[0]
        ),
        pltpu.make_async_copy(
            hidden.at[:, x_half : x_half + depth // 2], mine.at[:tokens, width:], sems.at[1]
        ),
    ]
    for copy in copies:
        copy.start()
    more = (mine.shape[0] - tokens, mine.shape[1])
    mine[tokens:, :] = (lax.broadcasted_iota(jnp.int32, more, 0) == 0).astype(F32).astype(BF16)
    position, count = numbers[...] % tokens, numbers[...] // tokens
    masked = lax.broadcasted_iota(jnp.int32, numbers.shape, 1) < count
    row = lax.broadcasted_iota(jnp.int32, (mine.shape[0], capacity), 0)
    source = jnp.where(masked, position, tokens)
    hot = jnp.where(row == source, jnp.where(masked, 1.0, MARK), 0.0).astype(BF16)
    for copy in copies:
        copy.wait()
    rows = lax.dot_general(hot, mine[...], TN, preferred_element_type=F32)
    rows = rows.astype(BF16)
    for s in range(shards):
        start = 0 if s % NCORE == Y_CORE else (1 + s // (NZ * NCORE)) * width
        out[s] = rows[:, start : start + width]


def compact_body(rows, picked, chosen, count):
    slots = rows.shape[0]
    capacity = 8
    valid = (rows[...].astype(F32)[:, 0:1] < MARK / 2).astype(F32)
    a = lax.broadcasted_iota(jnp.int32, (slots, slots), 0)
    b = lax.broadcasted_iota(jnp.int32, (slots, slots), 1)
    spread = jnp.broadcast_to(valid, (slots, slots))
    rank = jnp.sum(jnp.where(a < b, spread, 0.0), axis=0, keepdims=True)
    mine = jnp.sum(jnp.where(a == b, spread, 0.0), axis=0, keepdims=True)
    total = jnp.sum(jnp.where(a // capacity == b // capacity, spread, 0.0), axis=0, keepdims=True)
    place = jnp.where(mine > 0.5, rank, -1.0).astype(jnp.int32)
    target = lax.broadcasted_iota(jnp.int32, (MASKED, slots), 0)
    hot = (target == place).astype(F32).astype(BF16)
    chosen[...] = hot
    picked[...] = jnp.dot(hot, rows[...], preferred_element_type=F32).astype(BF16)
    totals = jnp.broadcast_to(total, (8, slots)).astype(BF16)
    count[...] = lax.dot_general(totals, hot, NT, preferred_element_type=F32)


def logsumexp(x):
    top = jnp.max(x, axis=0, keepdims=True)
    return top + jnp.log(jnp.sum(jnp.exp(x - top), axis=0, keepdims=True))


def teacher_body(teacher_hbm, chosen, out, lse, back, teacher, sem):
    move = pltpu.make_async_copy(teacher_hbm, teacher, sem)
    move.start()
    halves, sent, masked = back.shape
    slots = chosen.shape[1]
    row = lax.broadcasted_iota(jnp.int32, (sent, slots), 0)
    second, z, first, q = row // 256, (row // 32 + NZ // 2) % NZ, (row // 8 + 1) % RING, row % 8
    straight = lax.axis_index("core") == Y_CORE
    x, y = jnp.where(straight, second, first), jnp.where(straight, first, second)
    slot = (x * NZ + z) * 16 + q // 4 * 8 + y * 2 + q // 2 % 2
    column = lax.broadcasted_iota(jnp.int32, (sent, slots), 1)
    pick = (column == slot).astype(F32).astype(BF16)
    placed = lax.dot_general(pick, chosen[...], NT, preferred_element_type=F32)
    odd = lax.broadcasted_iota(jnp.int32, (sent, masked), 0) % 2
    for h in range(halves):
        back[h] = jnp.where(odd == h, placed, 0.0).astype(BF16)
    move.wait()
    rows = lax.dot_general(teacher[...], chosen[...], NT, preferred_element_type=F32)
    out[...] = rows.astype(BF16)
    lse[...] = jnp.broadcast_to(logsumexp(rows), lse.shape)


def student_part(blocks, which, weight, total):
    for block, (side, k) in zip(blocks, which):
        total += lax.dot_general(
            weight[:, columns(part_at(side, -k), block.shape[1])], block[...],
            NT, preferred_element_type=F32,
        )
    return total


def student_first_body(*refs):
    blocks, (weight, total) = refs[: len(FIRST)], refs[len(FIRST) :]
    total[...] = student_part(blocks, FIRST, weight, jnp.zeros(total.shape, F32))


def student_last_body(*refs):
    blocks, (weight, first, lse_teacher, out, stats) = refs[: len(LAST)], refs[len(LAST) :]
    total = student_part(blocks, LAST, weight, first[...])
    out[...] = total
    both = jnp.concatenate([logsumexp(total), lse_teacher[0:1, :]], axis=0)
    stats[...] = jnp.broadcast_to(both[None], stats.shape)


def combine_body(stats, out):
    x = stats[...]
    top = jnp.max(x, axis=0)
    out[...] = top + jnp.log(jnp.sum(jnp.exp(x - top[None]), axis=0))


def join_body(a, b, c, d, out):
    top = jnp.maximum(jnp.maximum(a[...], b[...]), jnp.maximum(c[...], d[...]))
    out[...] = top + jnp.log(sum(jnp.exp(x[...] - top) for x in (a, b, c, d)))


def products(grad, weight, which, parts):
    for part, (side, k) in zip(parts, which):
        part[...] = lax.dot_general(
            grad, weight[:, columns(part_at(side, k), part.shape[1])], TN,
            preferred_element_type=F32,
        ).astype(part.dtype)


def logits_body(student, teacher, mine, other, count, weight, grad_logits, *parts, which):
    top = jnp.maximum(mine[...], other[...])
    lse = top + jnp.log(jnp.exp(mine[...] - top) + jnp.exp(other[...] - top))
    scale = LOSS_SCALE / count[0:1, :]
    prob_student = jnp.exp(student[...] - lse[0:1, :])
    prob_teacher = jnp.exp(teacher[...].astype(F32) - lse[1:2, :])
    grad = (scale * (prob_student - prob_teacher)).astype(BF16)
    grad_logits[...] = grad
    products(grad, weight, which, parts)


def products_body(grad_logits, weight, *parts, which):
    products(grad_logits[...], weight, which, parts)


def head_body(*refs):
    blocks, (grad_logits, out_hbm, out, sems) = refs[: NCORE * RING], refs[NCORE * RING :]
    copies = []
    for i, block in enumerate(blocks):
        span = columns(part_at(i // RING, -(i % RING)), block.shape[1])
        out[i] = jnp.dot(
            grad_logits[...], block[...], preferred_element_type=F32
        ).astype(BF16)
        copy = pltpu.make_async_copy(out.at[i], out_hbm.at[:, span], sems.at[i])
        copy.start()
        copies.append(copy)
    for copy in copies:
        copy.wait()


def spread_body(a, b, c, d, back, *outs):
    total = a[...].astype(F32) + b[...].astype(F32) + c[...].astype(F32) + d[...].astype(F32)
    total = total.astype(BF16)
    rows, half = outs[0].shape
    here = second_place(lax.axis_index("core"))
    for k, out in enumerate(outs):
        span = columns(lax.rem(here + k, RING), rows)
        out[...] = (
            jnp.dot(back[0, span, :], total[:, :half], preferred_element_type=F32)
            + jnp.dot(back[1, span, :], total[:, half:], preferred_element_type=F32)
        ).astype(BF16)


def collect_body(parts, mine, other):
    peers, rows, half = parts.shape
    total = jnp.sum(parts[...].astype(F32).reshape(NZ, RING, rows, half), axis=0)
    low, high = total[:, : rows // 2], total[:, rows // 2 :]
    first = lax.axis_index("core") == 0
    mine[...] = jnp.where(first, low, high)
    other[...] = jnp.where(first, high, low)


def finish_body(mine, other, out, whole):
    half = mine.shape[2]
    first = lax.axis_index("core") == 0
    by_core = (
        jnp.where(first, mine[...], other[...]), jnp.where(first, other[...], mine[...]),
    )
    for i in range(out.shape[0]):
        for core in range(NCORE):
            for at in range(RING):
                for h in range(2):
                    start = ((core * RING + at) * 2 + h) * half
                    row = 2 * i + h
                    near = PLACES.index(at)
                    whole[i : i + 1, start : start + half] = by_core[core][near, row : row + 1]
    out[...] = whole[...].astype(BF16)


def swap_core(x):
    return lax.ppermute(x, "core", [(0, 1), (1, 0)])


def index(x, z, core, y):
    return ((x * NZ + z) * NCORE + core) * NY + y


def shift(v, k, ring=1):
    moves = []
    for x in range(NX):
        for z in range(NZ):
            for y in range(NY):
                for core in range(NCORE):
                    if (core == Y_CORE) == (ring == 1):
                        to = index(x, z, core, (y + k) % NY)
                    else:
                        to = index((x + k) % NX, z, core, y)
                    moves.append((index(x, z, core, y), to))
    return lax.ppermute(v, ALL, moves)


def peers(places):
    groups = []
    for second in range(RING):
        groups.append([index(second, z, Y_CORE, y) for z in ZS for y in places])
        groups.append([index(x, z, 1 - Y_CORE, second) for z in ZS for x in places])
    return groups


def per_device(hidden, head_weight, teacher, positions, counts):
    tokens, depth = hidden.shape
    capacity = positions.shape[1]
    shards = NX * NZ * NCORE
    slots = shards * capacity
    vocab = head_weight.shape[1]
    part = depth // (RING * NCORE)
    own = capacity // NY
    weight = head_weight.T
    half_flops = vocab * depth * MASKED
    logits_shape = shape((vocab, MASKED), F32)

    numbers = positions + tokens * counts
    send = call(
        pick_body, shape((shards, capacity, part), BF16), numbers, hidden, specs=[VMEM, HBM],
        scratch=[pltpu.VMEM((tokens + 16, part + depth // 2), BF16), DMA((2,))],
        limit=PICK_LIMIT,
    )
    rows = lax.all_to_all(send, SEQ, 0, 0, tiled=True).reshape(slots, part)
    picked, chosen, count = call(
        compact_body,
        (
            shape((MASKED, part), BF16), shape((MASKED, slots), BF16), shape((8, MASKED), F32),
        ),
        rows, flops=2 * MASKED * slots * part,
    )
    blocks = {(0, 0): picked} | {(0, k): shift(picked, k) for k in range(1, RING)}
    staged = call(
        teacher_body,
        (
            shape((vocab, MASKED), BF16), shape((8, MASKED), F32),
            shape((2, 2 * slots, MASKED), BF16),
        ),
        teacher.T, chosen, specs=[HBM, VMEM],
        scratch=[pltpu.VMEM((vocab, slots), BF16), DMA(())],
        flops=2 * vocab * slots * MASKED + 4 * slots * slots * MASKED,
    )
    blocks[0, 2], staged = lax.optimization_barrier((blocks[0, 2], staged))
    teacher_rows, lse_teacher, back = staged
    blocks |= {(1, k): swap_core(blocks[0, k]) for k in range(RING)}
    total = call(
        student_first_body, logits_shape, *[blocks[at] for at in FIRST], weight, flops=half_flops
    )
    blocks[1, 1], total = lax.optimization_barrier((blocks[1, 1], total))
    student, stats = call(
        student_last_body, (logits_shape, shape((NZ * RING, 2, MASKED), F32)),
        *[blocks[at] for at in LAST], weight, total, lse_teacher, flops=half_flops,
    )
    stats = lax.all_to_all(
        stats, ALL, 0, 0, tiled=True, axis_index_groups=peers(range(RING))
    )
    lse = call(combine_body, shape((2, MASKED), F32), stats)
    lse = call(join_body, shape((2, MASKED), F32), lse, *[shift(lse, k, ring=2) for k in (3, 1, 2)])
    parts = {}
    which = ((1, 2),)
    grad_logits, parts[1, 2] = call(
        functools.partial(logits_body, which=which),
        (shape((vocab, MASKED), BF16), shape((MASKED, part), BF16)),
        student, teacher_rows, lse, swap_core(lse), count, weight, flops=half_flops // 4,
    )
    sums = {}

    def make(which, tie):
        grad, tie = lax.optimization_barrier((grad_logits, tie))
        out = tuple(shape((MASKED, part), BF16 if side else F32) for side, k in which)
        made = call(
            functools.partial(products_body, which=which), out, grad, weight,
            flops=half_flops * len(which) // 4,
        )
        parts.update(zip(which, made))
        return tie

    def add(k):
        return (parts[0, k] + swap_core(parts[1, k]).astype(F32)).astype(BF16)

    make(((0, 2), (1, 1)), lse)
    make(((1, 3), (0, 1), (0, 3)), lse)
    both = {k: add(k) for k in (2, 1, 3)}
    both[1] = make(((1, 0), (0, 0)), both[1])
    sums = [add(0)] + [shift(both[k], k) for k in range(1, RING)]
    grad_head = call(
        head_body, shape((vocab, depth), BF16),
        *[blocks[side, k] for side in range(NCORE) for k in range(RING)], grad_logits, outs=HBM,
        scratch=[pltpu.VMEM((NCORE * RING, vocab, part), BF16), DMA((NCORE * RING,))],
        flops=2 * half_flops,
    )
    sums[1], grad_head = lax.optimization_barrier((sums[1], grad_head))
    steps = call(
        spread_body, (shape((2 * slots // RING, part // 2), BF16),) * RING, *sums, back,
        flops=4 * MASKED * slots * part,
    )
    steps = [steps[0]] + [shift(steps[k], k, ring=2) for k in (2, 1, 3)]
    partial = sum(step.astype(F32) for step in steps).astype(BF16)
    partial = lax.all_to_all(
        partial.reshape(NZ * RING, 8, part // 2), ALL, 0, 0, tiled=True,
        axis_index_groups=peers(PLACES),
    )
    mine, other = call(collect_body, (shape((RING, 4, part // 2), F32),) * 2, partial)
    grad_hidden = call(
        finish_body, shape((own, depth), BF16), mine, swap_core(other),
        scratch=[pltpu.VMEM((own, depth), F32)],
    )
    return grad_hidden, grad_head.T


def solution(mesh):
    fine = Mesh(mesh.devices.reshape(NX, NZ, NCORE, NY), ALL)
    return jax.shard_map(
        per_device,
        mesh=fine,
        in_specs=(P(SEQ, None), P(None, ALL), P(None, ALL), P(SEQ, None), P(SEQ)),
        out_specs=(P(ALL, None), P(None, ALL)),
        check_vma=False,
    )
```

```python
import functools

import jax
import jax.numpy as jnp
from jax import lax
from jax.experimental import pallas as pl
from jax.experimental.pallas import tpu as pltpu
from jax.sharding import Mesh, PartitionSpec as P

LOSS_SCALE = 1024.0
MASKED = 256
MARK = 64.0

SEQ = ("x", "z", "core")
ALL = ("x", "z", "core", "y")
NX, NZ, NCORE, NY = 4, 8, 2, 4
RING = 4
ZS = tuple((z + NZ // 2) % NZ for z in range(NZ))
PLACES = tuple((place + 1) % RING for place in range(RING))
FIRST = ((0, 0), (0, 1), (0, 2), (0, 3), (1, 0), (1, 2))
LAST = ((1, 3), (1, 1))
Y_CORE = 1
assert NX == NY == RING
F32, BF16 = jnp.float32, jnp.bfloat16
NT = (((1,), (1,)), ((), ()))
TN = (((0,), (0,)), ((), ()))
VMEM = pl.BlockSpec(memory_space=pltpu.VMEM)
HBM = pl.BlockSpec(memory_space=pltpu.HBM)
DMA = pltpu.SemaphoreType.DMA
LIMIT, PICK_LIMIT = 32 << 20, 55996416


def call(body, out, *args, specs=None, outs=VMEM, flops=0, scratch=(), limit=LIMIT):
    leaves = jax.tree.leaves((args, out))
    nbytes = sum(x.size * x.dtype.itemsize for x in leaves)
    return pl.pallas_call(
        body,
        out_shape=out,
        in_specs=specs or [VMEM] * len(args),
        out_specs=jax.tree.map(lambda _: outs, out),
        scratch_shapes=list(scratch),
        cost_estimate=pl.CostEstimate(flops=flops, bytes_accessed=nbytes, transcendentals=0),
        compiler_params=pltpu.CompilerParams(vmem_limit_bytes=limit),
    )(*args)


def shape(dims, dtype):
    return jax.ShapeDtypeStruct(dims, dtype)


def columns(block, width):
    return pl.ds(pl.multiple_of(block * width, width), width)


def place(core):
    return jnp.where(core == Y_CORE, lax.axis_index("y"), lax.axis_index("x"))


def second_place(core):
    return jnp.where(core == Y_CORE, lax.axis_index("x"), lax.axis_index("y"))


def part_at(side, steps):
    core = lax.axis_index("core")
    core = core if side == 0 else 1 - core
    return core * RING + lax.rem(place(core) + steps + RING, RING)


def pick_body(numbers, hidden, out, mine, sems):
    shards, capacity, width = out.shape
    tokens, depth = hidden.shape
    mine_y, x_half = Y_CORE * RING + lax.axis_index("y"), (1 - Y_CORE) * (depth // 2)
    copies = [
        pltpu.make_async_copy(
            hidden.at[:, columns(mine_y, width)], mine.at[:tokens, :width], sems.at[0]
        ),
        pltpu.make_async_copy(
            hidden.at[:, x_half : x_half + depth // 2], mine.at[:tokens, width:], sems.at[1]
        ),
    ]
    for copy in copies:
        copy.start()
    more = (mine.shape[0] - tokens, mine.shape[1])
    mine[tokens:, :] = (lax.broadcasted_iota(jnp.int32, more, 0) == 0).astype(F32).astype(BF16)
    position, count = numbers[...] % tokens, numbers[...] // tokens
    masked = lax.broadcasted_iota(jnp.int32, numbers.shape, 1) < count
    row = lax.broadcasted_iota(jnp.int32, (mine.shape[0], capacity), 0)
    source = jnp.where(masked, position, tokens)
    hot = jnp.where(row == source, jnp.where(masked, 1.0, MARK), 0.0).astype(BF16)
    for copy in copies:
        copy.wait()
    rows = lax.dot_general(hot, mine[...], TN, preferred_element_type=F32)
    rows = rows.astype(BF16)
    for s in range(shards):
        start = 0 if s % NCORE == Y_CORE else (1 + s // (NZ * NCORE)) * width
        out[s] = rows[:, start : start + width]


def compact_body(rows, picked, chosen, count):
    slots = rows.shape[0]
    capacity = 8
    valid = (rows[...].astype(F32)[:, 0:1] < MARK / 2).astype(F32)
    a = lax.broadcasted_iota(jnp.int32, (slots, slots), 0)
    b = lax.broadcasted_iota(jnp.int32, (slots, slots), 1)
    spread = jnp.broadcast_to(valid, (slots, slots))
    rank = jnp.sum(jnp.where(a < b, spread, 0.0), axis=0, keepdims=True)
    mine = jnp.sum(jnp.where(a == b, spread, 0.0), axis=0, keepdims=True)
    total = jnp.sum(jnp.where(a // capacity == b // capacity, spread, 0.0), axis=0, keepdims=True)
    place = jnp.where(mine > 0.5, rank, -1.0).astype(jnp.int32)
    target = lax.broadcasted_iota(jnp.int32, (MASKED, slots), 0)
    hot = (target == place).astype(F32).astype(BF16)
    chosen[...] = hot
    picked[...] = jnp.dot(hot, rows[...], preferred_element_type=F32).astype(BF16)
    totals = jnp.broadcast_to(total, (8, slots)).astype(BF16)
    count[...] = lax.dot_general(totals, hot, NT, preferred_element_type=F32)


def logsumexp(x):
    top = jnp.max(x, axis=0, keepdims=True)
    return top + jnp.log(jnp.sum(jnp.exp(x - top), axis=0, keepdims=True))


def teacher_body(teacher_hbm, chosen, out, lse, back, teacher, sem):
    move = pltpu.make_async_copy(teacher_hbm, teacher, sem)
    move.start()
    halves, sent, masked = back.shape
    slots = chosen.shape[1]
    row = lax.broadcasted_iota(jnp.int32, (sent, slots), 0)
    second, z, first, q = row // 256, (row // 32 + NZ // 2) % NZ, (row // 8 + 1) % RING, row % 8
    straight = lax.axis_index("core") == Y_CORE
    x, y = jnp.where(straight, second, first), jnp.where(straight, first, second)
    slot = (x * NZ + z) * 16 + q // 4 * 8 + y * 2 + q // 2 % 2
    column = lax.broadcasted_iota(jnp.int32, (sent, slots), 1)
    pick = (column == slot).astype(F32).astype(BF16)
    placed = lax.dot_general(pick, chosen[...], NT, preferred_element_type=F32)
    odd = lax.broadcasted_iota(jnp.int32, (sent, masked), 0) % 2
    for h in range(halves):
        back[h] = jnp.where(odd == h, placed, 0.0).astype(BF16)
    move.wait()
    rows = lax.dot_general(teacher[...], chosen[...], NT, preferred_element_type=F32)
    out[...] = rows.astype(BF16)
    lse[...] = jnp.broadcast_to(logsumexp(rows), lse.shape)


def student_part(blocks, which, weight, total):
    for block, (side, k) in zip(blocks, which):
        total += lax.dot_general(
            weight[:, columns(part_at(side, -k), block.shape[1])], block[...],
            NT, preferred_element_type=F32,
        )
    return total


def student_first_body(*refs):
    blocks, (weight, total) = refs[: len(FIRST)], refs[len(FIRST) :]
    total[...] = student_part(blocks, FIRST, weight, jnp.zeros(total.shape, F32))


def student_last_body(*refs):
    blocks, (weight, first, lse_teacher, out, stats) = refs[: len(LAST)], refs[len(LAST) :]
    total = student_part(blocks, LAST, weight, first[...])
    out[...] = total
    both = jnp.concatenate([logsumexp(total), lse_teacher[0:1, :]], axis=0)
    stats[...] = jnp.broadcast_to(both[None], stats.shape)


def combine_body(stats, out):
    x = stats[...]
    top = jnp.max(x, axis=0)
    out[...] = top + jnp.log(jnp.sum(jnp.exp(x - top[None]), axis=0))


def join_body(a, b, c, d, out):
    top = jnp.maximum(jnp.maximum(a[...], b[...]), jnp.maximum(c[...], d[...]))
    out[...] = top + jnp.log(sum(jnp.exp(x[...] - top) for x in (a, b, c, d)))


def products(grad, weight, which, parts):
    for part, (side, k) in zip(parts, which):
        part[...] = lax.dot_general(
            grad, weight[:, columns(part_at(side, k), part.shape[1])], TN,
            preferred_element_type=F32,
        ).astype(part.dtype)


def logits_body(student, teacher, mine, other, count, weight, grad_logits, *parts, which):
    top = jnp.maximum(mine[...], other[...])
    lse = top + jnp.log(jnp.exp(mine[...] - top) + jnp.exp(other[...] - top))
    scale = LOSS_SCALE / count[0:1, :]
    prob_student = jnp.exp(student[...] - lse[0:1, :])
    prob_teacher = jnp.exp(teacher[...].astype(F32) - lse[1:2, :])
    grad = (scale * (prob_student - prob_teacher)).astype(BF16)
    grad_logits[...] = grad
    products(grad, weight, which, parts)


def products_body(grad_logits, weight, *parts, which):
    products(grad_logits[...], weight, which, parts)


def head_body(*refs):
    blocks, (grad_logits, out_hbm, out, sems) = refs[: NCORE * RING], refs[NCORE * RING :]
    copies = []
    for i, block in enumerate(blocks):
        span = columns(part_at(i // RING, -(i % RING)), block.shape[1])
        out[i] = jnp.dot(
            grad_logits[...], block[...], preferred_element_type=F32
        ).astype(BF16)
        copy = pltpu.make_async_copy(out.at[i], out_hbm.at[:, span], sems.at[i])
        copy.start()
        copies.append(copy)
    for copy in copies:
        copy.wait()


def spread_body(a, b, c, d, back, *outs):
    total = a[...].astype(F32) + b[...].astype(F32) + c[...].astype(F32) + d[...].astype(F32)
    total = total.astype(BF16)
    rows, half = outs[0].shape
    here = second_place(lax.axis_index("core"))
    for k, out in enumerate(outs):
        span = columns(lax.rem(here + k, RING), rows)
        out[...] = (
            jnp.dot(back[0, span, :], total[:, :half], preferred_element_type=F32)
            + jnp.dot(back[1, span, :], total[:, half:], preferred_element_type=F32)
        ).astype(BF16)


def collect_body(parts, mine, other):
    peers, rows, half = parts.shape
    total = jnp.sum(parts[...].astype(F32).reshape(NZ, RING, rows, half), axis=0)
    low, high = total[:, : rows // 2], total[:, rows // 2 :]
    first = lax.axis_index("core") == 0
    mine[...] = jnp.where(first, low, high)
    other[...] = jnp.where(first, high, low)


def finish_body(mine, other, out, whole):
    half = mine.shape[2]
    first = lax.axis_index("core") == 0
    by_core = (
        jnp.where(first, mine[...], other[...]), jnp.where(first, other[...], mine[...]),
    )
    for i in range(out.shape[0]):
        for core in range(NCORE):
            for at in range(RING):
                for h in range(2):
                    start = ((core * RING + at) * 2 + h) * half
                    row = 2 * i + h
                    near = PLACES.index(at)
                    whole[i : i + 1, start : start + half] = by_core[core][near, row : row + 1]
    out[...] = whole[...].astype(BF16)


def swap_core(x):
    return lax.ppermute(x, "core", [(0, 1), (1, 0)])


def index(x, z, core, y):
    return ((x * NZ + z) * NCORE + core) * NY + y


def shift(v, k, ring=1):
    moves = []
    for x in range(NX):
        for z in range(NZ):
            for y in range(NY):
                for core in range(NCORE):
                    if (core == Y_CORE) == (ring == 1):
                        to = index(x, z, core, (y + k) % NY)
                    else:
                        to = index((x + k) % NX, z, core, y)
                    moves.append((index(x, z, core, y), to))
    return lax.ppermute(v, ALL, moves)


def peers():
    groups = []
    for second in range(RING):
        groups.append([index(second, z, Y_CORE, y) for z in ZS for y in PLACES])
        groups.append([index(x, z, 1 - Y_CORE, second) for z in ZS for x in PLACES])
    return groups


def per_device(hidden, head_weight, teacher, positions, counts):
    tokens, depth = hidden.shape
    capacity = positions.shape[1]
    shards = NX * NZ * NCORE
    slots = shards * capacity
    vocab = head_weight.shape[1]
    part = depth // (RING * NCORE)
    own = capacity // NY
    weight = head_weight.T
    half_flops = vocab * depth * MASKED
    logits_shape = shape((vocab, MASKED), F32)

    numbers = positions + tokens * counts
    send = call(
        pick_body, shape((shards, capacity, part), BF16), numbers, hidden, specs=[VMEM, HBM],
        scratch=[pltpu.VMEM((tokens + 16, part + depth // 2), BF16), DMA((2,))],
        limit=PICK_LIMIT,
    )
    rows = lax.all_to_all(send, SEQ, 0, 0, tiled=True).reshape(slots, part)
    picked, chosen, count = call(
        compact_body,
        (
            shape((MASKED, part), BF16), shape((MASKED, slots), BF16), shape((8, MASKED), F32),
        ),
        rows, flops=2 * MASKED * slots * part,
    )
    blocks = {(0, 0): picked} | {(0, k): shift(picked, k) for k in range(1, RING)}
    staged = call(
        teacher_body,
        (
            shape((vocab, MASKED), BF16), shape((8, MASKED), F32),
            shape((2, 2 * slots, MASKED), BF16),
        ),
        teacher.T, chosen, specs=[HBM, VMEM],
        scratch=[pltpu.VMEM((vocab, slots), BF16), DMA(())],
        flops=2 * vocab * slots * MASKED + 4 * slots * slots * MASKED,
    )
    blocks[0, 2], staged = lax.optimization_barrier((blocks[0, 2], staged))
    teacher_rows, lse_teacher, back = staged
    blocks |= {(1, k): swap_core(blocks[0, k]) for k in range(RING)}
    total = call(
        student_first_body, logits_shape, *[blocks[at] for at in FIRST], weight, flops=half_flops
    )
    blocks[1, 1], total = lax.optimization_barrier((blocks[1, 1], total))
    student, stats = call(
        student_last_body, (logits_shape, shape((NZ * RING, 2, MASKED), F32)),
        *[blocks[at] for at in LAST], weight, total, lse_teacher, flops=half_flops,
    )
    stats = lax.all_to_all(
        stats, ALL, 0, 0, tiled=True, axis_index_groups=peers()
    )
    lse = call(combine_body, shape((2, MASKED), F32), stats)
    lse = call(join_body, shape((2, MASKED), F32), lse, *[shift(lse, k, ring=2) for k in (3, 1, 2)])
    parts = {}
    which = ((1, 2),)
    grad_logits, parts[1, 2] = call(
        functools.partial(logits_body, which=which),
        (shape((vocab, MASKED), BF16), shape((MASKED, part), BF16)),
        student, teacher_rows, lse, swap_core(lse), count, weight, flops=half_flops // 4,
    )
    sums = {}

    def make(which, tie):
        grad, tie = lax.optimization_barrier((grad_logits, tie))
        out = tuple(shape((MASKED, part), BF16 if side else F32) for side, k in which)
        made = call(
            functools.partial(products_body, which=which), out, grad, weight,
            flops=half_flops * len(which) // 4,
        )
        parts.update(zip(which, made))
        return tie

    def add(k):
        return (parts[0, k] + swap_core(parts[1, k]).astype(F32)).astype(BF16)

    make(((0, 2), (1, 1)), lse)
    make(((1, 3), (0, 1), (0, 3)), lse)
    both = {k: add(k) for k in (2, 1, 3)}
    both[1] = make(((1, 0), (0, 0)), both[1])
    sums = [add(0)] + [shift(both[k], k) for k in range(1, RING)]
    grad_head = call(
        head_body, shape((vocab, depth), BF16),
        *[blocks[side, k] for side in range(NCORE) for k in range(RING)], grad_logits, outs=HBM,
        scratch=[pltpu.VMEM((NCORE * RING, vocab, part), BF16), DMA((NCORE * RING,))],
        flops=2 * half_flops,
    )
    sums[1], grad_head = lax.optimization_barrier((sums[1], grad_head))
    steps = call(
        spread_body, (shape((2 * slots // RING, part // 2), BF16),) * RING, *sums, back,
        flops=4 * MASKED * slots * part,
    )
    steps = [steps[0]] + [shift(steps[k], k, ring=2) for k in (2, 1, 3)]
    partial = sum(step.astype(F32) for step in steps).astype(BF16)
    partial = lax.all_to_all(
        partial.reshape(NZ * RING, 8, part // 2), ALL, 0, 0, tiled=True,
        axis_index_groups=peers(),
    )
    mine, other = call(collect_body, (shape((RING, 4, part // 2), F32),) * 2, partial)
    grad_hidden = call(
        finish_body, shape((own, depth), BF16), mine, swap_core(other),
        scratch=[pltpu.VMEM((own, depth), F32)],
    )
    return grad_hidden, grad_head.T


def solution(mesh):
    fine = Mesh(mesh.devices.reshape(NX, NZ, NCORE, NY), ALL)
    return jax.shard_map(
        per_device,
        mesh=fine,
        in_specs=(P(SEQ, None), P(None, ALL), P(None, ALL), P(SEQ, None), P(SEQ)),
        out_specs=(P(ALL, None), P(None, ALL)),
        check_vma=False,
    )
```
